32 devices in a mesh: horiz: 8 (over y, x, core), vert: 4 (over z).
Axes of the slice: x: 2, y: 2, z: 4, core: 2. Of those that a mesh axis runs over, the one named last changes fastest.
Arguments:
- velocity: float32 [3, 64, 32, 128], P(None, 'horiz', 'vert'), may hold values from -3 to 3
- heights: float32 [4], P('vert'), may hold values from 0.5 to 2
- time_step: float32 [], replicated, may hold values from 0.005 to 0.02
Outputs:
- rate: float32 [3, 64, 32, 128], P(None, 'horiz', 'vert')
The draws below stay inside these ranges and needn't reach their ends.
All inputs are finite; a program needn't handle non-finite values.
Results may differ from the reference program's by a relative error of at most 0.000084.
Values sent between devices are 32-bit elements; how exact they have to be, the bound alone decides.
No kernel may reach another device: no remote copies, remote signals or barrier semaphores. Data moves between devices by JAX's collectives and lax.ppermute only.
A program may use at most 64 MiB of HBM per device.

```python
import math
import jax
import jax.numpy as jnp
import numpy as np
from jax import lax

NX = 64
NZ = 32
NY = 128
LAYERS = 4
N_HORIZ = 8


def block_levels(stream_key, shape, pieces, low, top_value):
    loudness = 1.0
    for dim, parts in pieces:
        steps = jax.random.uniform(jax.random.fold_in(jax.random.fold_in(stream_key, 6), dim), (parts,), jnp.float32, low / len(pieces), top_value / len(pieces))
        loudness = loudness * jnp.repeat(jnp.exp(steps), shape[dim] // parts).reshape((-1,) + (1,) * (len(shape) - 1 - dim))
    return loudness


def centred(stream_key, dims, width, most, pieces=(), dtype=jnp.bfloat16):
    drawn = jax.random.normal(stream_key, dims, jnp.float32) * width
    if len(pieces) > 0:
        drawn = block_levels(stream_key, dims, pieces, -0.22, 0.18) * drawn
    return jnp.clip(drawn, min=-most, max=most).astype(dtype)


def setup_inputs(seed: int = 0) -> dict:
    key_list = jax.random.split(jax.random.key(seed), 4)
    velocity = centred(key_list[0], (3, NX, NZ, NY), 0.5, 3.0, ((1, 8), (2, 4)), jnp.float32)
    heights = jnp.clip(jnp.exp(math.log(2.0) - 1.3862944 * jax.random.uniform(key_list[1], (LAYERS,), jnp.float32) ** block_levels(key_list[1], (LAYERS,), ((0, 4),), -0.2, 0.2)), 0.5, 2.0)
    time_step = jnp.clip(jnp.exp(jax.random.uniform(key_list[2], (), jnp.float32, math.log(0.005), math.log(0.02))), 0.005, 0.02)
    return dict(velocity=velocity, heights=heights, time_step=time_step)


gll_half = [1.0, 0.8717401485096066, 0.5917001814331423, 0.2092992179024789]
gll_half_weights = [0.03571428571428571, 0.21070422714350603, 0.34112269248350436, 0.4124587946587038]
gauss_half = [0.9815606342467192, 0.9041172563704749, 0.7699026741943047, 0.5873179542866175, 0.3678314989981802, 0.1252334085114689]
gauss_half_weights = [0.0471753363865118, 0.1069393259953184, 0.1600783285433462, 0.2031674267230659, 0.2334925365383548, 0.2491470458134028]


def mirrored(values, sign):
    return np.concatenate([sign * np.array(values), np.array(values[::-1])])


def lagrange(targets, sources):
    matrix = np.ones((targets.size, sources.size))
    for j in range(sources.size):
        for k in range(sources.size):
            if k != j:
                matrix[:, j] = matrix[:, j] * (targets - sources[k]) / (sources[j] - sources[k])
    return matrix


def node_tables():
    gll_points = mirrored(gll_half, -1.0)
    gll_weights = mirrored(gll_half_weights, 1.0)
    fine_points = mirrored(gauss_half, -1.0)
    fine_weights = mirrored(gauss_half_weights, 1.0)
    to_fine = lagrange(fine_points, gll_points)
    products = np.ones(8)
    for i in range(8):
        for k in range(8):
            if k != i:
                products[i] = products[i] * (gll_points[i] - gll_points[k])
    deriv_mat = np.zeros((8, 8))
    for i in range(8):
        for j in range(8):
            if i != j:
                deriv_mat[i, j] = products[i] / (products[j] * (gll_points[i] - gll_points[j]))
                deriv_mat[i, i] = deriv_mat[i, i] + 1.0 / (gll_points[i] - gll_points[j])
    return (jnp.asarray(to_fine, jnp.float32), jnp.asarray(to_fine @ deriv_mat, jnp.float32),
            jnp.asarray(gll_weights, jnp.float32), jnp.asarray(fine_weights, jnp.float32))


def to_elements(field):
    comps, nodes_x, nodes_z, nodes_y = field.shape
    grouped = field.reshape(comps, nodes_x // 8, 8, nodes_z // 8, 8, nodes_y // 8, 8)
    return grouped.transpose(0, 2, 4, 6, 1, 3, 5).reshape(comps, 8, 8, 8, -1)


def from_elements(grouped, nodes_x, nodes_z, nodes_y):
    comps = grouped.shape[0]
    grouped = grouped.reshape(comps, 8, 8, 8, nodes_x // 8, nodes_z // 8, nodes_y // 8)
    return grouped.transpose(0, 4, 1, 5, 2, 6, 3).reshape(comps, nodes_x, nodes_z, nodes_y)


def tensor_apply(field, mat_x, mat_z, mat_y):
    hp = lax.Precision.HIGHEST
    partial_value = jnp.einsum('rg,cabge->cabre', mat_y, field, precision=hp)
    partial_value = jnp.einsum('qb,cabre->caqre', mat_z, partial_value, precision=hp)
    return jnp.einsum('pa,caqre->cpqre', mat_x, partial_value, precision=hp)


def element_heights(heights, count_x, count_y):
    return (jnp.ones((count_x, 1, 1), jnp.float32) * heights[None, :, None] * jnp.ones((1, 1, count_y), jnp.float32)).reshape(-1)


def weak_form(field, heights):
    to_fine, deriv_fine, gll_weights, fine_weights = node_tables()
    nodes_x, nodes_z, nodes_y = field.shape[1:]
    height_elem = element_heights(heights, nodes_x // 8, nodes_y // 8)
    grouped = to_elements(field)
    values_fine = tensor_apply(grouped, to_fine, to_fine, to_fine)
    grad_x = tensor_apply(grouped, deriv_fine, to_fine, to_fine) * 2.0
    grad_z = tensor_apply(grouped, to_fine, deriv_fine, to_fine) * (2.0 / height_elem)
    grad_y = tensor_apply(grouped, to_fine, to_fine, deriv_fine) * 2.0
    convect = values_fine[0][None] * grad_x + values_fine[1][None] * grad_y + values_fine[2][None] * grad_z
    quad = fine_weights[:, None, None] * fine_weights[None, :, None] * fine_weights[None, None, :]
    convect = convect * quad[..., None]
    back = tensor_apply(convect, to_fine.T, to_fine.T, to_fine.T) * (height_elem / 8.0)
    return from_elements(back, nodes_x, nodes_z, nodes_y)


def assemble(field, axis_pos, wrap_round):
    layout = field.shape
    count = layout[axis_pos] // 8
    grouped = field.reshape(layout[:axis_pos] + (count, 8) + layout[axis_pos + 1:])
    inner_pos = axis_pos + 1
    first_nodes = lax.index_in_dim(grouped, 0, inner_pos, keepdims=False)
    last_nodes = lax.index_in_dim(grouped, 7, inner_pos, keepdims=False)
    middle = lax.slice_in_dim(grouped, 1, 7, axis=inner_pos)
    if wrap_round:
        summed_nodes = last_nodes + jnp.roll(first_nodes, -1, axis=axis_pos)
        new_first = jnp.roll(summed_nodes, 1, axis=axis_pos)
    else:
        zero_row = jnp.zeros_like(lax.slice_in_dim(first_nodes, 0, 1, axis=axis_pos))
        next_nodes = jnp.concatenate([lax.slice_in_dim(first_nodes, 1, count, axis=axis_pos), zero_row], axis=axis_pos)
        summed_nodes = last_nodes + next_nodes
        new_first = jnp.concatenate([lax.slice_in_dim(first_nodes, 0, 1, axis=axis_pos),
                                     lax.slice_in_dim(summed_nodes, 0, count - 1, axis=axis_pos)], axis=axis_pos)
    grouped = jnp.concatenate([jnp.expand_dims(new_first, inner_pos), middle,
                               jnp.expand_dims(summed_nodes, inner_pos)], axis=inner_pos)
    return grouped.reshape(layout)


def assemble_all(field):
    field = assemble(field, 1, False)
    field = assemble(field, 2, False)
    return assemble(field, 3, True)


def reference(velocity, heights, time_step):
    to_fine, deriv_fine, gll_weights, fine_weights = node_tables()
    cube = gll_weights[:, None, None] * gll_weights[None, :, None] * gll_weights[None, None, :]
    height_elem = element_heights(heights, NX // 8, NY // 8)
    element_mass = cube[None, ..., None] * (height_elem / 8.0)
    mass_total = assemble_all(from_elements(element_mass, NX, NZ, NY))

    def slope(field):
        blocks = field.reshape(3, N_HORIZ, NX // N_HORIZ, NZ, NY).transpose(1, 0, 2, 3, 4)
        weak_terms = lax.map(lambda block: weak_form(block, heights), blocks)
        weak_terms = weak_terms.transpose(1, 0, 2, 3, 4).reshape(field.shape)
        return -assemble_all(weak_terms) / mass_total

    slope_one = slope(velocity)
    slope_two = slope(velocity + 0.5 * time_step * slope_one)
    slope_three = slope(velocity + 0.5 * time_step * slope_two)
    slope_four = slope(velocity + time_step * slope_three)
    return (slope_one + 2.0 * slope_two + 2.0 * slope_three + slope_four) / 6.0
```

```python
import functools

import jax
import jax.numpy as jnp
import ml_dtypes
import numpy as np
from jax import lax
from jax.experimental import pallas as pl
from jax.experimental.pallas import tpu as pltpu
from jax.sharding import PartitionSpec as P

gll_half = [1.0, 0.8717401485096066, 0.5917001814331423, 0.2092992179024789]
gll_half_weights = [
    0.03571428571428571,
    0.21070422714350603,
    0.34112269248350435,
    0.4124587946587038,
]
gauss_half = [
    0.9815606342467192,
    0.9041172563704749,
    0.7699026741943047,
    0.5873179542866175,
    0.3678314989981802,
    0.1252334085114689,
]
gauss_half_weights = [
    0.0471753363865118,
    0.1069393259953184,
    0.1600783285433462,
    0.2031674267230659,
    0.2334925365383548,
    0.2491470458134028,
]

f32 = jnp.float32
bf16 = jnp.bfloat16
ROWS = 192
SPAN = 128
SPAN_ELEMENTS = 16


def mirrored(values, sign):
    return np.concatenate([sign * np.array(values), np.array(values[::-1])])


def lagrange(targets, sources):
    matrix = np.ones((targets.size, sources.size))
    for j in range(sources.size):
        for k in range(sources.size):
            if k != j:
                matrix[:, j] = matrix[:, j] * (targets - sources[k]) / (sources[j] - sources[k])
    return matrix


def node_tables():
    gll_points = mirrored(gll_half, -1.0)
    gll_weights = mirrored(gll_half_weights, 1.0)
    fine_points = mirrored(gauss_half, -1.0)
    fine_weights = mirrored(gauss_half_weights, 1.0)
    to_fine = lagrange(fine_points, gll_points)
    products = np.ones(8)
    for i in range(8):
        for k in range(8):
            if k != i:
                products[i] = products[i] * (gll_points[i] - gll_points[k])
    deriv_mat = np.zeros((8, 8))
    for i in range(8):
        for j in range(8):
            if i != j:
                deriv_mat[i, j] = products[i] / (products[j] * (gll_points[i] - gll_points[j]))
                deriv_mat[i, i] = deriv_mat[i, i] + 1.0 / (gll_points[i] - gll_points[j])
    return to_fine, to_fine @ deriv_mat, gll_weights, fine_weights


def halves(matrix):
    high = matrix.astype(ml_dtypes.bfloat16)
    low = (matrix - high.astype(np.float64)).astype(ml_dtypes.bfloat16)
    return high, low


def stack_rows(matrix):
    high, low = halves(matrix)
    return np.concatenate([high, high, low], axis=0)


def stack_columns(matrix):
    high, low = halves(matrix)
    return np.concatenate([high, high, low], axis=1)


def span_blocks(block, first, count):
    out = np.zeros((SPAN, SPAN_ELEMENTS * count))
    for e in range(SPAN_ELEMENTS):
        out[e * 8 : e * 8 + 8, e * count : (e + 1) * count] = block[first : first + count].T
    return out


@functools.cache
def matrices():
    interp, deriv, gll_w, fine_w = node_tables()
    a_both = np.concatenate([span_blocks(interp, 0, 8), span_blocks(2.0 * deriv, 0, 8)], axis=1)
    span_a = stack_rows(a_both)
    interp_b = span_blocks(interp, 8, 4)
    deriv_b = span_blocks(2.0 * deriv, 8, 4)
    none = np.zeros_like(interp_b)
    first_b = stack_rows(np.concatenate([interp_b, none, deriv_b, none], axis=1))
    second_b = stack_rows(np.concatenate([none, interp_b, none, deriv_b], axis=1))
    span_b = np.concatenate([first_b, second_b], axis=0)
    values = np.kron(interp, interp)
    plane = np.concatenate([values, np.kron(2.0 * deriv, interp), np.kron(interp, 2.0 * deriv)])
    plane = stack_columns(plane)
    values = stack_columns(values)
    back = interp.T * fine_w[None, :] / gll_w[:, None]
    plane_back = stack_columns(-np.kron(back, back))
    a_back = np.zeros((SPAN, SPAN))
    b_back = np.zeros((SPAN // 2, SPAN))
    for e in range(SPAN_ELEMENTS):
        a_back[e * 8 : e * 8 + 8, e * 8 : e * 8 + 8] = back[:, :8].T
        b_back[e * 4 : e * 4 + 4, e * 8 : e * 8 + 8] = back[:, 8:].T
    span = np.concatenate([a_back, b_back], axis=0)
    summed = span.copy()
    for e in range(SPAN_ELEMENTS):
        last, first = e * 8 + 7, (e * 8 + 8) % SPAN
        mean = 0.5 * (span[:, last] + span[:, first])
        summed[:, last] = mean
        summed[:, first] = mean
    a_back, b_back = summed[:SPAN], summed[SPAN:]
    zero_a, zero_b = np.zeros_like(a_back), np.zeros_like(b_back)
    pair_back = np.concatenate(
        [
            np.concatenate([a_back, zero_a], axis=1),
            np.concatenate([zero_a, a_back], axis=1),
            np.concatenate([b_back, zero_b], axis=1),
            np.concatenate([zero_b, b_back], axis=1),
        ],
        axis=0,
    )
    one_back = np.concatenate([a_back, b_back, zero_b], axis=0)
    return span_a, span_b, plane, values, plane_back, stack_rows(pair_back), stack_rows(one_back)


def split(x):
    high = x.astype(bf16)
    return high, (x - high.astype(f32)).astype(bf16)


def dot(a, b):
    return jnp.dot(a, b, preferred_element_type=f32)


def weak_layers(fields, inverse_heights, mats):
    span_a, span_b, plane, values, plane_back, pair_back, one_back = (m[...] for m in mats)
    count = len(fields)
    parts = [split(field) for field in fields]
    lefts = [jnp.concatenate([high, low, high], axis=1) for high, low in parts]
    spots = []
    lane = lax.broadcasted_iota(jnp.int32, (1, SPAN), 1)
    for first in range(0, count, 2):
        group = range(first, min(first + 2, count))
        for l in group:
            out = dot(lefts[l], span_a)
            spots.append((out[:, :SPAN], out[:, SPAN:], inverse_heights[l]))
        if len(group) == 2:
            out = dot(jnp.concatenate([lefts[first], lefts[first + 1]], axis=1), span_b)
            inverse = jnp.where(lane < 64, inverse_heights[first], inverse_heights[first + 1])
        else:
            out = dot(lefts[first], span_b[: 3 * SPAN])
            inverse = inverse_heights[first]
        spots.append((out[:, :SPAN], out[:, SPAN:], inverse))
    backs = []
    for first in range(0, len(spots), 2):
        group = spots[first : first + 2]
        interp, deriv, inverse = (jnp.concatenate([s[i] for s in group], axis=1) for i in range(3))
        planes, spans = [], []
        interp_parts = split(interp)
        deriv_parts = split(deriv)
        for c in range(3):
            rows = slice(c * 64, c * 64 + 64)
            high, low = interp_parts[0][rows], interp_parts[1][rows]
            planes.append(dot(plane, jnp.concatenate([high, low, high], axis=0)))
            high, low = deriv_parts[0][rows], deriv_parts[1][rows]
            spans.append(dot(values, jnp.concatenate([high, low, high], axis=0)))
        speed_x, speed_y = planes[0][:144], planes[1][:144]
        speed_z = planes[2][:144] * inverse
        outs = []
        for c in range(3):
            convect = (
                speed_x * planes[c][144:288] + speed_y * spans[c] + speed_z * planes[c][288:]
            )
            high, low = split(convect)
            outs.append(dot(plane_back, jnp.concatenate([high, low, high], axis=0)))
        out = jnp.concatenate(outs, axis=0)
        for i in range(len(group)):
            backs.append(out[:, i * SPAN : (i + 1) * SPAN])
    results = []
    place = 0
    for first in range(0, count, 2):
        size = min(2, count - first)
        joined = jnp.concatenate(backs[place : place + size + 1], axis=1)
        place += size + 1
        high, low = split(joined)
        left = jnp.concatenate([high, low, high], axis=1)
        out = dot(left, pair_back if size == 2 else one_back)
        for i in range(size):
            results.append(out[:, i * SPAN : (i + 1) * SPAN])
    return results


def join_heights(own, above, below, height, height_above, height_below, has_above, has_below):
    level = lax.broadcasted_iota(jnp.int32, (8, SPAN), 0)
    keep = jnp.ones((8, SPAN), f32)
    out = own.reshape(24, 8, SPAN)
    if above is not None:
        share = jnp.where(has_above, height_above / (height + height_above), 0.0)
        take = jnp.where(level == 7, share, 0.0)
        keep = keep - take
        taken_above = pltpu.roll(above.reshape(24, 8, SPAN), 7, 1) * take[None]
    if below is not None:
        share = jnp.where(has_below, height_below / (height + height_below), 0.0)
        take = jnp.where(level == 0, share, 0.0)
        keep = keep - take
        taken_below = pltpu.roll(below.reshape(24, 8, SPAN), 1, 1) * take[None]
    out = out * keep[None]
    if above is not None:
        out = out + taken_above
    if below is not None:
        out = out + taken_below
    return out.reshape(ROWS, SPAN)


def join_stream(own, cross, core):
    place = lax.axis_index("horiz")
    odd = lax.rem(place, 2) == 1
    left = jnp.where(odd, core, cross)
    right = jnp.where(odd, cross, core)
    left_share = jnp.where(place > 0, 0.5, 0.0).astype(f32)
    right_share = jnp.where(place < lax.axis_size("horiz") - 1, 0.5, 0.0).astype(f32)
    own = own.reshape(3, 8, 8, SPAN)
    first = own[:, 0] * (1.0 - left_share) + left * left_share
    last = own[:, 7] * (1.0 - right_share) + right * right_share
    out = jnp.concatenate([first[:, None], own[:, 1:7], last[:, None]], axis=1)
    return out.reshape(ROWS, SPAN)


def put_faces(own, cross_ref, core_ref, at):
    odd = lax.rem(lax.axis_index("horiz"), 2) == 1
    own = own.reshape(3, 8, 8, SPAN)
    first, last = own[:, 0], own[:, 7]
    cross_ref[at] = jnp.where(odd, last, first)
    core_ref[at] = jnp.where(odd, first, last)


def put_layers(results, heights, partial_ref, cross_ref, core_ref):
    count = len(results)
    for l in range(count):
        above = results[l + 1] if l + 1 < count else None
        below = results[l - 1] if l > 0 else None
        joined = join_heights(
            results[l],
            above,
            below,
            heights[l],
            heights[l + 1] if l + 1 < count else None,
            heights[l - 1] if l > 0 else None,
            True,
            True,
        )
        partial_ref[l] = joined
        put_faces(joined, cross_ref, core_ref, l)


def pack_kernel(velocity_ref, height_ref, packed_ref):
    packed_ref[:ROWS] = velocity_ref[...]
    packed_ref[ROWS:] = jnp.full((8, SPAN), height_ref[0], f32)


def own_layer_kernel(*refs):
    mats, (packed_ref, out_ref) = refs[:7], refs[7:]
    inverse = 1.0 / packed_ref[ROWS : ROWS + 1]
    out_ref[...] = weak_layers([packed_ref[:ROWS]], [inverse], mats)[0]


def other_layers_kernel(count, *refs):
    mats, refs = refs[:7], refs[7:]
    packed, done_ref = refs[:count], refs[count]
    field_ref, heights_ref, partial_ref, cross_ref, core_ref, raw_ref = refs[count + 1 :]
    place = lax.axis_index("vert")
    slots = [jnp.bitwise_xor(place, j) for j in range(count)]
    for j in range(count):
        field_ref[slots[j]] = packed[j][:ROWS]
        heights_ref[slots[j]] = packed[j][ROWS:]
    raw_ref[place] = done_ref[...]
    if count > 1:
        results = weak_layers(
            [packed[j][:ROWS] for j in range(1, count)],
            [1.0 / packed[j][ROWS : ROWS + 1] for j in range(1, count)],
            mats,
        )
        for j in range(1, count):
            raw_ref[slots[j]] = results[j - 1]
    heights = [heights_ref[l] for l in range(count)]
    put_layers([raw_ref[l] for l in range(count)], heights, partial_ref, cross_ref, core_ref)


def first_kernel(count, *refs):
    mats, refs = refs[:7], refs[7:]
    packed_ref, field_ref, heights_ref, partial_ref, cross_ref, core_ref = refs
    for l in range(count):
        field_ref[l] = packed_ref[l, :ROWS]
        heights_ref[l] = packed_ref[l, ROWS:]
    heights = [packed_ref[l, ROWS:] for l in range(count)]
    results = weak_layers(
        [packed_ref[l, :ROWS] for l in range(count)], [1.0 / h[:1] for h in heights], mats
    )
    put_layers(results, heights, partial_ref, cross_ref, core_ref)


def middle_kernel(count, step_share, first, *refs):
    mats, refs = refs[:7], refs[7:]
    step_ref, field_ref, heights_ref, partial_ref, cross_ref, core_ref = refs[:6]
    refs = refs[6:]
    if first:
        total = None
    else:
        total, refs = refs[0][...], refs[1:]
    total_ref, next_partial_ref, next_cross_ref, next_core_ref = refs
    place = lax.axis_index("vert")
    step = step_ref[0] * step_share
    own = join_stream(partial_ref[place], cross_ref[place], core_ref[place])
    total_ref[...] = own if first else total + 2.0 * own
    fields = []
    for l in range(count):
        slope = join_stream(partial_ref[l], cross_ref[l], core_ref[l])
        fields.append(field_ref[l] + step * slope)
    heights = [heights_ref[l] for l in range(count)]
    results = weak_layers(fields, [1.0 / h[:1] for h in heights], mats)
    put_layers(results, heights, next_partial_ref, next_cross_ref, next_core_ref)


def last_kernel(count, *refs):
    mats, refs = refs[:7], refs[7:]
    step_ref, field_ref, heights_ref, partial_ref, cross_ref, core_ref, total_ref = refs[:7]
    next_total_ref, next_partial_ref, next_cross_ref, next_core_ref = refs[7:]
    place = lax.axis_index("vert")
    step = step_ref[0]
    layers = [place, jnp.minimum(place + 1, count - 1), jnp.maximum(place - 1, 0)]
    fields, heights = [], []
    for l in layers:
        slope = join_stream(partial_ref[l], cross_ref[l], core_ref[l])
        if not fields:
            next_total_ref[...] = total_ref[...] + 2.0 * slope
        fields.append(field_ref[l] + step * slope)
        heights.append(heights_ref[l])
    own, above, below = weak_layers(fields, [1.0 / h[:1] for h in heights], mats)
    joined = join_heights(own, above, below, *heights, place < count - 1, place > 0)
    next_partial_ref[...] = joined
    put_faces(joined, next_cross_ref, next_core_ref, slice(None))


def rate_kernel(partial_ref, cross_ref, core_ref, total_ref, rate_ref):
    slope = join_stream(partial_ref[...], cross_ref[...], core_ref[...])
    rate_ref[...] = (total_ref[...] + slope) / 6.0


VMEM = pl.BlockSpec(memory_space=pltpu.VMEM)
SMEM = pl.BlockSpec(memory_space=pltpu.SMEM)


def call(kernel, outs, args, smem=(), scratch=(), flops=0):
    shapes = [jax.ShapeDtypeStruct(shape, f32) for shape in outs]
    one = len(shapes) == 1
    return pl.pallas_call(
        kernel,
        out_shape=shapes[0] if one else shapes,
        in_specs=[SMEM if i in smem else VMEM for i in range(len(args))],
        out_specs=VMEM if one else [VMEM] * len(shapes),
        scratch_shapes=list(scratch),
        compiler_params=pltpu.CompilerParams(vmem_limit_bytes=48 * 1024 * 1024),
        cost_estimate=pl.CostEstimate(flops=flops, bytes_accessed=1 << 20, transcendentals=0),
    )(*args)


def swap_stream(cross, core):
    count = lax.axis_size("horiz")
    cores = [(i, i ^ 1) for i in range(count)]
    crosses = [(i, (i + 1) % count if i % 2 else (i - 1) % count) for i in range(count)]
    return lax.ppermute(cross, "horiz", crosses), lax.ppermute(core, "horiz", cores)


def on_device(velocity, heights, time_step):
    layers = lax.axis_size("vert")
    mats = [jnp.asarray(m) for m in matrices()]
    unit = 2 * 256 * 256 * 3000
    field = (layers, ROWS, SPAN)
    face = (layers, 3, 8, SPAN)
    small = (3, 8, SPAN)
    first_outs = [field, (layers, 8, SPAN), field, face, face]
    step = time_step.reshape(1)
    packed = call(
        pack_kernel, [(ROWS + 8, SPAN)], [velocity.reshape(ROWS, SPAN), heights], smem=(1,)
    )
    if layers in (1, 2, 4):
        slots = [packed]
        for j in range(1, layers):
            slots.append(lax.ppermute(packed, "vert", [(i, i ^ j) for i in range(layers)]))
        own = call(own_layer_kernel, [(ROWS, SPAN)], mats + [packed], flops=unit)
        fields, all_heights, partial, cross, core = call(
            functools.partial(other_layers_kernel, layers),
            first_outs,
            mats + slots + [own],
            scratch=[pltpu.VMEM(field, f32)],
            flops=(layers - 1) * unit,
        )
    else:
        gathered = lax.all_gather(packed, "vert")
        fields, all_heights, partial, cross, core = call(
            functools.partial(first_kernel, layers), first_outs, mats + [gathered]
        )
    cross, core = swap_stream(cross, core)
    total = None
    for stage in range(2):
        args = mats + [step, fields, all_heights, partial, cross, core]
        if stage:
            args.append(total)
        total, partial, cross, core = call(
            functools.partial(middle_kernel, layers, 0.5, stage == 0),
            [(ROWS, SPAN), field, face, face],
            args,
            smem=(7,),
            flops=layers * unit,
        )
        cross, core = swap_stream(cross, core)
    total, partial, cross, core = call(
        functools.partial(last_kernel, layers),
        [(ROWS, SPAN), (ROWS, SPAN), small, small],
        mats + [step, fields, all_heights, partial, cross, core, total],
        smem=(7,),
        flops=3 * unit,
    )
    cross, core = swap_stream(cross, core)
    rate = call(rate_kernel, [(ROWS, SPAN)], [partial, cross, core, total])
    return rate.reshape(velocity.shape)


def solution(mesh):
    in_specs = (P(None, "horiz", "vert", None), P("vert"), P())
    out_specs = P(None, "horiz", "vert", None)
    return jax.shard_map(
        on_device, mesh=mesh, in_specs=in_specs, out_specs=out_specs, check_vma=False
    )
```

```python
import functools

import jax
import jax.numpy as jnp
import ml_dtypes
import numpy as np
from jax import lax
from jax.experimental import pallas as pl
from jax.experimental.pallas import tpu as pltpu
from jax.sharding import PartitionSpec as P

gll_half = [1.0, 0.8717401485096066, 0.5917001814331423, 0.2092992179024789]
gll_half_weights = [
    0.03571428571428571,
    0.21070422714350603,
    0.34112269248350435,
    0.4124587946587038,
]
gauss_half = [
    0.9815606342467192,
    0.9041172563704749,
    0.7699026741943047,
    0.5873179542866175,
    0.3678314989981802,
    0.1252334085114689,
]
gauss_half_weights = [
    0.0471753363865118,
    0.1069393259953184,
    0.1600783285433462,
    0.2031674267230659,
    0.2334925365383548,
    0.2491470458134028,
]

f32 = jnp.float32
bf16 = jnp.bfloat16
ROWS = 192
SPAN = 128
SPAN_ELEMENTS = 16


def mirrored(values, sign):
    return np.concatenate([sign * np.array(values), np.array(values[::-1])])


def lagrange(targets, sources):
    matrix = np.ones((targets.size, sources.size))
    for j in range(sources.size):
        for k in range(sources.size):
            if k != j:
                matrix[:, j] = matrix[:, j] * (targets - sources[k]) / (sources[j] - sources[k])
    return matrix


def node_tables():
    gll_points = mirrored(gll_half, -1.0)
    gll_weights = mirrored(gll_half_weights, 1.0)
    fine_points = mirrored(gauss_half, -1.0)
    fine_weights = mirrored(gauss_half_weights, 1.0)
    to_fine = lagrange(fine_points, gll_points)
    products = np.ones(8)
    for i in range(8):
        for k in range(8):
            if k != i:
                products[i] = products[i] * (gll_points[i] - gll_points[k])
    deriv_mat = np.zeros((8, 8))
    for i in range(8):
        for j in range(8):
            if i != j:
                deriv_mat[i, j] = products[i] / (products[j] * (gll_points[i] - gll_points[j]))
                deriv_mat[i, i] = deriv_mat[i, i] + 1.0 / (gll_points[i] - gll_points[j])
    return to_fine, to_fine @ deriv_mat, gll_weights, fine_weights


def halves(matrix):
    high = matrix.astype(ml_dtypes.bfloat16)
    low = (matrix - high.astype(np.float64)).astype(ml_dtypes.bfloat16)
    return high, low


def stack_columns(matrix):
    high, low = halves(matrix)
    return np.concatenate([high, high, low], axis=1)


def span_blocks(block, first, count):
    out = np.zeros((SPAN, SPAN_ELEMENTS * count))
    for e in range(SPAN_ELEMENTS):
        out[e * 8 : e * 8 + 8, e * count : (e + 1) * count] = block[first : first + count].T
    return out


@functools.cache
def matrices():
    interp, deriv, gll_w, fine_w = node_tables()
    a_both = np.concatenate([span_blocks(interp, 0, 8), span_blocks(2.0 * deriv, 0, 8)], axis=1)
    span_a = np.concatenate(halves(a_both), axis=0)
    interp_b = span_blocks(interp, 8, 4)
    deriv_b = span_blocks(2.0 * deriv, 8, 4)
    none = np.zeros_like(interp_b)
    first_b = halves(np.concatenate([interp_b, none, deriv_b, none], axis=1))
    second_b = halves(np.concatenate([none, interp_b, none, deriv_b], axis=1))
    span_b = np.concatenate(first_b + second_b, axis=0)
    values = np.kron(interp, interp)
    plane = np.concatenate([values, np.kron(2.0 * deriv, interp), np.kron(interp, 2.0 * deriv)])
    plane = stack_columns(plane)
    values = stack_columns(values)
    back = interp.T * fine_w[None, :] / gll_w[:, None]
    plane_back = stack_columns(-np.kron(back, back))
    a_back = np.zeros((SPAN, SPAN))
    b_back = np.zeros((SPAN // 2, SPAN))
    for e in range(SPAN_ELEMENTS):
        a_back[e * 8 : e * 8 + 8, e * 8 : e * 8 + 8] = back[:, :8].T
        b_back[e * 4 : e * 4 + 4, e * 8 : e * 8 + 8] = back[:, 8:].T
    span = np.concatenate([a_back, b_back], axis=0)
    summed = span.copy()
    for e in range(SPAN_ELEMENTS):
        last, first = e * 8 + 7, (e * 8 + 8) % SPAN
        mean = 0.5 * (span[:, last] + span[:, first])
        summed[:, last] = mean
        summed[:, first] = mean
    a_back, b_back = summed[:SPAN], summed[SPAN:]
    zero_a, zero_b = np.zeros_like(a_back), np.zeros_like(b_back)
    pair_back = np.concatenate(
        [
            np.concatenate([a_back, zero_a], axis=1),
            np.concatenate([zero_a, a_back], axis=1),
            np.concatenate([b_back, zero_b], axis=1),
            np.concatenate([zero_b, b_back], axis=1),
        ],
        axis=0,
    )
    wide = {
        "span_a": span_a,
        "span_b": span_b,
        "plane": plane,
        "values": values,
        "plane_back": plane_back[:, :256],
        "plane_back_rest": plane_back[:, 256:],
        "pair_back": np.concatenate(halves(pair_back), axis=0),
    }
    rows, places = [], {}
    start = 0
    for name, matrix in wide.items():
        places[name] = (start, matrix.shape[0], matrix.shape[1])
        rows.append(np.pad(matrix, ((0, 0), (0, 256 - matrix.shape[1]))))
        start += matrix.shape[0]
    return np.concatenate(rows, axis=0), places


def read(mats_ref, name):
    start, count, width = matrices()[1][name]
    return mats_ref[start : start + count, :width]


def read_rows(mats_ref, name, *pieces):
    start, count, width = matrices()[1][name]
    half = count // 2
    out = []
    for offset in (0, 0, half):
        for first, rows in pieces:
            at = start + offset + first
            out.append(mats_ref[at : at + rows, :width])
    return jnp.concatenate(out, axis=0)


def read_span_a(mats_ref):
    return read_rows(mats_ref, "span_a", (0, SPAN))


def read_span_b(mats_ref):
    start = matrices()[1]["span_b"][0]
    order = (0, 0, 1, 2, 2, 3)
    return jnp.concatenate(
        [mats_ref[start + i * SPAN : start + i * SPAN + SPAN] for i in order], axis=0
    )


def read_back(mats_ref, size):
    if size == 2:
        return read_rows(mats_ref, "pair_back", (0, 3 * SPAN))
    return read_rows(mats_ref, "pair_back", (0, SPAN), (2 * SPAN, SPAN))[:, :SPAN]


def split(x):
    high = x.astype(bf16)
    return high, (x - high.astype(f32)).astype(bf16)


def dot(a, b):
    return jnp.dot(a, b, preferred_element_type=f32)


def triple(x, axis):
    high, low = split(x)
    return jnp.concatenate([high, low, high], axis=axis)


def spots_of(count):
    spots = []
    for first in range(0, count, 2):
        group = tuple(range(first, min(first + 2, count)))
        spots += [(l,) for l in group] + [group + (None,) * (3 - len(group))]
    return spots


def chunks_of(count):
    spots = spots_of(count)
    return [spots[first : first + 2] for first in range(0, len(spots), 2)]


def span_forward(fields, mats):
    span_a, span_b = read_span_a(mats), read_span_b(mats)
    lefts = [triple(field, 1) for field in fields]
    spots = []
    for spot in spots_of(len(fields)):
        if len(spot) == 1:
            out = dot(lefts[spot[0]], span_a)
        elif spot[1] is None:
            out = dot(lefts[spot[0]], span_b[: 3 * SPAN])
        else:
            out = dot(jnp.concatenate([lefts[spot[0]], lefts[spot[1]]], axis=1), span_b)
        spots.append((out[:, :SPAN], out[:, SPAN:]))
    return spots


def plane_forward(spots, mats):
    plane, values = read(mats, "plane"), read(mats, "values")
    interp, deriv = (jnp.concatenate([s[i] for s in spots], axis=1) for i in range(2))
    interp, deriv = split(interp), split(deriv)
    outs = []
    for c in range(3):
        rows = slice(c * 64, c * 64 + 64)
        high, low = interp[0][rows], interp[1][rows]
        first = dot(plane, jnp.concatenate([high, low, high], axis=0))
        high, low = deriv[0][rows], deriv[1][rows]
        outs.append((first, dot(values, jnp.concatenate([high, low, high], axis=0))))
    return outs


def chunk_inverse(chunk, inverses):
    lane = lax.broadcasted_iota(jnp.int32, (1, SPAN), 1)
    out = []
    for spot in chunk:
        if len(spot) == 1 or spot[1] is None:
            out.append(inverses[spot[0]])
        else:
            out.append(jnp.where(lane < 64, inverses[spot[0]], inverses[spot[1]]))
    return jnp.concatenate(out, axis=1)


def convect_back(fine, inverse, mats):
    back = jnp.concatenate([read(mats, "plane_back"), read(mats, "plane_back_rest")], axis=1)
    parts = [([], []) for _ in range(3)]
    for first in range(0, 144, 48):
        rows = slice(first, first + 48)
        speeds = [fine(c, 0, rows) for c in range(3)]
        speeds[2] = speeds[2] * inverse
        for c in range(3):
            convect = (
                speeds[0] * fine(c, 1, rows)
                + speeds[1] * fine(c, 3, rows)
                + speeds[2] * fine(c, 2, rows)
            )
            for part, half in zip(parts[c], split(convect)):
                part.append(half)
    outs = []
    for high, low in parts:
        outs.append(dot(back, jnp.concatenate(high + low + high, axis=0)))
    return jnp.concatenate(outs, axis=0)


def span_back(count, backs, results, mats):
    for place, spot in enumerate(spots_of(count)):
        if len(spot) == 1 or place >= len(backs) or spot[0] < len(results):
            continue
        size = 1 if spot[1] is None else 2
        joined = jnp.concatenate(backs[place - size : place + 1], axis=1)
        out = dot(triple(joined, 1), read_back(mats, size))
        results += [out[:, i * SPAN : (i + 1) * SPAN] for i in range(size)]


def weak_layers(fields, inverses, mats):
    return weak_spots(span_forward(fields, mats), inverses, mats)


def weak_spots(spots, inverses, mats):
    count = len(inverses)
    chunks = chunks_of(count)
    planes = []
    backs, results = [], []

    def finish(i):
        def fine(c, kind, rows):
            first, along_y = planes[i][c]
            if kind == 3:
                return along_y[rows]
            return first[kind * 144 + rows.start : kind * 144 + rows.stop]

        out = convect_back(fine, chunk_inverse(chunks[i], inverses), mats)
        backs.extend(out[:, j * SPAN : (j + 1) * SPAN] for j in range(len(chunks[i])))
        span_back(count, backs, results, mats)

    for i in range(len(chunks)):
        planes.append(plane_forward(spots[2 * i : 2 * i + 2], mats))
        if i > 0:
            finish(i - 1)
    finish(len(chunks) - 1)
    return results


def face_spots(faces, mats):
    out_a = dot(triple(jnp.concatenate(faces, axis=0), 1), read_span_a(mats))
    even, odd = faces[0::2], faces[1::2]
    odd = odd + [jnp.zeros_like(faces[0])] * (len(even) - len(odd))
    even, odd = (triple(jnp.concatenate(x, axis=0), 1) for x in (even, odd))
    out_b = dot(jnp.concatenate([even, odd], axis=1), read_span_b(mats))
    spots = []
    for spot in spots_of(len(faces)):
        if len(spot) == 1:
            out = out_a[spot[0] * 48 : spot[0] * 48 + 48]
        else:
            out = out_b[spot[0] * 24 : spot[0] * 24 + 48]
        spots.append((out[:, :SPAN], out[:, SPAN:]))
    return spots


def with_faces(inner, faces):
    inner = inner.reshape(3, 6, 8, SPAN)
    faces = faces.reshape(3, 2, 8, SPAN)
    return jnp.concatenate([faces[:, :1], inner, faces[:, 1:]], axis=1).reshape(ROWS, SPAN)


def join_heights(own, above, below, height, height_above, height_below, has_above, has_below):
    level = lax.broadcasted_iota(jnp.int32, (8, SPAN), 0)
    keep = jnp.ones((8, SPAN), f32)
    out = own.reshape(24, 8, SPAN)
    if above is not None:
        share = jnp.where(has_above, height_above / (height + height_above), 0.0)
        take = jnp.where(level == 7, share, 0.0)
        keep = keep - take
        taken_above = pltpu.roll(above.reshape(24, 8, SPAN), 7, 1) * take[None]
    if below is not None:
        share = jnp.where(has_below, height_below / (height + height_below), 0.0)
        take = jnp.where(level == 0, share, 0.0)
        keep = keep - take
        taken_below = pltpu.roll(below.reshape(24, 8, SPAN), 1, 1) * take[None]
    out = out * keep[None]
    if above is not None:
        out = out + taken_above
    if below is not None:
        out = out + taken_below
    return out.reshape(ROWS, SPAN)


def sides():
    place = lax.axis_index("horiz")
    left_share = jnp.where(place > 0, 0.5, 0.0).astype(f32)
    right_share = jnp.where(place < lax.axis_size("horiz") - 1, 0.5, 0.0).astype(f32)
    return lax.rem(place, 2) == 1, left_share, right_share


def join_ends(own, cross, core):
    odd, left_share, right_share = sides()
    left = jnp.where(odd, core, cross)
    right = jnp.where(odd, cross, core)
    own = own.reshape(3, 8, 8, SPAN)
    first = own[:, 0] * (1.0 - left_share) + left * left_share
    last = own[:, 7] * (1.0 - right_share) + right * right_share
    return first, last


def join_stream(own, cross, core):
    first, last = join_ends(own, cross, core)
    own = own.reshape(3, 8, 8, SPAN)
    out = jnp.concatenate([first[:, None], own[:, 1:7], last[:, None]], axis=1)
    return out.reshape(ROWS, SPAN)


def put_faces(own, cross_ref, core_ref, at):
    odd = lax.rem(lax.axis_index("horiz"), 2) == 1
    own = own.reshape(3, 8, 8, SPAN)
    first, last = own[:, 0], own[:, 7]
    cross_ref[at] = jnp.where(odd, last, first)
    core_ref[at] = jnp.where(odd, first, last)


def put_layers(results, heights, partial_ref, cross_ref, core_ref):
    count = len(results)
    for l in range(count):
        above = results[l + 1] if l + 1 < count else None
        below = results[l - 1] if l > 0 else None
        joined = join_heights(
            results[l],
            above,
            below,
            heights[l],
            heights[l + 1] if l + 1 < count else None,
            heights[l - 1] if l > 0 else None,
            True,
            True,
        )
        partial_ref[l] = joined
        put_faces(joined, cross_ref, core_ref, l)


def pack_kernel(velocity_ref, height_ref, packed_ref):
    packed_ref[:ROWS] = velocity_ref[...]
    packed_ref[ROWS:] = jnp.broadcast_to(height_ref[...], (8, SPAN))


def own_layer_kernel(mats, packed_ref, step_ref, out_ref, step_tile_ref):
    inverse = 1.0 / packed_ref[ROWS : ROWS + 1]
    out_ref[...] = weak_layers([packed_ref[:ROWS]], [inverse], mats)[0]
    step_tile_ref[...] = jnp.broadcast_to(step_ref[...], (8, SPAN))


def other_layers_kernel(count, *refs):
    mats, packed, done_ref, refs = refs[0], refs[1 : count + 1], refs[count + 1], refs[count + 2 :]
    field_ref, heights_ref, partial_ref, cross_ref, core_ref, raw_ref = refs
    place = lax.axis_index("vert")
    slots = [jnp.bitwise_xor(place, j) for j in range(count)]
    for j in range(count):
        field_ref[slots[j]] = packed[j][:ROWS]
        heights_ref[slots[j]] = packed[j][ROWS:]
    raw_ref[place] = done_ref[...]
    if count > 1:
        results = weak_layers(
            [packed[j][:ROWS] for j in range(1, count)],
            [1.0 / packed[j][ROWS : ROWS + 1] for j in range(1, count)],
            mats,
        )
        for j in range(1, count):
            raw_ref[slots[j]] = results[j - 1]
    heights = [heights_ref[l] for l in range(count)]
    put_layers([raw_ref[l] for l in range(count)], heights, partial_ref, cross_ref, core_ref)


def first_kernel(count, *refs):
    mats, refs = refs[0], refs[1:]
    packed_ref, step_ref, field_ref, heights_ref, partial_ref, cross_ref, core_ref = refs[:7]
    refs[7][...] = jnp.broadcast_to(step_ref[...], (8, SPAN))
    heights = [packed_ref[l, ROWS:] for l in range(count)]
    for l in range(count):
        field_ref[l] = packed_ref[l, :ROWS]
        heights_ref[l] = heights[l]
    results = weak_layers(
        [packed_ref[l, :ROWS] for l in range(count)], [1.0 / h[:1] for h in heights], mats
    )
    put_layers(results, heights, partial_ref, cross_ref, core_ref)


def stage_layers(count, last):
    if not last:
        return list(range(count))
    place = lax.axis_index("vert")
    return [place, jnp.minimum(place + 1, count - 1), jnp.maximum(place - 1, 0)]


def inner_kernel(count, share, last, mats, step_ref, field_ref, partial_ref, spots_ref):
    step = step_ref[:1] * share
    fields = []
    for l in stage_layers(count, last):
        field = (field_ref[l] + step * partial_ref[l]).reshape(3, 8, 8, SPAN)
        fields.append(field[:, 1:7].reshape(144, SPAN))
    for i, pair in enumerate(span_forward(fields, mats)):
        for part in range(2):
            spots_ref[i, part] = pair[part]


def stage_kernel(count, share, first, last, *refs):
    mats, step_ref, field_ref, heights_ref, partial_ref, cross_ref, core_ref, spots_ref = refs[:8]
    refs = refs[8:]
    total = None if first else refs[0][...]
    total_ref, next_partial_ref, next_cross_ref, next_core_ref = refs[-4:]
    place = lax.axis_index("vert")
    step = step_ref[:1] * share
    layers = stage_layers(count, last)
    heights = [heights_ref[l] for l in layers]
    faces = []
    for l in layers:
        ends = join_ends(partial_ref[l], cross_ref[l], core_ref[l])
        ends = jnp.concatenate([end[:, None] for end in ends], axis=1)
        field = field_ref[l].reshape(3, 8, 8, SPAN)
        field = jnp.concatenate([field[:, :1], field[:, 7:]], axis=1)
        faces.append((field + step * ends).reshape(48, SPAN))
    spots = []
    for i, pair in enumerate(face_spots(faces, mats)):
        spots.append([with_faces(spots_ref[i, part], pair[part]) for part in range(2)])
    results = weak_spots(spots, [1.0 / h[:1] for h in heights], mats)
    own = join_stream(partial_ref[place], cross_ref[place], core_ref[place])
    total_ref[...] = own if first else total + 2.0 * own
    if last:
        joined = join_heights(*results, *heights, place < count - 1, place > 0)
        next_partial_ref[...] = joined
        put_faces(joined, next_cross_ref, next_core_ref, slice(None))
    else:
        put_layers(results, heights, next_partial_ref, next_cross_ref, next_core_ref)


def rate_kernel(partial_ref, cross_ref, core_ref, total_ref, rate_ref):
    slope = join_stream(partial_ref[...], cross_ref[...], core_ref[...])
    rate_ref[...] = (total_ref[...] + slope) / 6.0


VMEM = pl.BlockSpec(memory_space=pltpu.VMEM)


def call(kernel, outs, args, scratch=(), flops=0):
    shapes = [jax.ShapeDtypeStruct(shape, f32) for shape in outs]
    one = len(shapes) == 1
    return pl.pallas_call(
        kernel,
        out_shape=shapes[0] if one else shapes,
        in_specs=[VMEM] * len(args),
        out_specs=VMEM if one else [VMEM] * len(shapes),
        scratch_shapes=list(scratch),
        compiler_params=pltpu.CompilerParams(vmem_limit_bytes=32 * 1024 * 1024),
        cost_estimate=pl.CostEstimate(flops=flops, bytes_accessed=1 << 20, transcendentals=0),
    )(*args)


def swap_stream(cross, core):
    count = lax.axis_size("horiz")
    cores = [(i, i ^ 1) for i in range(count)]
    crosses = [(i, (i + 1) % count if i % 2 else (i - 1) % count) for i in range(count)]
    return lax.ppermute(cross, "horiz", crosses), lax.ppermute(core, "horiz", cores)


def on_device(velocity, heights, time_step):
    layers = lax.axis_size("vert")
    mats = jnp.asarray(matrices()[0])
    unit = 2 * 256 * 256 * 3000
    field = (layers, ROWS, SPAN)
    face = (layers, 3, 8, SPAN)
    small = (3, 8, SPAN)
    first_outs = [field, (layers, 8, SPAN), field, face, face]
    step = time_step.reshape(1, 1)
    tile = (8, SPAN)
    packed = call(
        pack_kernel,
        [(ROWS + 8, SPAN)],
        [velocity.reshape(ROWS, SPAN), heights.reshape(1, 1)],
    )
    if layers in (1, 2, 4):
        slots = [packed]
        for j in range(1, layers):
            slots.append(lax.ppermute(packed, "vert", [(i, i ^ j) for i in range(layers)]))
        own, step = call(own_layer_kernel, [(ROWS, SPAN), tile], [mats, packed, step], flops=unit)
        fields, all_heights, partial, cross, core = call(
            functools.partial(other_layers_kernel, layers),
            first_outs,
            [mats] + slots + [own],
            scratch=[pltpu.VMEM(field, f32)],
            flops=(layers - 1) * unit,
        )
    else:
        gathered = lax.all_gather(packed, "vert")
        fields, all_heights, partial, cross, core, step = call(
            functools.partial(first_kernel, layers), first_outs + [tile], [mats, gathered, step]
        )
    cross, core = swap_stream(cross, core)
    total = None
    for stage, share in enumerate((0.5, 0.5, 1.0)):
        last = stage == 2
        used = 3 if last else layers
        spots = call(
            functools.partial(inner_kernel, layers, share, last),
            [(len(spots_of(used)), 2, 144, SPAN)],
            [mats, step, fields, partial],
            flops=used * unit // 4,
        )
        args = [mats, step, fields, all_heights, partial, cross, core, spots]
        total, partial, cross, core = call(
            functools.partial(stage_kernel, layers, share, stage == 0, last),
            [(ROWS, SPAN)] + ([(ROWS, SPAN), small, small] if last else [field, face, face]),
            args + ([] if stage == 0 else [total]),
            flops=used * unit,
        )
        cross, core = swap_stream(cross, core)
    rate = call(rate_kernel, [(ROWS, SPAN)], [partial, cross, core, total])
    return rate.reshape(velocity.shape)


def solution(mesh):
    in_specs = (P(None, "horiz", "vert", None), P("vert"), P())
    out_specs = P(None, "horiz", "vert", None)
    return jax.shard_map(
        on_device, mesh=mesh, in_specs=in_specs, out_specs=out_specs, check_vma=False
    )
```

```python
import functools

import jax
import jax.numpy as jnp
import ml_dtypes
import numpy as np
from jax import lax
from jax.experimental import pallas as pl
from jax.experimental.pallas import tpu as pltpu
from jax.sharding import PartitionSpec as P

gll_half = [1.0, 0.8717401485096066, 0.5917001814331423, 0.2092992179024789]
gll_half_weights = [
    0.03571428571428571,
    0.21070422714350603,
    0.34112269248350435,
    0.4124587946587038,
]
gauss_half = [
    0.9815606342467192,
    0.9041172563704749,
    0.7699026741943047,
    0.5873179542866175,
    0.3678314989981802,
    0.1252334085114689,
]
gauss_half_weights = [
    0.0471753363865118,
    0.1069393259953184,
    0.1600783285433462,
    0.2031674267230659,
    0.2334925365383548,
    0.2491470458134028,
]

f32 = jnp.float32
bf16 = jnp.bfloat16
ROWS = 192
SPAN = 128
SPAN_ELEMENTS = 16


def mirrored(values, sign):
    return np.concatenate([sign * np.array(values), np.array(values[::-1])])


def lagrange(targets, sources):
    matrix = np.ones((targets.size, sources.size))
    for j in range(sources.size):
        for k in range(sources.size):
            if k != j:
                matrix[:, j] = matrix[:, j] * (targets - sources[k]) / (sources[j] - sources[k])
    return matrix


def node_tables():
    gll_points = mirrored(gll_half, -1.0)
    gll_weights = mirrored(gll_half_weights, 1.0)
    fine_points = mirrored(gauss_half, -1.0)
    fine_weights = mirrored(gauss_half_weights, 1.0)
    to_fine = lagrange(fine_points, gll_points)
    products = np.ones(8)
    for i in range(8):
        for k in range(8):
            if k != i:
                products[i] = products[i] * (gll_points[i] - gll_points[k])
    deriv_mat = np.zeros((8, 8))
    for i in range(8):
        for j in range(8):
            if i != j:
                deriv_mat[i, j] = products[i] / (products[j] * (gll_points[i] - gll_points[j]))
                deriv_mat[i, i] = deriv_mat[i, i] + 1.0 / (gll_points[i] - gll_points[j])
    return to_fine, to_fine @ deriv_mat, gll_weights, fine_weights


def halves(matrix):
    high = matrix.astype(ml_dtypes.bfloat16)
    low = (matrix - high.astype(np.float64)).astype(ml_dtypes.bfloat16)
    return high, low


def stack_columns(matrix):
    high, low = halves(matrix)
    return np.concatenate([high, high, low], axis=1)


def span_blocks(block, first, count):
    out = np.zeros((SPAN, SPAN_ELEMENTS * count))
    for e in range(SPAN_ELEMENTS):
        out[e * 8 : e * 8 + 8, e * count : (e + 1) * count] = block[first : first + count].T
    return out


@functools.cache
def matrices():
    interp, deriv, gll_w, fine_w = node_tables()
    a_both = np.concatenate([span_blocks(interp, 0, 8), span_blocks(2.0 * deriv, 0, 8)], axis=1)
    span_a = np.concatenate(halves(a_both), axis=0)
    interp_b = span_blocks(interp, 8, 4)
    deriv_b = span_blocks(2.0 * deriv, 8, 4)
    none = np.zeros_like(interp_b)
    first_b = halves(np.concatenate([interp_b, none, deriv_b, none], axis=1))
    second_b = halves(np.concatenate([none, interp_b, none, deriv_b], axis=1))
    span_b = np.concatenate(first_b + second_b, axis=0)
    values = np.kron(interp, interp)
    plane = np.concatenate([values, np.kron(2.0 * deriv, interp), np.kron(interp, 2.0 * deriv)])
    plane = stack_columns(plane)
    values = stack_columns(values)
    back = interp.T * fine_w[None, :] / gll_w[:, None]
    plane_back = stack_columns(-np.kron(back, back))
    a_back = np.zeros((SPAN, SPAN))
    b_back = np.zeros((SPAN // 2, SPAN))
    for e in range(SPAN_ELEMENTS):
        a_back[e * 8 : e * 8 + 8, e * 8 : e * 8 + 8] = back[:, :8].T
        b_back[e * 4 : e * 4 + 4, e * 8 : e * 8 + 8] = back[:, 8:].T
    span = np.concatenate([a_back, b_back], axis=0)
    summed = span.copy()
    for e in range(SPAN_ELEMENTS):
        last, first = e * 8 + 7, (e * 8 + 8) % SPAN
        mean = 0.5 * (span[:, last] + span[:, first])
        summed[:, last] = mean
        summed[:, first] = mean
    a_back, b_back = summed[:SPAN], summed[SPAN:]
    zero_a, zero_b = np.zeros_like(a_back), np.zeros_like(b_back)
    pair_back = np.concatenate(
        [
            np.concatenate([a_back, zero_a], axis=1),
            np.concatenate([zero_a, a_back], axis=1),
            np.concatenate([b_back, zero_b], axis=1),
            np.concatenate([zero_b, b_back], axis=1),
        ],
        axis=0,
    )
    wide = {
        "span_a": span_a,
        "span_b": span_b,
        "plane": plane,
        "values": values,
        "plane_back": plane_back[:, :256],
        "plane_back_rest": plane_back[:, 256:],
        "pair_back": np.concatenate(halves(pair_back), axis=0),
    }
    rows, places = [], {}
    start = 0
    for name, matrix in wide.items():
        places[name] = (start, matrix.shape[0], matrix.shape[1])
        rows.append(np.pad(matrix, ((0, 0), (0, 256 - matrix.shape[1]))))
        start += matrix.shape[0]
    return np.concatenate(rows, axis=0), places


def read(mats_ref, name):
    start, count, width = matrices()[1][name]
    return mats_ref[start : start + count, :width]


def read_rows(mats_ref, name, *pieces):
    start, count, width = matrices()[1][name]
    half = count // 2
    out = []
    for offset in (0, 0, half):
        for first, rows in pieces:
            at = start + offset + first
            out.append(mats_ref[at : at + rows, :width])
    return jnp.concatenate(out, axis=0)


def read_span_a(mats_ref):
    return read_rows(mats_ref, "span_a", (0, SPAN))


def read_span_b(mats_ref):
    start = matrices()[1]["span_b"][0]
    order = (0, 0, 1, 2, 2, 3)
    return jnp.concatenate(
        [mats_ref[start + i * SPAN : start + i * SPAN + SPAN] for i in order], axis=0
    )


def read_back(mats_ref, size):
    if size == 2:
        return read_rows(mats_ref, "pair_back", (0, 3 * SPAN))
    return read_rows(mats_ref, "pair_back", (0, SPAN), (2 * SPAN, SPAN))[:, :SPAN]


def split(x):
    high = x.astype(bf16)
    return high, (x - high.astype(f32)).astype(bf16)


def dot(a, b):
    return jnp.dot(a, b, preferred_element_type=f32)


def triple(x, axis):
    high, low = split(x)
    return jnp.concatenate([high, low, high], axis=axis)


def spots_of(count):
    spots = []
    for first in range(0, count, 2):
        group = tuple(range(first, min(first + 2, count)))
        spots += [(l,) for l in group] + [group + (None,) * (3 - len(group))]
    return spots


def chunks_of(count):
    spots = spots_of(count)
    return [spots[first : first + 2] for first in range(0, len(spots), 2)]


def span_forward(fields, mats):
    span_a, span_b = read_span_a(mats), read_span_b(mats)
    lefts = [triple(field, 1) for field in fields]
    spots = []
    for spot in spots_of(len(fields)):
        if len(spot) == 1:
            out = dot(lefts[spot[0]], span_a)
        elif spot[1] is None:
            out = dot(lefts[spot[0]], span_b[: 3 * SPAN])
        else:
            out = dot(jnp.concatenate([lefts[spot[0]], lefts[spot[1]]], axis=1), span_b)
        spots.append((out[:, :SPAN], out[:, SPAN:]))
    return spots


def plane_forward(spots, mats):
    plane, values = read(mats, "plane"), read(mats, "values")
    interp, deriv = (jnp.concatenate([s[i] for s in spots], axis=1) for i in range(2))
    interp, deriv = split(interp), split(deriv)
    outs = []
    for c in range(3):
        rows = slice(c * 64, c * 64 + 64)
        high, low = interp[0][rows], interp[1][rows]
        first = dot(plane, jnp.concatenate([high, low, high], axis=0))
        high, low = deriv[0][rows], deriv[1][rows]
        outs.append((first, dot(values, jnp.concatenate([high, low, high], axis=0))))
    return outs


def chunk_inverse(chunk, inverses):
    lane = lax.broadcasted_iota(jnp.int32, (1, SPAN), 1)
    out = []
    for spot in chunk:
        if len(spot) == 1 or spot[1] is None:
            out.append(inverses[spot[0]])
        else:
            out.append(jnp.where(lane < 64, inverses[spot[0]], inverses[spot[1]]))
    return jnp.concatenate(out, axis=1)


def convect_back(fine, inverse, mats):
    back = jnp.concatenate([read(mats, "plane_back"), read(mats, "plane_back_rest")], axis=1)
    parts = [([], []) for _ in range(3)]
    for first in range(0, 144, 48):
        rows = slice(first, first + 48)
        speeds = [fine(c, 0, rows) for c in range(3)]
        speeds[2] = speeds[2] * inverse
        for c in range(3):
            convect = (
                speeds[0] * fine(c, 1, rows)
                + speeds[1] * fine(c, 3, rows)
                + speeds[2] * fine(c, 2, rows)
            )
            for part, half in zip(parts[c], split(convect)):
                part.append(half)
    outs = []
    for high, low in parts:
        outs.append(dot(back, jnp.concatenate(high + low + high, axis=0)))
    return jnp.concatenate(outs, axis=0)


def span_back(count, backs, results, mats):
    for place, spot in enumerate(spots_of(count)):
        if len(spot) == 1 or place >= len(backs) or spot[0] < len(results):
            continue
        size = 1 if spot[1] is None else 2
        joined = jnp.concatenate(backs[place - size : place + 1], axis=1)
        out = dot(triple(joined, 1), read_back(mats, size))
        results += [out[:, i * SPAN : (i + 1) * SPAN] for i in range(size)]


def weak_layers(fields, inverses, mats):
    return weak_spots(span_forward(fields, mats), inverses, mats)


def weak_spots(spots, inverses, mats):
    count = len(inverses)
    chunks = chunks_of(count)
    planes = []
    backs, results = [], []

    def finish(i):
        def fine(c, kind, rows):
            first, along_y = planes[i][c]
            if kind == 3:
                return along_y[rows]
            return first[kind * 144 + rows.start : kind * 144 + rows.stop]

        out = convect_back(fine, chunk_inverse(chunks[i], inverses), mats)
        backs.extend(out[:, j * SPAN : (j + 1) * SPAN] for j in range(len(chunks[i])))
        span_back(count, backs, results, mats)

    for i in range(len(chunks)):
        planes.append(plane_forward(spots[2 * i : 2 * i + 2], mats))
        if i > 0:
            finish(i - 1)
    finish(len(chunks) - 1)
    return results


def face_spots(faces, mats):
    out_a = dot(triple(jnp.concatenate(faces, axis=0), 1), read_span_a(mats))
    even, odd = faces[0::2], faces[1::2]
    odd = odd + [jnp.zeros_like(faces[0])] * (len(even) - len(odd))
    even, odd = (triple(jnp.concatenate(x, axis=0), 1) for x in (even, odd))
    out_b = dot(jnp.concatenate([even, odd], axis=1), read_span_b(mats))
    spots = []
    for spot in spots_of(len(faces)):
        if len(spot) == 1:
            out = out_a[spot[0] * 48 : spot[0] * 48 + 48]
        else:
            out = out_b[spot[0] * 24 : spot[0] * 24 + 48]
        spots.append((out[:, :SPAN], out[:, SPAN:]))
    return spots


def with_faces(inner, faces):
    inner = inner.reshape(3, 6, 8, SPAN)
    faces = faces.reshape(3, 2, 8, SPAN)
    return jnp.concatenate([faces[:, :1], inner, faces[:, 1:]], axis=1).reshape(ROWS, SPAN)


def join_heights(own, above, below, height, height_above, height_below, has_above, has_below):
    level = lax.broadcasted_iota(jnp.int32, (8, SPAN), 0)
    keep = jnp.ones((8, SPAN), f32)
    out = own.reshape(24, 8, SPAN)
    if above is not None:
        share = jnp.where(has_above, height_above / (height + height_above), 0.0)
        take = jnp.where(level == 7, share, 0.0)
        keep = keep - take
        taken_above = pltpu.roll(above.reshape(24, 8, SPAN), 7, 1) * take[None]
    if below is not None:
        share = jnp.where(has_below, height_below / (height + height_below), 0.0)
        take = jnp.where(level == 0, share, 0.0)
        keep = keep - take
        taken_below = pltpu.roll(below.reshape(24, 8, SPAN), 1, 1) * take[None]
    out = out * keep[None]
    if above is not None:
        out = out + taken_above
    if below is not None:
        out = out + taken_below
    return out.reshape(ROWS, SPAN)


def sides():
    place = lax.axis_index("horiz")
    left_share = jnp.where(place > 0, 0.5, 0.0).astype(f32)
    right_share = jnp.where(place < lax.axis_size("horiz") - 1, 0.5, 0.0).astype(f32)
    return lax.rem(place, 2) == 1, left_share, right_share


def join_ends(own, cross, core):
    odd, left_share, right_share = sides()
    left = jnp.where(odd, core, cross)
    right = jnp.where(odd, cross, core)
    own = own.reshape(3, 8, 8, SPAN)
    first = own[:, 0] * (1.0 - left_share) + left * left_share
    last = own[:, 7] * (1.0 - right_share) + right * right_share
    return first, last


def join_stream(own, cross, core):
    first, last = join_ends(own, cross, core)
    own = own.reshape(3, 8, 8, SPAN)
    out = jnp.concatenate([first[:, None], own[:, 1:7], last[:, None]], axis=1)
    return out.reshape(ROWS, SPAN)


def put_faces(own, cross_ref, core_ref, at):
    odd = lax.rem(lax.axis_index("horiz"), 2) == 1
    own = own.reshape(3, 8, 8, SPAN)
    first, last = own[:, 0], own[:, 7]
    cross_ref[at] = jnp.where(odd, last, first)
    core_ref[at] = jnp.where(odd, first, last)


def put_layers(results, heights, partial_ref, cross_ref, core_ref):
    count = len(results)
    for l in range(count):
        above = results[l + 1] if l + 1 < count else None
        below = results[l - 1] if l > 0 else None
        joined = join_heights(
            results[l],
            above,
            below,
            heights[l],
            heights[l + 1] if l + 1 < count else None,
            heights[l - 1] if l > 0 else None,
            True,
            True,
        )
        partial_ref[l] = joined
        put_faces(joined, cross_ref, core_ref, l)


def pack_kernel(velocity_ref, height_ref, packed_ref):
    packed_ref[:ROWS] = velocity_ref[...]
    packed_ref[ROWS:] = jnp.broadcast_to(height_ref[...], (8, SPAN))


def one_layer_kernel_with_step(mats, packed_ref, step_ref, out_ref, step_tile_ref):
    inverse = 1.0 / packed_ref[ROWS : ROWS + 1]
    out_ref[...] = weak_layers([packed_ref[:ROWS]], [inverse], mats)[0]
    step_tile_ref[...] = jnp.broadcast_to(step_ref[...], (8, SPAN))


def other_layers_kernel(order, *refs):
    count = len(order)
    ready = min(count, 2)
    mats, packed, refs = refs[0], refs[1 : count + 1], refs[count + 1 :]
    given, refs = refs[:ready], refs[ready:]
    field_ref, heights_ref, partial_ref, cross_ref, core_ref, raw_ref = refs
    place = lax.axis_index("vert")
    slots = [jnp.bitwise_xor(place, j) for j in order]
    for i in range(count):
        field_ref[slots[i]] = packed[i][:ROWS]
        heights_ref[slots[i]] = packed[i][ROWS:]
    for i in range(ready):
        raw_ref[slots[i]] = given[i][...]
    if count > ready:
        results = weak_layers(
            [packed[i][:ROWS] for i in range(ready, count)],
            [1.0 / packed[i][ROWS : ROWS + 1] for i in range(ready, count)],
            mats,
        )
        for i in range(ready, count):
            raw_ref[slots[i]] = results[i - ready]
    heights = [heights_ref[l] for l in range(count)]
    put_layers([raw_ref[l] for l in range(count)], heights, partial_ref, cross_ref, core_ref)


def one_layer_kernel(mats, packed_ref, out_ref):
    inverse = 1.0 / packed_ref[ROWS : ROWS + 1]
    out_ref[...] = weak_layers([packed_ref[:ROWS]], [inverse], mats)[0]


def first_kernel(count, *refs):
    mats, refs = refs[0], refs[1:]
    packed_ref, step_ref, field_ref, heights_ref, partial_ref, cross_ref, core_ref = refs[:7]
    refs[7][...] = jnp.broadcast_to(step_ref[...], (8, SPAN))
    heights = [packed_ref[l, ROWS:] for l in range(count)]
    for l in range(count):
        field_ref[l] = packed_ref[l, :ROWS]
        heights_ref[l] = heights[l]
    results = weak_layers(
        [packed_ref[l, :ROWS] for l in range(count)], [1.0 / h[:1] for h in heights], mats
    )
    put_layers(results, heights, partial_ref, cross_ref, core_ref)


def stage_layers(count, last):
    if not last:
        return list(range(count))
    place = lax.axis_index("vert")
    return [place, jnp.minimum(place + 1, count - 1), jnp.maximum(place - 1, 0)]


def inner_kernel(count, share, last, mats, step_ref, field_ref, partial_ref, spots_ref):
    step = step_ref[:1] * share
    fields = []
    for l in stage_layers(count, last):
        field = (field_ref[l] + step * partial_ref[l]).reshape(3, 8, 8, SPAN)
        fields.append(field[:, 1:7].reshape(144, SPAN))
    for i, pair in enumerate(span_forward(fields, mats)):
        for part in range(2):
            spots_ref[i, part] = pair[part]


def stage_kernel(count, share, first, last, *refs):
    mats, step_ref, field_ref, heights_ref, partial_ref, cross_ref, core_ref, spots_ref = refs[:8]
    refs = refs[8:]
    total = None if first else refs[0][...]
    total_ref, next_partial_ref, next_cross_ref, next_core_ref = refs[-4:]
    place = lax.axis_index("vert")
    step = step_ref[:1] * share
    layers = stage_layers(count, last)
    heights = [heights_ref[l] for l in layers]
    faces = []
    for l in layers:
        ends = join_ends(partial_ref[l], cross_ref[l], core_ref[l])
        ends = jnp.concatenate([end[:, None] for end in ends], axis=1)
        field = field_ref[l].reshape(3, 8, 8, SPAN)
        field = jnp.concatenate([field[:, :1], field[:, 7:]], axis=1)
        faces.append((field + step * ends).reshape(48, SPAN))
    spots = []
    for i, pair in enumerate(face_spots(faces, mats)):
        spots.append([with_faces(spots_ref[i, part], pair[part]) for part in range(2)])
    results = weak_spots(spots, [1.0 / h[:1] for h in heights], mats)
    own = join_stream(partial_ref[place], cross_ref[place], core_ref[place])
    total_ref[...] = own if first else total + 2.0 * own
    if last:
        joined = join_heights(*results, *heights, place < count - 1, place > 0)
        next_partial_ref[...] = joined
        put_faces(joined, next_cross_ref, next_core_ref, slice(None))
    else:
        put_layers(results, heights, next_partial_ref, next_cross_ref, next_core_ref)


def rate_kernel(partial_ref, cross_ref, core_ref, total_ref, rate_ref):
    slope = join_stream(partial_ref[...], cross_ref[...], core_ref[...])
    rate_ref[...] = (total_ref[...] + slope) / 6.0


VMEM = pl.BlockSpec(memory_space=pltpu.VMEM)


def call(kernel, outs, args, scratch=(), flops=0):
    shapes = [jax.ShapeDtypeStruct(shape, f32) for shape in outs]
    one = len(shapes) == 1
    return pl.pallas_call(
        kernel,
        out_shape=shapes[0] if one else shapes,
        in_specs=[VMEM] * len(args),
        out_specs=VMEM if one else [VMEM] * len(shapes),
        scratch_shapes=list(scratch),
        compiler_params=pltpu.CompilerParams(vmem_limit_bytes=32 * 1024 * 1024),
        cost_estimate=pl.CostEstimate(flops=flops, bytes_accessed=1 << 20, transcendentals=0),
    )(*args)


def swap_stream(cross, core):
    count = lax.axis_size("horiz")
    cores = [(i, i ^ 1) for i in range(count)]
    crosses = [(i, (i + 1) % count if i % 2 else (i - 1) % count) for i in range(count)]
    return lax.ppermute(cross, "horiz", crosses), lax.ppermute(core, "horiz", cores)


def on_device(velocity, heights, time_step):
    layers = lax.axis_size("vert")
    mats = jnp.asarray(matrices()[0])
    unit = 2 * 256 * 256 * 3000
    field = (layers, ROWS, SPAN)
    face = (layers, 3, 8, SPAN)
    small = (3, 8, SPAN)
    first_outs = [field, (layers, 8, SPAN), field, face, face]
    step = time_step.reshape(1, 1)
    tile = (8, SPAN)
    packed = call(
        pack_kernel,
        [(ROWS + 8, SPAN)],
        [velocity.reshape(ROWS, SPAN), heights.reshape(1, 1)],
    )
    if layers in (1, 2, 4):
        slots = [packed]
        for j in range(1, layers):
            slots.append(lax.ppermute(packed, "vert", [(i, i ^ j) for i in range(layers)]))
        order = [0] + [layers - 1] * (layers > 1) + list(range(1, layers - 1))
        own, step = call(
            one_layer_kernel_with_step, [(ROWS, SPAN), tile], [mats, packed, step], flops=unit
        )
        given = [own]
        if layers > 1:
            given.append(
                call(one_layer_kernel, [(ROWS, SPAN)], [mats, slots[layers - 1]], flops=unit)
            )
        fields, all_heights, partial, cross, core = call(
            functools.partial(other_layers_kernel, order),
            first_outs,
            [mats] + [slots[j] for j in order] + given,
            scratch=[pltpu.VMEM(field, f32)],
            flops=max(layers - 2, 0) * unit,
        )
    else:
        gathered = lax.all_gather(packed, "vert")
        fields, all_heights, partial, cross, core, step = call(
            functools.partial(first_kernel, layers), first_outs + [tile], [mats, gathered, step]
        )
    cross, core = swap_stream(cross, core)
    total = None
    for stage, share in enumerate((0.5, 0.5, 1.0)):
        last = stage == 2
        used = 3 if last else layers
        spots = call(
            functools.partial(inner_kernel, layers, share, last),
            [(len(spots_of(used)), 2, 144, SPAN)],
            [mats, step, fields, partial],
            flops=used * unit // 4,
        )
        args = [mats, step, fields, all_heights, partial, cross, core, spots]
        total, partial, cross, core = call(
            functools.partial(stage_kernel, layers, share, stage == 0, last),
            [(ROWS, SPAN)] + ([(ROWS, SPAN), small, small] if last else [field, face, face]),
            args + ([] if stage == 0 else [total]),
            flops=used * unit,
        )
        cross, core = swap_stream(cross, core)
    rate = call(rate_kernel, [(ROWS, SPAN)], [partial, cross, core, total])
    return rate.reshape(velocity.shape)


def solution(mesh):
    in_specs = (P(None, "horiz", "vert", None), P("vert"), P())
    out_specs = P(None, "horiz", "vert", None)
    return jax.shard_map(
        on_device, mesh=mesh, in_specs=in_specs, out_specs=out_specs, check_vma=False
    )
```

```python
import functools

import jax
import jax.numpy as jnp
import ml_dtypes
import numpy as np
from jax import lax
from jax.experimental import pallas as pl
from jax.experimental.pallas import tpu as pltpu
from jax.sharding import PartitionSpec as P

gll_half = [1.0, 0.8717401485096066, 0.5917001814331423, 0.2092992179024789]
gll_half_weights = [
    0.03571428571428571,
    0.21070422714350603,
    0.34112269248350435,
    0.4124587946587038,
]
gauss_half = [
    0.9815606342467192,
    0.9041172563704749,
    0.7699026741943047,
    0.5873179542866175,
    0.3678314989981802,
    0.1252334085114689,
]
gauss_half_weights = [
    0.0471753363865118,
    0.1069393259953184,
    0.1600783285433462,
    0.2031674267230659,
    0.2334925365383548,
    0.2491470458134028,
]

f32 = jnp.float32
bf16 = jnp.bfloat16
ROWS = 192
SPAN = 128
SPAN_ELEMENTS = 16


def mirrored(values, sign):
    return np.concatenate([sign * np.array(values), np.array(values[::-1])])


def lagrange(targets, sources):
    matrix = np.ones((targets.size, sources.size))
    for j in range(sources.size):
        for k in range(sources.size):
            if k != j:
                matrix[:, j] = matrix[:, j] * (targets - sources[k]) / (sources[j] - sources[k])
    return matrix


def node_tables():
    gll_points = mirrored(gll_half, -1.0)
    gll_weights = mirrored(gll_half_weights, 1.0)
    fine_points = mirrored(gauss_half, -1.0)
    fine_weights = mirrored(gauss_half_weights, 1.0)
    to_fine = lagrange(fine_points, gll_points)
    products = np.ones(8)
    for i in range(8):
        for k in range(8):
            if k != i:
                products[i] = products[i] * (gll_points[i] - gll_points[k])
    deriv_mat = np.zeros((8, 8))
    for i in range(8):
        for j in range(8):
            if i != j:
                deriv_mat[i, j] = products[i] / (products[j] * (gll_points[i] - gll_points[j]))
                deriv_mat[i, i] = deriv_mat[i, i] + 1.0 / (gll_points[i] - gll_points[j])
    return to_fine, to_fine @ deriv_mat, gll_weights, fine_weights


def halves(matrix):
    high = matrix.astype(ml_dtypes.bfloat16)
    low = (matrix - high.astype(np.float64)).astype(ml_dtypes.bfloat16)
    return high, low


def stack_columns(matrix):
    high, low = halves(matrix)
    return np.concatenate([high, high, low], axis=1)


def span_blocks(block, first, count):
    out = np.zeros((SPAN, SPAN_ELEMENTS * count))
    for e in range(SPAN_ELEMENTS):
        out[e * 8 : e * 8 + 8, e * count : (e + 1) * count] = block[first : first + count].T
    return out


@functools.cache
def matrices():
    interp, deriv, gll_w, fine_w = node_tables()
    a_both = np.concatenate([span_blocks(interp, 0, 8), span_blocks(2.0 * deriv, 0, 8)], axis=1)
    span_a = np.concatenate(halves(a_both), axis=0)
    interp_b = span_blocks(interp, 8, 4)
    deriv_b = span_blocks(2.0 * deriv, 8, 4)
    none = np.zeros_like(interp_b)
    first_b = halves(np.concatenate([interp_b, none, deriv_b, none], axis=1))
    second_b = halves(np.concatenate([none, interp_b, none, deriv_b], axis=1))
    span_b = np.concatenate(first_b + second_b, axis=0)
    values = np.kron(interp, interp)
    plane = np.concatenate([values, np.kron(2.0 * deriv, interp), np.kron(interp, 2.0 * deriv)])
    plane = stack_columns(plane)
    values = stack_columns(values)
    back = interp.T * fine_w[None, :] / gll_w[:, None]
    plane_back = np.concatenate(halves(-np.kron(back, back)), axis=0)
    a_back = np.zeros((SPAN, SPAN))
    b_back = np.zeros((SPAN // 2, SPAN))
    for e in range(SPAN_ELEMENTS):
        a_back[e * 8 : e * 8 + 8, e * 8 : e * 8 + 8] = back[:, :8].T
        b_back[e * 4 : e * 4 + 4, e * 8 : e * 8 + 8] = back[:, 8:].T
    span = np.concatenate([a_back, b_back], axis=0)
    summed = span.copy()
    for e in range(SPAN_ELEMENTS):
        last, first = e * 8 + 7, (e * 8 + 8) % SPAN
        mean = 0.5 * (span[:, last] + span[:, first])
        summed[:, last] = mean
        summed[:, first] = mean
    a_back, b_back = summed[:SPAN], summed[SPAN:]
    zero_a, zero_b = np.zeros_like(a_back), np.zeros_like(b_back)
    pair_back = np.concatenate(
        [
            np.concatenate([a_back, zero_a], axis=1),
            np.concatenate([zero_a, a_back], axis=1),
            np.concatenate([b_back, zero_b], axis=1),
            np.concatenate([zero_b, b_back], axis=1),
        ],
        axis=0,
    )
    wide = {
        "span_a": span_a,
        "span_b": span_b,
        "plane": plane,
        "values": values,
        "plane_back": plane_back,
        "pair_back": np.concatenate(halves(pair_back), axis=0),
    }
    rows, places = [], {}
    start = 0
    for name, matrix in wide.items():
        places[name] = (start, matrix.shape[0], matrix.shape[1])
        rows.append(np.pad(matrix, ((0, 0), (0, 256 - matrix.shape[1]))))
        start += matrix.shape[0]
    return np.concatenate(rows, axis=0), places


def read(mats_ref, name):
    start, count, width = matrices()[1][name]
    return mats_ref[start : start + count, :width]


def read_rows(mats_ref, name, *pieces):
    start, count, width = matrices()[1][name]
    half = count // 2
    out = []
    for offset in (0, 0, half):
        for first, rows in pieces:
            at = start + offset + first
            out.append(mats_ref[at : at + rows, :width])
    return jnp.concatenate(out, axis=0)


def read_span_a(mats_ref):
    return read_rows(mats_ref, "span_a", (0, SPAN))


def read_span_b(mats_ref):
    start = matrices()[1]["span_b"][0]
    order = (0, 0, 1, 2, 2, 3)
    return jnp.concatenate(
        [mats_ref[start + i * SPAN : start + i * SPAN + SPAN] for i in order], axis=0
    )


def read_back(mats_ref, size):
    if size == 2:
        return read_rows(mats_ref, "pair_back", (0, 3 * SPAN))
    return read_rows(mats_ref, "pair_back", (0, SPAN), (2 * SPAN, SPAN))[:, :SPAN]


def split(x):
    high = x.astype(bf16)
    return high, (x - high.astype(f32)).astype(bf16)


def dot(a, b):
    return jnp.dot(a, b, preferred_element_type=f32)


def triple(x, axis):
    high, low = split(x)
    return jnp.concatenate([high, low, high], axis=axis)


def spots_of(count):
    spots = []
    for first in range(0, count, 2):
        group = tuple(range(first, min(first + 2, count)))
        spots += [(l,) for l in group] + [group + (None,) * (3 - len(group))]
    return spots


def chunks_of(count):
    spots = spots_of(count)
    return [spots[first : first + 2] for first in range(0, len(spots), 2)]


def span_forward(fields, mats):
    span_a, span_b = read_span_a(mats), read_span_b(mats)
    lefts = [triple(field, 1) for field in fields]
    spots = []
    for spot in spots_of(len(fields)):
        if len(spot) == 1:
            out = dot(lefts[spot[0]], span_a)
        elif spot[1] is None:
            out = dot(lefts[spot[0]], span_b[: 3 * SPAN])
        else:
            out = dot(jnp.concatenate([lefts[spot[0]], lefts[spot[1]]], axis=1), span_b)
        spots.append((out[:, :SPAN], out[:, SPAN:]))
    return spots


def plane_forward(spots, mats):
    plane, values = read(mats, "plane"), read(mats, "values")
    interp, deriv = (jnp.concatenate([s[i] for s in spots], axis=1) for i in range(2))
    interp, deriv = split(interp), split(deriv)
    outs = []
    for c in range(3):
        rows = slice(c * 64, c * 64 + 64)
        high, low = interp[0][rows], interp[1][rows]
        first = dot(plane, jnp.concatenate([high, low, high], axis=0))
        high, low = deriv[0][rows], deriv[1][rows]
        outs.append((first, dot(values, jnp.concatenate([high, low, high], axis=0))))
    return outs


def chunk_inverse(chunk, inverses):
    lane = lax.broadcasted_iota(jnp.int32, (1, SPAN), 1)
    out = []
    for spot in chunk:
        if len(spot) == 1 or spot[1] is None:
            out.append(inverses[spot[0]])
        else:
            out.append(jnp.where(lane < 64, inverses[spot[0]], inverses[spot[1]]))
    return jnp.concatenate(out, axis=1)


def convect_back(fine, inverse, mats):
    back = read(mats, "plane_back")
    parts = [([], []) for _ in range(3)]
    for first in range(0, 144, 48):
        rows = slice(first, first + 48)
        speeds = [fine(c, 0, rows) for c in range(3)]
        speeds[2] = speeds[2] * inverse
        for c in range(3):
            convect = (
                speeds[0] * fine(c, 1, rows)
                + speeds[1] * fine(c, 3, rows)
                + speeds[2] * fine(c, 2, rows)
            )
            for part, half in zip(parts[c], split(convect)):
                part.append(half)
    outs = []
    for high, low in parts:
        out = dot(back, jnp.concatenate(high, axis=0))
        outs.append(out[:64] + out[64:] + dot(back[:64], jnp.concatenate(low, axis=0)))
    return jnp.concatenate(outs, axis=0)


def span_back(count, backs, results, mats):
    for place, spot in enumerate(spots_of(count)):
        if len(spot) == 1 or place >= len(backs) or spot[0] < len(results):
            continue
        size = 1 if spot[1] is None else 2
        joined = jnp.concatenate(backs[place - size : place + 1], axis=1)
        out = dot(triple(joined, 1), read_back(mats, size))
        results += [out[:, i * SPAN : (i + 1) * SPAN] for i in range(size)]


def weak_layers(fields, inverses, mats):
    return weak_spots(span_forward(fields, mats), inverses, mats)


def weak_spots(spots, inverses, mats):
    count = len(inverses)
    chunks = chunks_of(count)
    planes = []
    backs, results = [], []

    def finish(i):
        def fine(c, kind, rows):
            first, along_y = planes[i][c]
            if kind == 3:
                return along_y[rows]
            return first[kind * 144 + rows.start : kind * 144 + rows.stop]

        out = convect_back(fine, chunk_inverse(chunks[i], inverses), mats)
        backs.extend(out[:, j * SPAN : (j + 1) * SPAN] for j in range(len(chunks[i])))
        span_back(count, backs, results, mats)

    for i in range(len(chunks)):
        planes.append(plane_forward(spots[2 * i : 2 * i + 2], mats))
        if i > 0:
            finish(i - 1)
    finish(len(chunks) - 1)
    return results


def face_spots(faces, mats):
    out_a = dot(triple(jnp.concatenate(faces, axis=0), 1), read_span_a(mats))
    even, odd = faces[0::2], faces[1::2]
    odd = odd + [jnp.zeros_like(faces[0])] * (len(even) - len(odd))
    even, odd = (triple(jnp.concatenate(x, axis=0), 1) for x in (even, odd))
    out_b = dot(jnp.concatenate([even, odd], axis=1), read_span_b(mats))
    spots = []
    for spot in spots_of(len(faces)):
        if len(spot) == 1:
            out = out_a[spot[0] * 48 : spot[0] * 48 + 48]
        else:
            out = out_b[spot[0] * 24 : spot[0] * 24 + 48]
        spots.append((out[:, :SPAN], out[:, SPAN:]))
    return spots


def with_faces(inner, faces):
    inner = inner.reshape(3, 6, 8, SPAN)
    faces = faces.reshape(3, 2, 8, SPAN)
    return jnp.concatenate([faces[:, :1], inner, faces[:, 1:]], axis=1).reshape(ROWS, SPAN)


def height_rows(level, rows=ROWS):
    return pl.ds(level, rows // 8, stride=8)


def join_heights(layers, heights, joins):
    for lower, upper, wanted in joins:
        share = heights[upper] / (heights[lower] + heights[upper])
        share = share[:1]
        below = layers[lower][height_rows(7), :]
        above = layers[upper][height_rows(0), :]
        mean = below * (1.0 - share) + above * share
        if wanted is True:
            layers[lower][height_rows(7), :] = mean
            layers[upper][height_rows(0), :] = mean
        else:
            layers[lower][height_rows(7), :] = jnp.where(wanted, mean, below)
            layers[upper][height_rows(0), :] = jnp.where(wanted, mean, above)


def sides():
    place = lax.axis_index("horiz")
    left_share = jnp.where(place > 0, 0.5, 0.0).astype(f32)
    right_share = jnp.where(place < lax.axis_size("horiz") - 1, 0.5, 0.0).astype(f32)
    return lax.rem(place, 2) == 1, left_share, right_share


def join_ends(own, cross, core):
    odd, left_share, right_share = sides()
    left = jnp.where(odd, core, cross)
    right = jnp.where(odd, cross, core)
    own = own.reshape(3, 8, 8, SPAN)
    first = own[:, 0] * (1.0 - left_share) + left * left_share
    last = own[:, 7] * (1.0 - right_share) + right * right_share
    return first, last


def join_stream(own, cross, core):
    first, last = join_ends(own, cross, core)
    own = own.reshape(3, 8, 8, SPAN)
    out = jnp.concatenate([first[:, None], own[:, 1:7], last[:, None]], axis=1)
    return out.reshape(ROWS, SPAN)


def put_faces(own, cross_ref, core_ref, at):
    odd = lax.rem(lax.axis_index("horiz"), 2) == 1
    own = own.reshape(3, 8, 8, SPAN)
    first, last = own[:, 0], own[:, 7]
    cross_ref[at] = jnp.where(odd, last, first)
    core_ref[at] = jnp.where(odd, first, last)


def put_layers(results, heights, partial_ref, cross_ref, core_ref):
    count = len(results)
    for l in range(count):
        partial_ref[l] = results[l]
    layers = [partial_ref.at[l] for l in range(count)]
    join_heights(layers, heights, [(l, l + 1, True) for l in range(count - 1)])
    for l in range(count):
        put_faces(partial_ref[l], cross_ref, core_ref, l)


def step_kernel(mats, step_ref, tile_ref):
    tile_ref[...] = jnp.broadcast_to(step_ref[...], (8, SPAN))


def raw_kernel(count, *refs):
    mats, packed, raws = refs[0], refs[2 : count + 2], refs[count + 2 :]
    results = weak_layers(
        [p[:ROWS] for p in packed], [1.0 / p[ROWS : ROWS + 1] for p in packed], mats
    )
    for raw_ref, result in zip(raws, results):
        raw_ref[...] = result


def slots_kernel(order, ready, *refs):
    count = len(order)
    mats, packed, given = refs[0], refs[2 : count + 2], refs[count + 2 : count + 2 + ready]
    field_ref, heights_ref, partial_ref, cross_ref, core_ref, raw_ref = refs[count + 2 + ready :]
    place = lax.axis_index("vert")
    slots = [jnp.bitwise_xor(place, j) for j in order]
    for i in range(count):
        field_ref[slots[i]] = packed[i][:ROWS]
        heights_ref[slots[i]] = packed[i][ROWS:]
    for i in range(ready):
        raw_ref[slots[i]] = given[i][...]
    results = weak_layers(
        [packed[i][:ROWS] for i in range(ready, count)],
        [1.0 / packed[i][ROWS : ROWS + 1] for i in range(ready, count)],
        mats,
    )
    for i in range(ready, count):
        raw_ref[slots[i]] = results[i - ready]
    heights = [heights_ref[l] for l in range(count)]
    put_layers([raw_ref[l] for l in range(count)], heights, partial_ref, cross_ref, core_ref)


def first_kernel(count, *refs):
    mats, packed_ref, refs = refs[0], refs[2], refs[3:]
    field_ref, heights_ref, partial_ref, cross_ref, core_ref = refs
    heights = [packed_ref[l, ROWS:] for l in range(count)]
    for l in range(count):
        field_ref[l] = packed_ref[l, :ROWS]
        heights_ref[l] = heights[l]
    results = weak_layers(
        [packed_ref[l, :ROWS] for l in range(count)], [1.0 / h[:1] for h in heights], mats
    )
    put_layers(results, heights, partial_ref, cross_ref, core_ref)


def stage_layers(count, last):
    if not last:
        return list(range(count))
    place = lax.axis_index("vert")
    return [place, jnp.minimum(place + 1, count - 1), jnp.maximum(place - 1, 0)]


def inner_kernel(count, share, last, mats, step_ref, field_ref, partial_ref, spots_ref):
    step = step_ref[:1] * share
    fields = []
    for l in stage_layers(count, last):
        field = (field_ref[l] + step * partial_ref[l]).reshape(3, 8, 8, SPAN)
        fields.append(field[:, 1:7].reshape(144, SPAN))
    for i, pair in enumerate(span_forward(fields, mats)):
        for part in range(2):
            spots_ref[i, part] = pair[part]


def stage_kernel(count, share, first, last, *refs):
    mats, step_ref, field_ref, heights_ref, partial_ref, cross_ref, core_ref, spots_ref = refs[:8]
    refs = refs[8:]
    total = None if first else refs[0][...]
    *outs, above_ref, below_ref = refs[-6:]
    total_ref, next_partial_ref, next_cross_ref, next_core_ref = outs
    place = lax.axis_index("vert")
    step = step_ref[:1] * share
    layers = stage_layers(count, last)
    heights = [heights_ref[l] for l in layers]
    faces = []
    for l in layers:
        ends = join_ends(partial_ref[l], cross_ref[l], core_ref[l])
        ends = jnp.concatenate([end[:, None] for end in ends], axis=1)
        field = field_ref[l].reshape(3, 8, 8, SPAN)
        field = jnp.concatenate([field[:, :1], field[:, 7:]], axis=1)
        faces.append((field + step * ends).reshape(48, SPAN))
    spots = []
    for i, pair in enumerate(face_spots(faces, mats)):
        spots.append([with_faces(spots_ref[i, part], pair[part]) for part in range(2)])
    results = weak_spots(spots, [1.0 / h[:1] for h in heights], mats)
    own = join_stream(partial_ref[place], cross_ref[place], core_ref[place])
    total_ref[...] = own if first else total + 2.0 * own
    if last:
        own, above, below = results
        next_partial_ref[...] = own
        above_ref[...] = above
        below_ref[...] = below
        joins = [(0, 1, place < count - 1), (2, 0, place > 0)]
        join_heights([next_partial_ref, above_ref, below_ref], heights, joins)
        put_faces(next_partial_ref[...], next_cross_ref, next_core_ref, slice(None))
    else:
        put_layers(results, heights, next_partial_ref, next_cross_ref, next_core_ref)


def rate_kernel(partial_ref, cross_ref, core_ref, total_ref, rate_ref):
    slope = join_stream(partial_ref[...], cross_ref[...], core_ref[...])
    rate_ref[...] = (total_ref[...] + slope) / 6.0


VMEM = pl.BlockSpec(memory_space=pltpu.VMEM)


def call(kernel, outs, args, scratch=(), flops=0):
    shapes = [jax.ShapeDtypeStruct(shape, f32) for shape in outs]
    one = len(shapes) == 1
    return pl.pallas_call(
        kernel,
        out_shape=shapes[0] if one else shapes,
        in_specs=[VMEM] * len(args),
        out_specs=VMEM if one else [VMEM] * len(shapes),
        scratch_shapes=list(scratch),
        compiler_params=pltpu.CompilerParams(vmem_limit_bytes=32 * 1024 * 1024),
        cost_estimate=pl.CostEstimate(flops=flops, bytes_accessed=1 << 20, transcendentals=0),
    )(*args)


def swap_stream(cross, core):
    count = lax.axis_size("horiz")
    cores = [(i, i ^ 1) for i in range(count)]
    crosses = [(i, (i + 1) % count if i % 2 else (i - 1) % count) for i in range(count)]
    return lax.ppermute(cross, "horiz", crosses), lax.ppermute(core, "horiz", cores)


def on_device(velocity, heights, time_step):
    layers = lax.axis_size("vert")
    mats = jnp.asarray(matrices()[0])
    unit = 2 * 256 * 256 * 3000
    field = (layers, ROWS, SPAN)
    face = (layers, 3, 8, SPAN)
    small = (3, 8, SPAN)
    first_outs = [field, (layers, 8, SPAN), field, face, face]
    step = time_step.reshape(1, 1)
    tile = (8, SPAN)
    step = call(step_kernel, [tile], [mats, step], flops=2 * unit)
    own_field = velocity.reshape(ROWS, SPAN)
    packed = jnp.concatenate([own_field, jnp.broadcast_to(heights[:, None], (8, SPAN))], axis=0)
    if layers in (1, 2, 4):
        groups = {1: [[0]], 2: [[0], [1]], 4: [[0, 2], [3, 1]]}[layers]
        slots = {0: packed}
        for j in range(layers - 1, 0, -1):
            slots[j] = lax.ppermute(packed, "vert", [(i, i ^ j) for i in range(layers)])
        given = []
        for group in groups[:-1]:
            outs = [(ROWS, SPAN)] * len(group)
            args = [mats, step] + [slots[j] for j in group]
            raw = call(
                functools.partial(raw_kernel, len(group)), outs, args, flops=len(group) * unit
            )
            given += [raw] if len(group) == 1 else raw
        order = sum(groups, [])
        args, scratch = [mats, step] + [slots[j] for j in order] + given, [pltpu.VMEM(field, f32)]
        first = functools.partial(slots_kernel, order, len(given))
    else:
        args, scratch = [mats, step, lax.all_gather(packed, "vert")], []
        first = functools.partial(first_kernel, layers)
    fields, all_heights, partial, cross, core = call(
        first, first_outs, args, scratch=scratch, flops=layers * unit
    )
    cross, core = swap_stream(cross, core)
    total = None
    for stage, share in enumerate((0.5, 0.5, 1.0)):
        last = stage == 2
        used = 3 if last else layers
        spots = call(
            functools.partial(inner_kernel, layers, share, last),
            [(len(spots_of(used)), 2, 144, SPAN)],
            [mats, step, fields, partial],
            flops=used * unit // 4,
        )
        args = [mats, step, fields, all_heights, partial, cross, core, spots]
        total, partial, cross, core = call(
            functools.partial(stage_kernel, layers, share, stage == 0, last),
            [(ROWS, SPAN)] + ([(ROWS, SPAN), small, small] if last else [field, face, face]),
            args + ([] if stage == 0 else [total]),
            scratch=[pltpu.VMEM((ROWS, SPAN), f32)] * 2,
            flops=used * unit,
        )
        cross, core = swap_stream(cross, core)
    rate = call(rate_kernel, [(ROWS, SPAN)], [partial, cross, core, total])
    return rate.reshape(velocity.shape)


def solution(mesh):
    in_specs = (P(None, "horiz", "vert", None), P("vert"), P())
    out_specs = P(None, "horiz", "vert", None)
    return jax.shard_map(
        on_device, mesh=mesh, in_specs=in_specs, out_specs=out_specs, check_vma=False
    )
```

```python
import functools

import jax
import jax.numpy as jnp
import ml_dtypes
import numpy as np
from jax import lax
from jax.experimental import pallas as pl
from jax.experimental.pallas import tpu as pltpu
from jax.sharding import PartitionSpec as P

gll_half = [1.0, 0.8717401485096066, 0.5917001814331423, 0.2092992179024789]
gll_half_weights = [
    0.03571428571428571,
    0.21070422714350603,
    0.34112269248350435,
    0.4124587946587038,
]
gauss_half = [
    0.9815606342467192,
    0.9041172563704749,
    0.7699026741943047,
    0.5873179542866175,
    0.3678314989981802,
    0.1252334085114689,
]
gauss_half_weights = [
    0.0471753363865118,
    0.1069393259953184,
    0.1600783285433462,
    0.2031674267230659,
    0.2334925365383548,
    0.2491470458134028,
]

f32 = jnp.float32
bf16 = jnp.bfloat16
ROWS = 192
SPAN = 128
SPAN_ELEMENTS = 16


def mirrored(values, sign):
    return np.concatenate([sign * np.array(values), np.array(values[::-1])])


def lagrange(targets, sources):
    matrix = np.ones((targets.size, sources.size))
    for j in range(sources.size):
        for k in range(sources.size):
            if k != j:
                matrix[:, j] = matrix[:, j] * (targets - sources[k]) / (sources[j] - sources[k])
    return matrix


def node_tables():
    gll_points = mirrored(gll_half, -1.0)
    gll_weights = mirrored(gll_half_weights, 1.0)
    fine_points = mirrored(gauss_half, -1.0)
    fine_weights = mirrored(gauss_half_weights, 1.0)
    to_fine = lagrange(fine_points, gll_points)
    products = np.ones(8)
    for i in range(8):
        for k in range(8):
            if k != i:
                products[i] = products[i] * (gll_points[i] - gll_points[k])
    deriv_mat = np.zeros((8, 8))
    for i in range(8):
        for j in range(8):
            if i != j:
                deriv_mat[i, j] = products[i] / (products[j] * (gll_points[i] - gll_points[j]))
                deriv_mat[i, i] = deriv_mat[i, i] + 1.0 / (gll_points[i] - gll_points[j])
    return to_fine, to_fine @ deriv_mat, gll_weights, fine_weights


def halves(matrix):
    high = matrix.astype(ml_dtypes.bfloat16)
    low = (matrix - high.astype(np.float64)).astype(ml_dtypes.bfloat16)
    return high, low


def stack_columns(matrix):
    high, low = halves(matrix)
    return np.concatenate([high, high, low], axis=1)


def span_blocks(block, first, count):
    out = np.zeros((SPAN, SPAN_ELEMENTS * count))
    for e in range(SPAN_ELEMENTS):
        out[e * 8 : e * 8 + 8, e * count : (e + 1) * count] = block[first : first + count].T
    return out


@functools.cache
def matrices():
    interp, deriv, gll_w, fine_w = node_tables()
    a_both = np.concatenate([span_blocks(interp, 0, 8), span_blocks(2.0 * deriv, 0, 8)], axis=1)
    span_a = np.concatenate(halves(a_both), axis=0)
    interp_b = span_blocks(interp, 8, 4)
    deriv_b = span_blocks(2.0 * deriv, 8, 4)
    none = np.zeros_like(interp_b)
    first_b = halves(np.concatenate([interp_b, none, deriv_b, none], axis=1))
    second_b = halves(np.concatenate([none, interp_b, none, deriv_b], axis=1))
    span_b = np.concatenate(first_b + second_b, axis=0)
    values = np.kron(interp, interp)
    plane = np.concatenate([values, np.kron(2.0 * deriv, interp), np.kron(interp, 2.0 * deriv)])
    plane = stack_columns(plane)
    values = stack_columns(values)
    back = interp.T * fine_w[None, :] / gll_w[:, None]
    plane_back = np.concatenate(halves(-np.kron(back, back)), axis=0)
    a_back = np.zeros((SPAN, SPAN))
    b_back = np.zeros((SPAN // 2, SPAN))
    for e in range(SPAN_ELEMENTS):
        a_back[e * 8 : e * 8 + 8, e * 8 : e * 8 + 8] = back[:, :8].T
        b_back[e * 4 : e * 4 + 4, e * 8 : e * 8 + 8] = back[:, 8:].T
    span = np.concatenate([a_back, b_back], axis=0)
    summed = span.copy()
    for e in range(SPAN_ELEMENTS):
        last, first = e * 8 + 7, (e * 8 + 8) % SPAN
        mean = 0.5 * (span[:, last] + span[:, first])
        summed[:, last] = mean
        summed[:, first] = mean
    a_back, b_back = summed[:SPAN], summed[SPAN:]
    zero_a, zero_b = np.zeros_like(a_back), np.zeros_like(b_back)
    pair_back = np.concatenate(
        [
            np.concatenate([a_back, zero_a], axis=1),
            np.concatenate([zero_a, a_back], axis=1),
            np.concatenate([b_back, zero_b], axis=1),
            np.concatenate([zero_b, b_back], axis=1),
        ],
        axis=0,
    )
    wide = {
        "span_a": span_a,
        "span_b": span_b,
        "plane": plane,
        "values": values,
        "plane_back": plane_back,
        "pair_back": np.concatenate(halves(pair_back), axis=0),
    }
    rows, places = [], {}
    start = 0
    for name, matrix in wide.items():
        places[name] = (start, matrix.shape[0], matrix.shape[1])
        rows.append(np.pad(matrix, ((0, 0), (0, 256 - matrix.shape[1]))))
        start += matrix.shape[0]
    return np.concatenate(rows, axis=0), places


def read(mats_ref, name):
    start, count, width = matrices()[1][name]
    return mats_ref[start : start + count, :width]


def read_rows(mats_ref, name, *pieces):
    start, count, width = matrices()[1][name]
    half = count // 2
    out = []
    for offset in (0, 0, half):
        for first, rows in pieces:
            at = start + offset + first
            out.append(mats_ref[at : at + rows, :width])
    return jnp.concatenate(out, axis=0)


def read_span_a(mats_ref):
    return read_rows(mats_ref, "span_a", (0, SPAN))


def read_span_b(mats_ref):
    start = matrices()[1]["span_b"][0]
    order = (0, 0, 1, 2, 2, 3)
    return jnp.concatenate(
        [mats_ref[start + i * SPAN : start + i * SPAN + SPAN] for i in order], axis=0
    )


def read_back(mats_ref, size):
    if size == 2:
        return read_rows(mats_ref, "pair_back", (0, 3 * SPAN))
    return read_rows(mats_ref, "pair_back", (0, SPAN), (2 * SPAN, SPAN))[:, :SPAN]


def split(x):
    high = x.astype(bf16)
    return high, (x - high.astype(f32)).astype(bf16)


def dot(a, b):
    return jnp.dot(a, b, preferred_element_type=f32)


def triple(x, axis):
    high, low = split(x)
    return jnp.concatenate([high, low, high], axis=axis)


def spots_of(count):
    spots = []
    for first in range(0, count, 2):
        group = tuple(range(first, min(first + 2, count)))
        spots += [(l,) for l in group] + [group + (None,) * (3 - len(group))]
    return spots


def chunks_of(count):
    spots = spots_of(count)
    return [spots[first : first + 2] for first in range(0, len(spots), 2)]


def span_forward(fields, mats):
    span_a, span_b = read_span_a(mats), read_span_b(mats)
    lefts = [triple(field, 1) for field in fields]
    spots = []
    for spot in spots_of(len(fields)):
        if len(spot) == 1:
            out = dot(lefts[spot[0]], span_a)
        elif spot[1] is None:
            out = dot(lefts[spot[0]], span_b[: 3 * SPAN])
        else:
            out = dot(jnp.concatenate([lefts[spot[0]], lefts[spot[1]]], axis=1), span_b)
        spots.append((out[:, :SPAN], out[:, SPAN:]))
    return spots


def plane_forward(spots, mats):
    plane, values = read(mats, "plane"), read(mats, "values")
    interp, deriv = (jnp.concatenate([s[i] for s in spots], axis=1) for i in range(2))
    interp, deriv = split(interp), split(deriv)
    outs = []
    for c in range(3):
        rows = slice(c * 64, c * 64 + 64)
        high, low = interp[0][rows], interp[1][rows]
        first = dot(plane, jnp.concatenate([high, low, high], axis=0))
        high, low = deriv[0][rows], deriv[1][rows]
        outs.append((first, dot(values, jnp.concatenate([high, low, high], axis=0))))
    return outs


def chunk_inverse(chunk, inverses):
    lane = lax.broadcasted_iota(jnp.int32, (1, SPAN), 1)
    out = []
    for spot in chunk:
        if len(spot) == 1 or spot[1] is None:
            out.append(inverses[spot[0]])
        else:
            out.append(jnp.where(lane < 64, inverses[spot[0]], inverses[spot[1]]))
    return jnp.concatenate(out, axis=1)


def convect_back(fine, inverse, mats):
    back = read(mats, "plane_back")
    parts = [([], []) for _ in range(3)]
    for first in range(0, 144, 48):
        rows = slice(first, first + 48)
        speeds = [fine(c, 0, rows) for c in range(3)]
        speeds[2] = speeds[2] * inverse
        for c in range(3):
            convect = (
                speeds[0] * fine(c, 1, rows)
                + speeds[1] * fine(c, 3, rows)
                + speeds[2] * fine(c, 2, rows)
            )
            for part, half in zip(parts[c], split(convect)):
                part.append(half)
    outs = []
    for high, low in parts:
        out = dot(back, jnp.concatenate(high, axis=0))
        outs.append(out[:64] + out[64:] + dot(back[:64], jnp.concatenate(low, axis=0)))
    return jnp.concatenate(outs, axis=0)


def span_back(count, backs, results, mats):
    for place, spot in enumerate(spots_of(count)):
        if len(spot) == 1 or place >= len(backs) or spot[0] < len(results):
            continue
        size = 1 if spot[1] is None else 2
        joined = jnp.concatenate(backs[place - size : place + 1], axis=1)
        out = dot(triple(joined, 1), read_back(mats, size))
        results += [out[:, i * SPAN : (i + 1) * SPAN] for i in range(size)]


def weak_spots(spots, inverses, mats, put):
    chunks = chunks_of(len(inverses))
    planes = []

    def finish(i):
        def fine(c, kind, rows):
            first, along_y = planes[i][c]
            if kind == 3:
                return along_y[rows]
            return first[kind * 144 + rows.start : kind * 144 + rows.stop]

        out = convect_back(fine, chunk_inverse(chunks[i], inverses), mats)
        for j in range(len(chunks[i])):
            put(2 * i + j, out[:, j * SPAN : (j + 1) * SPAN])

    for i in range(len(chunks)):
        planes.append(plane_forward(spots[2 * i : 2 * i + 2], mats))
        if i > 0:
            finish(i - 1)
    finish(len(chunks) - 1)


def weak_layers(fields, inverses, mats):
    backs, results = [], []

    def put(place, back):
        backs.append(back)
        span_back(len(fields), backs, results, mats)

    weak_spots(span_forward(fields, mats), inverses, mats, put)
    return results


def end_rows(x):
    x = x.reshape(3, 8, 8, SPAN)
    return jnp.concatenate([x[:, :1], x[:, 7:]], axis=1).reshape(48, SPAN)


def inner_rows(x):
    return x.reshape(3, 8, 8, SPAN)[:, 1:7].reshape(144, SPAN)


def face_spots(faces, mats):
    out_a = dot(triple(jnp.concatenate(faces, axis=0), 1), read_span_a(mats))
    even, odd = faces[0::2], faces[1::2]
    odd = odd + [jnp.zeros_like(faces[0])] * (len(even) - len(odd))
    even, odd = (triple(jnp.concatenate(x, axis=0), 1) for x in (even, odd))
    out_b = dot(jnp.concatenate([even, odd], axis=1), read_span_b(mats))
    spots = []
    for spot in spots_of(len(faces)):
        if len(spot) == 1:
            out = out_a[spot[0] * 48 : spot[0] * 48 + 48]
        else:
            out = out_b[spot[0] * 24 : spot[0] * 24 + 48]
        spots.append((out[:, :SPAN], out[:, SPAN:]))
    return spots


def with_faces(inner, faces):
    inner = inner.reshape(3, 6, 8, SPAN)
    faces = faces.reshape(3, 2, 8, SPAN)
    return jnp.concatenate([faces[:, :1], inner, faces[:, 1:]], axis=1).reshape(ROWS, SPAN)


def join_heights(layers, heights, joins):
    rows = layers[0].shape[0] // 8
    top, bottom = pl.ds(7, rows, stride=8), pl.ds(0, rows, stride=8)
    for lower, upper, wanted in joins:
        share = heights[upper] / (heights[lower] + heights[upper])
        share = share[:1]
        below, above = layers[lower][top, :], layers[upper][bottom, :]
        mean = below * (1.0 - share) + above * share
        if wanted is True:
            layers[lower][top, :] = mean
            layers[upper][bottom, :] = mean
        else:
            layers[lower][top, :] = jnp.where(wanted, mean, below)
            layers[upper][bottom, :] = jnp.where(wanted, mean, above)


def sides():
    place = lax.axis_index("horiz")
    left_share = jnp.where(place > 0, 0.5, 0.0).astype(f32)
    right_share = jnp.where(place < lax.axis_size("horiz") - 1, 0.5, 0.0).astype(f32)
    return lax.rem(place, 2) == 1, left_share, right_share


def join_ends(own_cross, own_core, cross, core):
    odd, left_share, right_share = sides()
    cross_share = jnp.where(odd, right_share, left_share)
    core_share = jnp.where(odd, left_share, right_share)
    cross = own_cross * (1.0 - cross_share) + cross * cross_share
    return cross, own_core * (1.0 - core_share) + core * core_share


def in_order(cross, core):
    odd = sides()[0]
    ends = jnp.where(odd, core, cross), jnp.where(odd, cross, core)
    return jnp.concatenate([end[:, None] for end in ends], axis=1)


def put_faces(ends, cross_ref, core_ref, at):
    odd = sides()[0]
    ends = ends.reshape(3, 2, 8, SPAN)
    first, last = ends[:, 0], ends[:, 1]
    cross_ref[at] = jnp.where(odd, last, first)
    core_ref[at] = jnp.where(odd, first, last)


def join_layers(heights, partial_ref, cross_ref, core_ref):
    count = len(heights)
    layers = [partial_ref.at[l] for l in range(count)]
    join_heights(layers, heights, [(l, l + 1, True) for l in range(count - 1)])
    for l in range(count):
        put_faces(end_rows(partial_ref[l]), cross_ref, core_ref, l)


def step_kernel(mats, step_ref, tile_ref):
    tile_ref[...] = jnp.broadcast_to(step_ref[...], (8, SPAN))


def raw_kernel(count, *refs):
    mats, packed, raws = refs[0], refs[2 : count + 2], refs[count + 2 :]
    results = weak_layers(
        [p[:ROWS] for p in packed], [1.0 / p[ROWS : ROWS + 1] for p in packed], mats
    )
    for raw_ref, result in zip(raws, results):
        raw_ref[...] = result


def slots_kernel(order, ready, *refs):
    count = len(order)
    mats, packed, given = refs[0], refs[2 : count + 2], refs[count + 2 : count + 2 + ready]
    field_ref, heights_ref, partial_ref, cross_ref, core_ref = refs[count + 2 + ready :]
    place = lax.axis_index("vert")
    slots = [jnp.bitwise_xor(place, j) for j in order]
    for i in range(count):
        field_ref[slots[i]] = packed[i][:ROWS]
        heights_ref[slots[i]] = packed[i][ROWS:]
    for i in range(ready):
        partial_ref[slots[i]] = given[i][...]
    results = weak_layers(
        [packed[i][:ROWS] for i in range(ready, count)],
        [1.0 / packed[i][ROWS : ROWS + 1] for i in range(ready, count)],
        mats,
    )
    for i in range(ready, count):
        partial_ref[slots[i]] = results[i - ready]
    heights = [heights_ref[l] for l in range(count)]
    join_layers(heights, partial_ref, cross_ref, core_ref)


def first_kernel(count, *refs):
    mats, packed_ref, refs = refs[0], refs[2], refs[3:]
    field_ref, heights_ref, partial_ref, cross_ref, core_ref = refs
    heights = [packed_ref[l, ROWS:] for l in range(count)]
    for l in range(count):
        field_ref[l] = packed_ref[l, :ROWS]
        heights_ref[l] = heights[l]
    results = weak_layers(
        [packed_ref[l, :ROWS] for l in range(count)], [1.0 / h[:1] for h in heights], mats
    )
    for l in range(count):
        partial_ref[l] = results[l]
    join_layers(heights, partial_ref, cross_ref, core_ref)


def stage_layers(count, last):
    if not last:
        return list(range(count))
    place = lax.axis_index("vert")
    return [place, jnp.minimum(place + 1, count - 1), jnp.maximum(place - 1, 0)]


def put_spots(partial, count, share, last, mats, step_ref, field_ref, spots_ref):
    step = step_ref[:1] * share
    fields = []
    for l in stage_layers(count, last):
        fields.append(inner_rows(field_ref[l]) + step * partial(l))
    for i, pair in enumerate(span_forward(fields, mats)):
        for part in range(2):
            spots_ref[i, part] = pair[part]


def first_inner_kernel(
    count, share, last, mats, step_ref, field_ref, partial_ref, spots_ref, total_ref
):
    def partial(l):
        return inner_rows(partial_ref[l])

    put_spots(partial, count, share, last, mats, step_ref, field_ref, spots_ref)
    total_ref[...] = partial(lax.axis_index("vert"))


def span_inner(backs_ref, partial_ref, count, mats):
    results = []
    span_back(count, [inner_rows(backs_ref[i]) for i in range(len(spots_of(count)))], results, mats)
    for l in range(count):
        partial_ref[l] = results[l]


def inner_kernel(count, share, last, *refs):
    mats, step_ref, field_ref, heights_ref, backs_ref, total_ref, spots_ref = refs[:7]
    next_total_ref, partial_ref = refs[7:]
    span_inner(backs_ref, partial_ref, count, mats)
    layers = [partial_ref.at[l] for l in range(count)]
    heights = [heights_ref[l] for l in range(count)]
    join_heights(layers, heights, [(l, l + 1, True) for l in range(count - 1)])

    def partial(l):
        return partial_ref[l]

    put_spots(partial, count, share, last, mats, step_ref, field_ref, spots_ref)
    next_total_ref[...] = total_ref[...] + 2.0 * partial(lax.axis_index("vert"))


def last_inner_kernel(count, mats, heights_ref, backs_ref, total_ref, rate_ref, partial_ref):
    place = lax.axis_index("vert")
    span_inner(backs_ref, partial_ref, 3, mats)
    heights = [heights_ref[l] for l in stage_layers(count, True)]
    layers = [partial_ref.at[i] for i in range(3)]
    join_heights(layers, heights, [(0, 1, place < count - 1), (2, 0, place > 0)])
    rate_ref[...] = (total_ref[...] + partial_ref[0]) / 6.0


def stage_kernel(count, share, first, last, *refs):
    mats, step_ref, field_ref, heights_ref, own_cross_ref, own_core_ref = refs[:6]
    cross_ref, core_ref, spots_ref = refs[6:9]
    total = None if first else refs[9]
    total_ref, backs_ref, next_cross_ref, next_core_ref, faces_ref = refs[-5:]
    place = lax.axis_index("vert")
    step = step_ref[:1] * share
    layers = stage_layers(count, last)
    heights = [heights_ref[l] for l in layers]
    fields = []
    for l in layers:
        ends = join_ends(own_cross_ref[l], own_core_ref[l], cross_ref[l], core_ref[l])
        ends = in_order(*ends).reshape(48, SPAN)
        fields.append(end_rows(field_ref[l]) + step * ends)
    spots = []
    for i, pair in enumerate(face_spots(fields, mats)):
        spots.append([with_faces(spots_ref[i, part], pair[part]) for part in range(2)])
    ends, results = [], []

    def put(i, back):
        backs_ref[i] = back
        ends.append(end_rows(back))
        span_back(len(layers), ends, results, mats)

    weak_spots(spots, [1.0 / h[:1] for h in heights], mats, put)
    for i, result in enumerate(results):
        faces_ref[i] = result
    faces = [faces_ref.at[i] for i in range(len(layers))]
    if last:
        join_heights(faces, heights, [(0, 1, place < count - 1), (2, 0, place > 0)])
        put_faces(faces_ref[0], next_cross_ref, next_core_ref, slice(None))
    else:
        join_heights(faces, heights, [(l, l + 1, True) for l in range(count - 1)])
        for l in range(count):
            put_faces(faces_ref[l], next_cross_ref, next_core_ref, l)
    own = join_ends(own_cross_ref[place], own_core_ref[place], cross_ref[place], core_ref[place])
    for k in range(2):
        total_ref[k] = own[k] if first else total[k] + 2.0 * own[k]


def rate_kernel(own_cross_ref, own_core_ref, cross_ref, core_ref, inner_ref, total_ref, rate_ref):
    ends = join_ends(own_cross_ref[...], own_core_ref[...], cross_ref[...], core_ref[...])
    ends = [(total_ref[k] + ends[k]) / 6.0 for k in range(2)]
    rate_ref[...] = with_faces(inner_ref[...], in_order(*ends))


VMEM = pl.BlockSpec(memory_space=pltpu.VMEM)


def call(kernel, outs, args, scratch=(), flops=0):
    shapes = [jax.ShapeDtypeStruct(shape, f32) for shape in outs]
    one = len(shapes) == 1
    return pl.pallas_call(
        kernel,
        out_shape=shapes[0] if one else shapes,
        in_specs=[VMEM] * len(args),
        out_specs=VMEM if one else [VMEM] * len(shapes),
        scratch_shapes=list(scratch),
        compiler_params=pltpu.CompilerParams(vmem_limit_bytes=32 * 1024 * 1024),
        cost_estimate=pl.CostEstimate(flops=flops, bytes_accessed=1 << 20, transcendentals=0),
    )(*args)


def swap_stream(cross, core):
    count = lax.axis_size("horiz")
    cores = [(i, i ^ 1) for i in range(count)]
    crosses = [(i, (i + 1) % count if i % 2 else (i - 1) % count) for i in range(count)]
    return lax.ppermute(cross, "horiz", crosses), lax.ppermute(core, "horiz", cores)


def on_device(velocity, heights, time_step):
    layers = lax.axis_size("vert")
    mats = jnp.asarray(matrices()[0])
    unit = 2 * 256 * 256 * 3000
    field = (layers, ROWS, SPAN)
    face = (layers, 3, 8, SPAN)
    small = (3, 8, SPAN)
    first_outs = [field, (layers, 8, SPAN), field, face, face]
    step = time_step.reshape(1, 1)
    tile = (8, SPAN)
    step = call(step_kernel, [tile], [mats, step], flops=2 * unit)
    own_field = velocity.reshape(ROWS, SPAN)
    packed = jnp.concatenate([own_field, jnp.broadcast_to(heights[:, None], (8, SPAN))], axis=0)
    if layers in (1, 2, 4):
        groups = {1: [[0]], 2: [[0], [1]], 4: [[0, 2], [3, 1]]}[layers]
        slots = {0: packed}
        for j in range(layers - 1, 0, -1):
            slots[j] = lax.ppermute(packed, "vert", [(i, i ^ j) for i in range(layers)])
        given = []
        for group in groups[:-1]:
            outs = [(ROWS, SPAN)] * len(group)
            args = [mats, step] + [slots[j] for j in group]
            raw = call(
                functools.partial(raw_kernel, len(group)), outs, args, flops=len(group) * unit
            )
            given += [raw] if len(group) == 1 else raw
        order = sum(groups, [])
        args = [mats, step] + [slots[j] for j in order] + given
        first = functools.partial(slots_kernel, order, len(given))
    else:
        args = [mats, step, lax.all_gather(packed, "vert")]
        first = functools.partial(first_kernel, layers)
    fields, all_heights, partial, cross, core = call(
        first, first_outs, args, flops=layers * unit
    )
    own_ends = cross, core
    ends = swap_stream(cross, core)
    backs = face_total = None
    for stage, share in enumerate((0.5, 0.5, 1.0)):
        last = stage == 2
        used = 3 if last else layers
        outs = [(len(spots_of(used)), 2, 144, SPAN), (144, SPAN)]
        if stage == 0:
            spots, total = call(
                functools.partial(first_inner_kernel, layers, share, last),
                outs,
                [mats, step, fields, partial],
                flops=used * unit // 4,
            )
        else:
            spots, total = call(
                functools.partial(inner_kernel, layers, share, last),
                outs,
                [mats, step, fields, all_heights, backs, total],
                scratch=[pltpu.VMEM((layers, 144, SPAN), f32)],
                flops=used * unit // 2,
            )
        args = [mats, step, fields, all_heights, *own_ends, *ends, spots]
        end = small if last else face
        face_total, backs, cross, core = call(
            functools.partial(stage_kernel, layers, share, stage == 0, last),
            [(2,) + small, (len(spots_of(used)), ROWS, SPAN), end, end],
            args + ([] if stage == 0 else [face_total]),
            scratch=[pltpu.VMEM((used, 48, SPAN), f32)],
            flops=used * unit,
        )
        own_ends = cross, core
        ends = swap_stream(cross, core)
    inner = call(
        functools.partial(last_inner_kernel, layers),
        [(144, SPAN)],
        [mats, all_heights, backs, total],
        scratch=[pltpu.VMEM((3, 144, SPAN), f32)],
        flops=unit // 2,
    )
    rate = call(rate_kernel, [(ROWS, SPAN)], [*own_ends, *ends, inner, face_total])
    return rate.reshape(velocity.shape)


def solution(mesh):
    in_specs = (P(None, "horiz", "vert", None), P("vert"), P())
    out_specs = P(None, "horiz", "vert", None)
    return jax.shard_map(
        on_device, mesh=mesh, in_specs=in_specs, out_specs=out_specs, check_vma=False
    )
```

```python
import functools

import jax
import jax.numpy as jnp
import ml_dtypes
import numpy as np
from jax import lax
from jax.experimental import pallas as pl
from jax.experimental.pallas import tpu as pltpu
from jax.sharding import PartitionSpec as P

gll_half = [1.0, 0.8717401485096066, 0.5917001814331423, 0.2092992179024789]
gll_half_weights = [
    0.03571428571428571,
    0.21070422714350603,
    0.34112269248350435,
    0.4124587946587038,
]
gauss_half = [
    0.9815606342467192,
    0.9041172563704749,
    0.7699026741943047,
    0.5873179542866175,
    0.3678314989981802,
    0.1252334085114689,
]
gauss_half_weights = [
    0.0471753363865118,
    0.1069393259953184,
    0.1600783285433462,
    0.2031674267230659,
    0.2334925365383548,
    0.2491470458134028,
]

f32 = jnp.float32
bf16 = jnp.bfloat16
ROWS = 192
SPAN = 128
SPAN_ELEMENTS = 16


def mirrored(values, sign):
    return np.concatenate([sign * np.array(values), np.array(values[::-1])])


def lagrange(targets, sources):
    matrix = np.ones((targets.size, sources.size))
    for j in range(sources.size):
        for k in range(sources.size):
            if k != j:
                matrix[:, j] = matrix[:, j] * (targets - sources[k]) / (sources[j] - sources[k])
    return matrix


def node_tables():
    gll_points = mirrored(gll_half, -1.0)
    gll_weights = mirrored(gll_half_weights, 1.0)
    fine_points = mirrored(gauss_half, -1.0)
    fine_weights = mirrored(gauss_half_weights, 1.0)
    to_fine = lagrange(fine_points, gll_points)
    products = np.ones(8)
    for i in range(8):
        for k in range(8):
            if k != i:
                products[i] = products[i] * (gll_points[i] - gll_points[k])
    deriv_mat = np.zeros((8, 8))
    for i in range(8):
        for j in range(8):
            if i != j:
                deriv_mat[i, j] = products[i] / (products[j] * (gll_points[i] - gll_points[j]))
                deriv_mat[i, i] = deriv_mat[i, i] + 1.0 / (gll_points[i] - gll_points[j])
    return to_fine, to_fine @ deriv_mat, gll_weights, fine_weights


def halves(matrix):
    high = matrix.astype(ml_dtypes.bfloat16)
    low = (matrix - high.astype(np.float64)).astype(ml_dtypes.bfloat16)
    return high, low


def stack_columns(matrix):
    high, low = halves(matrix)
    return np.concatenate([high, high, low], axis=1)


def span_blocks(block, first, count):
    out = np.zeros((SPAN, SPAN_ELEMENTS * count))
    for e in range(SPAN_ELEMENTS):
        out[e * 8 : e * 8 + 8, e * count : (e + 1) * count] = block[first : first + count].T
    return out


@functools.cache
def matrices():
    interp, deriv, gll_w, fine_w = node_tables()
    a_both = np.concatenate([span_blocks(interp, 0, 8), span_blocks(2.0 * deriv, 0, 8)], axis=1)
    span_a = np.concatenate(halves(a_both), axis=0)
    interp_b = span_blocks(interp, 8, 4)
    deriv_b = span_blocks(2.0 * deriv, 8, 4)
    none = np.zeros_like(interp_b)
    first_b = halves(np.concatenate([interp_b, none, deriv_b, none], axis=1))
    second_b = halves(np.concatenate([none, interp_b, none, deriv_b], axis=1))
    span_b = np.concatenate(first_b + second_b, axis=0)
    values = np.kron(interp, interp)
    plane = np.concatenate([values, np.kron(2.0 * deriv, interp), np.kron(interp, 2.0 * deriv)])
    plane = stack_columns(plane)
    values = stack_columns(values)
    back = interp.T * fine_w[None, :] / gll_w[:, None]
    plane_back = np.concatenate(halves(-np.kron(back, back)), axis=0)
    a_back = np.zeros((SPAN, SPAN))
    b_back = np.zeros((SPAN // 2, SPAN))
    for e in range(SPAN_ELEMENTS):
        a_back[e * 8 : e * 8 + 8, e * 8 : e * 8 + 8] = back[:, :8].T
        b_back[e * 4 : e * 4 + 4, e * 8 : e * 8 + 8] = back[:, 8:].T
    span = np.concatenate([a_back, b_back], axis=0)
    summed = span.copy()
    for e in range(SPAN_ELEMENTS):
        last, first = e * 8 + 7, (e * 8 + 8) % SPAN
        mean = 0.5 * (span[:, last] + span[:, first])
        summed[:, last] = mean
        summed[:, first] = mean
    a_back, b_back = summed[:SPAN], summed[SPAN:]
    zero_a, zero_b = np.zeros_like(a_back), np.zeros_like(b_back)
    pair_back = np.concatenate(
        [
            np.concatenate([a_back, zero_a], axis=1),
            np.concatenate([zero_a, a_back], axis=1),
            np.concatenate([b_back, zero_b], axis=1),
            np.concatenate([zero_b, b_back], axis=1),
        ],
        axis=0,
    )
    wide = {
        "span_a": span_a,
        "span_b": span_b,
        "plane": plane,
        "values": values,
        "plane_back": plane_back,
        "pair_back": np.concatenate(halves(pair_back), axis=0),
    }
    rows, places = [], {}
    start = 0
    for name, matrix in wide.items():
        places[name] = (start, matrix.shape[0], matrix.shape[1])
        rows.append(np.pad(matrix, ((0, 0), (0, 256 - matrix.shape[1]))))
        start += matrix.shape[0]
    return np.concatenate(rows, axis=0), places


def read(mats_ref, name):
    start, count, width = matrices()[1][name]
    return mats_ref[start : start + count, :width]


def read_rows(mats_ref, name, *pieces):
    start, count, width = matrices()[1][name]
    half = count // 2
    out = []
    for offset in (0, 0, half):
        for first, rows in pieces:
            at = start + offset + first
            out.append(mats_ref[at : at + rows, :width])
    return jnp.concatenate(out, axis=0)


def read_span_a(mats_ref):
    return read_rows(mats_ref, "span_a", (0, SPAN))


def read_span_b(mats_ref):
    start = matrices()[1]["span_b"][0]
    order = (0, 0, 1, 2, 2, 3)
    return jnp.concatenate(
        [mats_ref[start + i * SPAN : start + i * SPAN + SPAN] for i in order], axis=0
    )


def read_back(mats_ref, size):
    if size == 2:
        return read_rows(mats_ref, "pair_back", (0, 3 * SPAN))
    return read_rows(mats_ref, "pair_back", (0, SPAN), (2 * SPAN, SPAN))[:, :SPAN]


def split(x):
    high = x.astype(bf16)
    return high, (x - high.astype(f32)).astype(bf16)


def dot(a, b):
    return jnp.dot(a, b, preferred_element_type=f32)


def triple(x, axis):
    high, low = split(x)
    return jnp.concatenate([high, low, high], axis=axis)


def spots_of(count):
    spots = []
    for first in range(0, count, 2):
        group = tuple(range(first, min(first + 2, count)))
        spots += [(l,) for l in group] + [group + (None,) * (3 - len(group))]
    return spots


def chunks_of(count):
    spots = spots_of(count)
    return [spots[first : first + 2] for first in range(0, len(spots), 2)]


def span_forward(fields, mats):
    span_a, span_b = read_span_a(mats), read_span_b(mats)
    lefts = [triple(field, 1) for field in fields]
    spots = []
    for spot in spots_of(len(fields)):
        if len(spot) == 1:
            out = dot(lefts[spot[0]], span_a)
        elif spot[1] is None:
            out = dot(lefts[spot[0]], span_b[: 3 * SPAN])
        else:
            out = dot(jnp.concatenate([lefts[spot[0]], lefts[spot[1]]], axis=1), span_b)
        spots.append((out[:, :SPAN], out[:, SPAN:]))
    return spots


def plane_forward(spots, mats):
    plane, values = read(mats, "plane"), read(mats, "values")
    interp, deriv = (jnp.concatenate([s[i] for s in spots], axis=1) for i in range(2))
    interp, deriv = split(interp), split(deriv)
    outs = []
    for c in range(3):
        rows = slice(c * 64, c * 64 + 64)
        high, low = interp[0][rows], interp[1][rows]
        first = dot(plane, jnp.concatenate([high, low, high], axis=0))
        high, low = deriv[0][rows], deriv[1][rows]
        outs.append((first, dot(values, jnp.concatenate([high, low, high], axis=0))))
    return outs


def chunk_inverse(chunk, inverses):
    lane = lax.broadcasted_iota(jnp.int32, (1, SPAN), 1)
    out = []
    for spot in chunk:
        if len(spot) == 1 or spot[1] is None:
            out.append(inverses[spot[0]])
        else:
            out.append(jnp.where(lane < 64, inverses[spot[0]], inverses[spot[1]]))
    return jnp.concatenate(out, axis=1)


def convect_back(fine, inverse, mats):
    back = read(mats, "plane_back")
    parts = [([], []) for _ in range(3)]
    for first in range(0, 144, 48):
        rows = slice(first, first + 48)
        speeds = [fine(c, 0, rows) for c in range(3)]
        speeds[2] = speeds[2] * inverse
        for c in range(3):
            convect = (
                speeds[0] * fine(c, 1, rows)
                + speeds[1] * fine(c, 3, rows)
                + speeds[2] * fine(c, 2, rows)
            )
            for part, half in zip(parts[c], split(convect)):
                part.append(half)
    outs = []
    for high, low in parts:
        out = dot(back, jnp.concatenate(high, axis=0))
        outs.append(out[:64] + out[64:] + dot(back[:64], jnp.concatenate(low, axis=0)))
    return jnp.concatenate(outs, axis=0)


def span_back(count, backs, results, mats):
    for place, spot in enumerate(spots_of(count)):
        if len(spot) == 1 or place >= len(backs) or spot[0] < len(results):
            continue
        size = 1 if spot[1] is None else 2
        joined = jnp.concatenate(backs[place - size : place + 1], axis=1)
        out = dot(triple(joined, 1), read_back(mats, size))
        results += [out[:, i * SPAN : (i + 1) * SPAN] for i in range(size)]


def weak_spots(spots, inverses, mats, put):
    chunks = chunks_of(len(inverses))
    planes = []

    def finish(i):
        def fine(c, kind, rows):
            first, along_y = planes[i][c]
            if kind == 3:
                return along_y[rows]
            return first[kind * 144 + rows.start : kind * 144 + rows.stop]

        out = convect_back(fine, chunk_inverse(chunks[i], inverses), mats)
        for j in range(len(chunks[i])):
            put(2 * i + j, out[:, j * SPAN : (j + 1) * SPAN])

    for i in range(len(chunks)):
        planes.append(plane_forward(spots[2 * i : 2 * i + 2], mats))
        if i > 0:
            finish(i - 1)
    finish(len(chunks) - 1)


def weak_layers(fields, inverses, mats):
    backs, results = [], []

    def put(place, back):
        backs.append(back)
        span_back(len(fields), backs, results, mats)

    weak_spots(span_forward(fields, mats), inverses, mats, put)
    return results


def end_rows(x):
    x = x.reshape(3, 8, 8, SPAN)
    return jnp.concatenate([x[:, :1], x[:, 7:]], axis=1).reshape(48, SPAN)


def inner_rows(x):
    return x.reshape(3, 8, 8, SPAN)[:, 1:7].reshape(144, SPAN)


def face_spots(faces, mats):
    out_a = dot(triple(jnp.concatenate(faces, axis=0), 1), read_span_a(mats))
    even, odd = faces[0::2], faces[1::2]
    odd = odd + [jnp.zeros_like(faces[0])] * (len(even) - len(odd))
    even, odd = (triple(jnp.concatenate(x, axis=0), 1) for x in (even, odd))
    out_b = dot(jnp.concatenate([even, odd], axis=1), read_span_b(mats))
    spots = []
    for spot in spots_of(len(faces)):
        if len(spot) == 1:
            out = out_a[spot[0] * 48 : spot[0] * 48 + 48]
        else:
            out = out_b[spot[0] * 24 : spot[0] * 24 + 48]
        spots.append((out[:, :SPAN], out[:, SPAN:]))
    return spots


def with_faces(inner, faces):
    inner = inner.reshape(3, 6, 8, SPAN)
    faces = faces.reshape(3, 2, 8, SPAN)
    return jnp.concatenate([faces[:, :1], inner, faces[:, 1:]], axis=1).reshape(ROWS, SPAN)


def join_heights(layers, heights, joins):
    rows = layers[0].shape[0] // 8
    top, bottom = pl.ds(7, rows, stride=8), pl.ds(0, rows, stride=8)
    for lower, upper, wanted in joins:
        share = heights[upper] / (heights[lower] + heights[upper])
        share = share[:1]
        below, above = layers[lower][top, :], layers[upper][bottom, :]
        mean = below * (1.0 - share) + above * share
        if wanted is True:
            layers[lower][top, :] = mean
            layers[upper][bottom, :] = mean
        else:
            layers[lower][top, :] = jnp.where(wanted, mean, below)
            layers[upper][bottom, :] = jnp.where(wanted, mean, above)


def sides():
    place = lax.axis_index("horiz")
    left_share = jnp.where(place > 0, 0.5, 0.0).astype(f32)
    right_share = jnp.where(place < lax.axis_size("horiz") - 1, 0.5, 0.0).astype(f32)
    return lax.rem(place, 2) == 1, left_share, right_share


def join_ends(own_cross, own_core, cross, core):
    odd, left_share, right_share = sides()
    cross_share = jnp.where(odd, right_share, left_share)
    core_share = jnp.where(odd, left_share, right_share)
    cross = own_cross * (1.0 - cross_share) + cross * cross_share
    return cross, own_core * (1.0 - core_share) + core * core_share


def in_order(cross, core):
    odd = sides()[0]
    ends = jnp.where(odd, core, cross), jnp.where(odd, cross, core)
    return jnp.concatenate([end[:, None] for end in ends], axis=1)


def put_faces(ends, cross_ref, core_ref, at):
    odd = sides()[0]
    ends = ends.reshape(3, 2, 8, SPAN)
    first, last = ends[:, 0], ends[:, 1]
    cross_ref[at] = jnp.where(odd, last, first)
    core_ref[at] = jnp.where(odd, first, last)


def join_layers(heights, partial_ref, cross_ref, core_ref):
    count = len(heights)
    layers = [partial_ref.at[l] for l in range(count)]
    join_heights(layers, heights, [(l, l + 1, True) for l in range(count - 1)])
    for l in range(count):
        put_faces(end_rows(partial_ref[l]), cross_ref, core_ref, l)


def step_kernel(mats, step_ref, tile_ref):
    tile_ref[...] = jnp.broadcast_to(step_ref[...], (8, SPAN))


def raw_kernel(count, *refs):
    mats, packed, raws = refs[0], refs[2 : count + 2], refs[count + 2 :]
    results = weak_layers(
        [p[:ROWS] for p in packed], [1.0 / p[ROWS : ROWS + 1] for p in packed], mats
    )
    for raw_ref, result in zip(raws, results):
        raw_ref[...] = result


def slots_kernel(order, ready, *refs):
    count = len(order)
    mats, packed, given = refs[0], refs[2 : count + 2], refs[count + 2 : count + 2 + ready]
    field_ref, heights_ref, partial_ref, cross_ref, core_ref = refs[count + 2 + ready :]
    place = lax.axis_index("vert")
    slots = [jnp.bitwise_xor(place, j) for j in order]
    for i in range(count):
        field_ref[slots[i]] = packed[i][:ROWS]
        heights_ref[slots[i]] = packed[i][ROWS:]
    for i in range(ready):
        partial_ref[slots[i]] = given[i][...]
    results = weak_layers(
        [packed[i][:ROWS] for i in range(ready, count)],
        [1.0 / packed[i][ROWS : ROWS + 1] for i in range(ready, count)],
        mats,
    )
    for i in range(ready, count):
        partial_ref[slots[i]] = results[i - ready]
    heights = [heights_ref[l] for l in range(count)]
    join_layers(heights, partial_ref, cross_ref, core_ref)


def first_kernel(count, *refs):
    mats, packed_ref, refs = refs[0], refs[2], refs[3:]
    field_ref, heights_ref, partial_ref, cross_ref, core_ref = refs
    heights = [packed_ref[l, ROWS:] for l in range(count)]
    for l in range(count):
        field_ref[l] = packed_ref[l, :ROWS]
        heights_ref[l] = heights[l]
    results = weak_layers(
        [packed_ref[l, :ROWS] for l in range(count)], [1.0 / h[:1] for h in heights], mats
    )
    for l in range(count):
        partial_ref[l] = results[l]
    join_layers(heights, partial_ref, cross_ref, core_ref)


def stage_layers(count, last):
    if not last:
        return list(range(count))
    place = lax.axis_index("vert")
    return [place, jnp.minimum(place + 1, count - 1), jnp.maximum(place - 1, 0)]


def put_spots(partial, count, share, last, mats, step_ref, field_ref, spots_ref):
    step = step_ref[:1] * share
    fields = []
    for l in stage_layers(count, last):
        fields.append(inner_rows(field_ref[l]) + step * partial(l))
    for i, pair in enumerate(span_forward(fields, mats)):
        for part in range(2):
            spots_ref[i, part] = pair[part]


def first_inner_kernel(
    count, share, last, mats, step_ref, field_ref, partial_ref, spots_ref, total_ref
):
    def partial(l):
        return inner_rows(partial_ref[l])

    put_spots(partial, count, share, last, mats, step_ref, field_ref, spots_ref)
    total_ref[...] = partial(lax.axis_index("vert"))


def span_inner(backs_ref, partial_ref, count, mats):
    results = []
    span_back(count, [inner_rows(backs_ref[i]) for i in range(len(spots_of(count)))], results, mats)
    for l in range(count):
        partial_ref[l] = results[l]


def inner_kernel(count, share, last, *refs):
    mats, step_ref, field_ref, heights_ref, backs_ref, total_ref, spots_ref = refs[:7]
    next_total_ref, partial_ref = refs[7:]
    span_inner(backs_ref, partial_ref, count, mats)
    layers = [partial_ref.at[l] for l in range(count)]
    heights = [heights_ref[l] for l in range(count)]
    join_heights(layers, heights, [(l, l + 1, True) for l in range(count - 1)])

    def partial(l):
        return partial_ref[l]

    put_spots(partial, count, share, last, mats, step_ref, field_ref, spots_ref)
    next_total_ref[...] = total_ref[...] + 2.0 * partial(lax.axis_index("vert"))


def last_inner_kernel(count, mats, heights_ref, backs_ref, total_ref, rate_ref, partial_ref):
    place = lax.axis_index("vert")
    span_inner(backs_ref, partial_ref, 3, mats)
    heights = [heights_ref[l] for l in stage_layers(count, True)]
    layers = [partial_ref.at[i] for i in range(3)]
    join_heights(layers, heights, [(0, 1, place < count - 1), (2, 0, place > 0)])
    rate_ref[...] = (total_ref[...] + partial_ref[0]) / 6.0


def stage_kernel(count, share, first, last, *refs):
    mats, step_ref, field_ref, heights_ref, own_cross_ref, own_core_ref = refs[:6]
    cross_ref, core_ref, spots_ref = refs[6:9]
    total = None if first else refs[9]
    total_ref, backs_ref, next_cross_ref, next_core_ref, faces_ref = refs[-5:]
    place = lax.axis_index("vert")
    step = step_ref[:1] * share
    layers = stage_layers(count, last)
    heights = [heights_ref[l] for l in layers]
    fields = []
    for l in layers:
        ends = join_ends(own_cross_ref[l], own_core_ref[l], cross_ref[l], core_ref[l])
        ends = in_order(*ends).reshape(48, SPAN)
        fields.append(end_rows(field_ref[l]) + step * ends)
    spots = []
    for i, pair in enumerate(face_spots(fields, mats)):
        spots.append([with_faces(spots_ref[i, part], pair[part]) for part in range(2)])
    ends, results = [], []

    def put(i, back):
        backs_ref[i] = back
        ends.append(end_rows(back))
        span_back(len(layers), ends, results, mats)

    weak_spots(spots, [1.0 / h[:1] for h in heights], mats, put)
    for i, result in enumerate(results):
        faces_ref[i] = result
    faces = [faces_ref.at[i] for i in range(len(layers))]
    if last:
        join_heights(faces, heights, [(0, 1, place < count - 1), (2, 0, place > 0)])
        put_faces(faces_ref[0], next_cross_ref, next_core_ref, slice(None))
    else:
        join_heights(faces, heights, [(l, l + 1, True) for l in range(count - 1)])
        for l in range(count):
            put_faces(faces_ref[l], next_cross_ref, next_core_ref, l)
    own = join_ends(own_cross_ref[place], own_core_ref[place], cross_ref[place], core_ref[place])
    for k in range(2):
        total_ref[k] = own[k] if first else total[k] + 2.0 * own[k]


def rate_kernel(own_cross_ref, own_core_ref, cross_ref, core_ref, inner_ref, total_ref, rate_ref):
    ends = join_ends(own_cross_ref[...], own_core_ref[...], cross_ref[...], core_ref[...])
    ends = [(total_ref[k] + ends[k]) / 6.0 for k in range(2)]
    rate_ref[...] = with_faces(inner_ref[...], in_order(*ends))


VMEM = pl.BlockSpec(memory_space=pltpu.VMEM)


def call(kernel, outs, args, scratch=(), flops=0):
    shapes = [jax.ShapeDtypeStruct(shape, f32) for shape in outs]
    one = len(shapes) == 1
    return pl.pallas_call(
        kernel,
        out_shape=shapes[0] if one else shapes,
        in_specs=[VMEM] * len(args),
        out_specs=VMEM if one else [VMEM] * len(shapes),
        scratch_shapes=list(scratch),
        compiler_params=pltpu.CompilerParams(vmem_limit_bytes=32 * 1024 * 1024),
        cost_estimate=pl.CostEstimate(flops=flops, bytes_accessed=1 << 20, transcendentals=0),
    )(*args)


def swap_stream(cross, core):
    count = lax.axis_size("horiz")
    cores = [(i, i ^ 1) for i in range(count)]
    crosses = [(i, (i + 1) % count if i % 2 else (i - 1) % count) for i in range(count)]
    return lax.ppermute(cross, "horiz", crosses), lax.ppermute(core, "horiz", cores)


def on_device(velocity, heights, time_step):
    layers = lax.axis_size("vert")
    mats = jnp.asarray(matrices()[0])
    unit = 2 * 256 * 256 * 3000
    field = (layers, ROWS, SPAN)
    face = (layers, 3, 8, SPAN)
    small = (3, 8, SPAN)
    first_outs = [field, (layers, 8, SPAN), field, face, face]
    step = time_step.reshape(1, 1)
    tile = (8, SPAN)
    step = call(step_kernel, [tile], [mats, step], flops=2 * unit)
    own_field = velocity.reshape(ROWS, SPAN)
    packed = jnp.concatenate([own_field, jnp.broadcast_to(heights[:, None], (8, SPAN))], axis=0)
    if layers in (1, 2, 4):
        groups = {1: [[0]], 2: [[0], [1]], 4: [[0, 1, 2], [3]]}[layers]
        slots = {0: packed}
        for j in range(layers - 1, 0, -1):
            slots[j] = lax.ppermute(packed, "vert", [(i, i ^ j) for i in range(layers)])
        given = []
        for group in groups[:-1]:
            outs = [(ROWS, SPAN)] * len(group)
            args = [mats, step] + [slots[j] for j in group]
            raw = call(
                functools.partial(raw_kernel, len(group)), outs, args, flops=len(group) * unit
            )
            given += [raw] if len(group) == 1 else raw
        order = sum(groups, [])
        args = [mats, step] + [slots[j] for j in order] + given
        first = functools.partial(slots_kernel, order, len(given))
    else:
        args = [mats, step, lax.all_gather(packed, "vert")]
        first = functools.partial(first_kernel, layers)
    fields, all_heights, partial, cross, core = call(
        first, first_outs, args, flops=layers * unit
    )
    own_ends = cross, core
    ends = swap_stream(cross, core)
    backs = face_total = None
    for stage, share in enumerate((0.5, 0.5, 1.0)):
        last = stage == 2
        used = 3 if last else layers
        outs = [(len(spots_of(used)), 2, 144, SPAN), (144, SPAN)]
        if stage == 0:
            spots, total = call(
                functools.partial(first_inner_kernel, layers, share, last),
                outs,
                [mats, step, fields, partial],
                flops=used * unit // 4,
            )
        else:
            spots, total = call(
                functools.partial(inner_kernel, layers, share, last),
                outs,
                [mats, step, fields, all_heights, backs, total],
                scratch=[pltpu.VMEM((layers, 144, SPAN), f32)],
                flops=used * unit // 2,
            )
        args = [mats, step, fields, all_heights, *own_ends, *ends, spots]
        end = small if last else face
        face_total, backs, cross, core = call(
            functools.partial(stage_kernel, layers, share, stage == 0, last),
            [(2,) + small, (len(spots_of(used)), ROWS, SPAN), end, end],
            args + ([] if stage == 0 else [face_total]),
            scratch=[pltpu.VMEM((used, 48, SPAN), f32)],
            flops=used * unit,
        )
        own_ends = cross, core
        ends = swap_stream(cross, core)
    inner = call(
        functools.partial(last_inner_kernel, layers),
        [(144, SPAN)],
        [mats, all_heights, backs, total],
        scratch=[pltpu.VMEM((3, 144, SPAN), f32)],
        flops=unit // 2,
    )
    rate = call(rate_kernel, [(ROWS, SPAN)], [*own_ends, *ends, inner, face_total])
    return rate.reshape(velocity.shape)


def solution(mesh):
    in_specs = (P(None, "horiz", "vert", None), P("vert"), P())
    out_specs = P(None, "horiz", "vert", None)
    return jax.shard_map(
        on_device, mesh=mesh, in_specs=in_specs, out_specs=out_specs, check_vma=False
    )
```

```python
import functools

import jax
import jax.numpy as jnp
import ml_dtypes
import numpy as np
from jax import lax
from jax.experimental import pallas as pl
from jax.experimental.pallas import tpu as pltpu
from jax.sharding import PartitionSpec as P

gll_half = [1.0, 0.8717401485096066, 0.5917001814331423, 0.2092992179024789]
gll_half_weights = [
    0.03571428571428571,
    0.21070422714350603,
    0.34112269248350435,
    0.4124587946587038,
]
gauss_half = [
    0.9815606342467192,
    0.9041172563704749,
    0.7699026741943047,
    0.5873179542866175,
    0.3678314989981802,
    0.1252334085114689,
]
gauss_half_weights = [
    0.0471753363865118,
    0.1069393259953184,
    0.1600783285433462,
    0.2031674267230659,
    0.2334925365383548,
    0.2491470458134028,
]

f32 = jnp.float32
bf16 = jnp.bfloat16
ROWS = 192
SPAN = 128
SPAN_ELEMENTS = 16


def mirrored(values, sign):
    return np.concatenate([sign * np.array(values), np.array(values[::-1])])


def lagrange(targets, sources):
    matrix = np.ones((targets.size, sources.size))
    for j in range(sources.size):
        for k in range(sources.size):
            if k != j:
                matrix[:, j] = matrix[:, j] * (targets - sources[k]) / (sources[j] - sources[k])
    return matrix


def node_tables():
    gll_points = mirrored(gll_half, -1.0)
    gll_weights = mirrored(gll_half_weights, 1.0)
    fine_points = mirrored(gauss_half, -1.0)
    fine_weights = mirrored(gauss_half_weights, 1.0)
    to_fine = lagrange(fine_points, gll_points)
    products = np.ones(8)
    for i in range(8):
        for k in range(8):
            if k != i:
                products[i] = products[i] * (gll_points[i] - gll_points[k])
    deriv_mat = np.zeros((8, 8))
    for i in range(8):
        for j in range(8):
            if i != j:
                deriv_mat[i, j] = products[i] / (products[j] * (gll_points[i] - gll_points[j]))
                deriv_mat[i, i] = deriv_mat[i, i] + 1.0 / (gll_points[i] - gll_points[j])
    return to_fine, to_fine @ deriv_mat, gll_weights, fine_weights


def halves(matrix):
    high = matrix.astype(ml_dtypes.bfloat16)
    low = (matrix - high.astype(np.float64)).astype(ml_dtypes.bfloat16)
    return high, low


def stack_columns(matrix):
    high, low = halves(matrix)
    return np.concatenate([high, high, low], axis=1)


def span_blocks(block, first, count):
    out = np.zeros((SPAN, SPAN_ELEMENTS * count))
    for e in range(SPAN_ELEMENTS):
        out[e * 8 : e * 8 + 8, e * count : (e + 1) * count] = block[first : first + count].T
    return out


@functools.cache
def matrices():
    interp, deriv, gll_w, fine_w = node_tables()
    a_both = np.concatenate([span_blocks(interp, 0, 8), span_blocks(2.0 * deriv, 0, 8)], axis=1)
    span_a = np.concatenate(halves(a_both), axis=0)
    interp_b = span_blocks(interp, 8, 4)
    deriv_b = span_blocks(2.0 * deriv, 8, 4)
    none = np.zeros_like(interp_b)
    first_b = halves(np.concatenate([interp_b, none, deriv_b, none], axis=1))
    second_b = halves(np.concatenate([none, interp_b, none, deriv_b], axis=1))
    span_b = np.concatenate(first_b + second_b, axis=0)
    values = np.kron(interp, interp)
    plane = np.concatenate([values, np.kron(2.0 * deriv, interp), np.kron(interp, 2.0 * deriv)])
    order = np.concatenate([np.arange(8, 56), np.arange(8), np.arange(56, 64)])
    plane, values = plane[:, order], values[:, order]
    plane = stack_columns(plane)
    values = stack_columns(values)
    back = interp.T * fine_w[None, :] / gll_w[:, None]
    plane_back = np.concatenate(halves(-np.kron(back, back)), axis=0)
    a_back = np.zeros((SPAN, SPAN))
    b_back = np.zeros((SPAN // 2, SPAN))
    for e in range(SPAN_ELEMENTS):
        a_back[e * 8 : e * 8 + 8, e * 8 : e * 8 + 8] = back[:, :8].T
        b_back[e * 4 : e * 4 + 4, e * 8 : e * 8 + 8] = back[:, 8:].T
    span = np.concatenate([a_back, b_back], axis=0)
    summed = span.copy()
    for e in range(SPAN_ELEMENTS):
        last, first = e * 8 + 7, (e * 8 + 8) % SPAN
        mean = 0.5 * (span[:, last] + span[:, first])
        summed[:, last] = mean
        summed[:, first] = mean
    a_back, b_back = summed[:SPAN], summed[SPAN:]
    zero_a, zero_b = np.zeros_like(a_back), np.zeros_like(b_back)
    pair_back = np.concatenate(
        [
            np.concatenate([a_back, zero_a], axis=1),
            np.concatenate([zero_a, a_back], axis=1),
            np.concatenate([b_back, zero_b], axis=1),
            np.concatenate([zero_b, b_back], axis=1),
        ],
        axis=0,
    )
    wide = {
        "span_a": span_a,
        "span_b": span_b,
        "plane": plane,
        "values": values,
        "plane_back": plane_back,
        "pair_back": np.concatenate(halves(pair_back), axis=0),
    }
    rows, places = [], {}
    start = 0
    for name, matrix in wide.items():
        places[name] = (start, matrix.shape[0], matrix.shape[1])
        rows.append(np.pad(matrix, ((0, 0), (0, 256 - matrix.shape[1]))))
        start += matrix.shape[0]
    return np.concatenate(rows, axis=0), places


def read(mats_ref, name):
    start, count, width = matrices()[1][name]
    return mats_ref[start : start + count, :width]


def read_rows(mats_ref, name, *pieces):
    start, count, width = matrices()[1][name]
    half = count // 2
    out = []
    for offset in (0, 0, half):
        for first, rows in pieces:
            at = start + offset + first
            out.append(mats_ref[at : at + rows, :width])
    return jnp.concatenate(out, axis=0)


def read_span_a(mats_ref):
    return read_rows(mats_ref, "span_a", (0, SPAN))


def read_span_b(mats_ref):
    start = matrices()[1]["span_b"][0]
    order = (0, 0, 1, 2, 2, 3)
    return jnp.concatenate(
        [mats_ref[start + i * SPAN : start + i * SPAN + SPAN] for i in order], axis=0
    )


def read_back(mats_ref, size):
    if size == 2:
        return read_rows(mats_ref, "pair_back", (0, 3 * SPAN))
    return read_rows(mats_ref, "pair_back", (0, SPAN), (2 * SPAN, SPAN))[:, :SPAN]


def split(x):
    high = x.astype(bf16)
    return high, (x - high.astype(f32)).astype(bf16)


def dot(a, b):
    return jnp.dot(a, b, preferred_element_type=f32)


def triple(x, axis):
    high, low = split(x)
    return jnp.concatenate([high, low, high], axis=axis)


def spots_of(count):
    spots = []
    for first in range(0, count, 2):
        group = tuple(range(first, min(first + 2, count)))
        spots += [(l,) for l in group] + [group + (None,) * (3 - len(group))]
    return spots


def chunks_of(count):
    spots = spots_of(count)
    return [spots[first : first + 2] for first in range(0, len(spots), 2)]


def span_forward(fields, mats):
    span_a, span_b = read_span_a(mats), read_span_b(mats)
    lefts = [triple(field, 1) for field in fields]
    spots = []
    for spot in spots_of(len(fields)):
        if len(spot) == 1:
            out = dot(lefts[spot[0]], span_a)
        elif spot[1] is None:
            out = dot(lefts[spot[0]], span_b[: 3 * SPAN])
        else:
            out = dot(jnp.concatenate([lefts[spot[0]], lefts[spot[1]]], axis=1), span_b)
        spots.append((out[:, :SPAN], out[:, SPAN:]))
    return spots


def plane_parts(x):
    out = []
    for c in range(3):
        rows = x[c * 64 : c * 64 + 64]
        out.append(split(jnp.concatenate([rows[8:56], rows[:8], rows[56:]], axis=0)))
    return out


def plane_forward(spots, mats):
    plane, values = read(mats, "plane"), read(mats, "values")
    outs = []
    for c in range(3):
        pair = []
        for part, matrix in enumerate((plane, values)):
            high, low = (jnp.concatenate([s[part][c][k] for s in spots], axis=1) for k in range(2))
            pair.append(dot(matrix, jnp.concatenate([high, low, high], axis=0)))
        outs.append(pair)
    return outs


def chunk_inverse(chunk, inverses):
    lane = lax.broadcasted_iota(jnp.int32, (1, SPAN), 1)
    out = []
    for spot in chunk:
        if len(spot) == 1 or spot[1] is None:
            out.append(inverses[spot[0]])
        else:
            out.append(jnp.where(lane < 64, inverses[spot[0]], inverses[spot[1]]))
    return jnp.concatenate(out, axis=1)


def convect_back(fine, inverse, mats):
    back = read(mats, "plane_back")
    parts = [([], []) for _ in range(3)]
    for first in range(0, 144, 48):
        rows = slice(first, first + 48)
        speeds = [fine(c, 0, rows) for c in range(3)]
        speeds[2] = speeds[2] * inverse
        for c in range(3):
            convect = (
                speeds[0] * fine(c, 1, rows)
                + speeds[1] * fine(c, 3, rows)
                + speeds[2] * fine(c, 2, rows)
            )
            for part, half in zip(parts[c], split(convect)):
                part.append(half)
    outs = []
    for high, low in parts:
        out = dot(back, jnp.concatenate(high, axis=0))
        outs.append(out[:64] + out[64:] + dot(back[:64], jnp.concatenate(low, axis=0)))
    return jnp.concatenate(outs, axis=0)


def span_back(count, backs, results, mats):
    for place, spot in enumerate(spots_of(count)):
        if len(spot) == 1 or place >= len(backs) or spot[0] < len(results):
            continue
        size = 1 if spot[1] is None else 2
        joined = jnp.concatenate(backs[place - size : place + 1], axis=1)
        out = dot(triple(joined, 1), read_back(mats, size))
        results += [out[:, i * SPAN : (i + 1) * SPAN] for i in range(size)]


def weak_spots(spots, inverses, mats, put):
    chunks = chunks_of(len(inverses))
    planes = []

    def finish(i):
        def fine(c, kind, rows):
            first, along_y = planes[i][c]
            if kind == 3:
                return along_y[rows]
            return first[kind * 144 + rows.start : kind * 144 + rows.stop]

        out = convect_back(fine, chunk_inverse(chunks[i], inverses), mats)
        for j in range(len(chunks[i])):
            put(2 * i + j, out[:, j * SPAN : (j + 1) * SPAN])

    for i in range(len(chunks)):
        planes.append(plane_forward(spots[2 * i : 2 * i + 2], mats))
        if i > 0:
            finish(i - 1)
    finish(len(chunks) - 1)


def weak_layers(fields, inverses, mats):
    backs, results = [], []

    def put(place, back):
        backs.append(back)
        span_back(len(fields), backs, results, mats)

    spots = [[plane_parts(x) for x in pair] for pair in span_forward(fields, mats)]
    weak_spots(spots, inverses, mats, put)
    return results


def end_rows(x):
    x = x.reshape(3, 8, 8, SPAN)
    return jnp.concatenate([x[:, :1], x[:, 7:]], axis=1).reshape(48, SPAN)


def inner_rows(x):
    return x.reshape(3, 8, 8, SPAN)[:, 1:7].reshape(144, SPAN)


def face_spots(faces, mats):
    out_a = dot(triple(jnp.concatenate(faces, axis=0), 1), read_span_a(mats))
    even, odd = faces[0::2], faces[1::2]
    odd = odd + [jnp.zeros_like(faces[0])] * (len(even) - len(odd))
    even, odd = (triple(jnp.concatenate(x, axis=0), 1) for x in (even, odd))
    out_b = dot(jnp.concatenate([even, odd], axis=1), read_span_b(mats))
    spots = []
    for spot in spots_of(len(faces)):
        if len(spot) == 1:
            out = out_a[spot[0] * 48 : spot[0] * 48 + 48]
        else:
            out = out_b[spot[0] * 24 : spot[0] * 24 + 48]
        spots.append((out[:, :SPAN], out[:, SPAN:]))
    return spots


def with_faces(inner, faces):
    inner = inner.reshape(3, 6, 8, SPAN)
    faces = faces.reshape(3, 2, 8, SPAN)
    return jnp.concatenate([faces[:, :1], inner, faces[:, 1:]], axis=1).reshape(ROWS, SPAN)


def parts_with_faces(inner_ref, faces):
    out = []
    for c in range(3):
        ends = split(faces[c * 16 : c * 16 + 16])
        out.append(
            [
                jnp.concatenate([inner_ref[k, c * 48 : c * 48 + 48], ends[k]], axis=0)
                for k in range(2)
            ]
        )
    return out


def join_heights(layers, heights, joins):
    rows = layers[0].shape[0] // 8
    top, bottom = pl.ds(7, rows, stride=8), pl.ds(0, rows, stride=8)
    for lower, upper, wanted in joins:
        share = heights[upper] / (heights[lower] + heights[upper])
        share = share[:1]
        below, above = layers[lower][top, :], layers[upper][bottom, :]
        mean = below * (1.0 - share) + above * share
        if wanted is True:
            layers[lower][top, :] = mean
            layers[upper][bottom, :] = mean
        else:
            layers[lower][top, :] = jnp.where(wanted, mean, below)
            layers[upper][bottom, :] = jnp.where(wanted, mean, above)


def sides():
    place = lax.axis_index("horiz")
    left_share = jnp.where(place > 0, 0.5, 0.0).astype(f32)
    right_share = jnp.where(place < lax.axis_size("horiz") - 1, 0.5, 0.0).astype(f32)
    return lax.rem(place, 2) == 1, left_share, right_share


def join_ends(own_cross, own_core, cross, core):
    odd, left_share, right_share = sides()
    cross_share = jnp.where(odd, right_share, left_share)
    core_share = jnp.where(odd, left_share, right_share)
    cross = own_cross * (1.0 - cross_share) + cross * cross_share
    return cross, own_core * (1.0 - core_share) + core * core_share


def in_order(cross, core):
    odd = sides()[0]
    ends = jnp.where(odd, core, cross), jnp.where(odd, cross, core)
    return jnp.concatenate([end[:, None] for end in ends], axis=1)


def put_faces(ends, cross_ref, core_ref, at):
    odd = sides()[0]
    ends = ends.reshape(3, 2, 8, SPAN)
    first, last = ends[:, 0], ends[:, 1]
    cross_ref[at] = jnp.where(odd, last, first)
    core_ref[at] = jnp.where(odd, first, last)


def join_layers(heights, partial_ref, cross_ref, core_ref):
    count = len(heights)
    layers = [partial_ref.at[l] for l in range(count)]
    join_heights(layers, heights, [(l, l + 1, True) for l in range(count - 1)])
    for l in range(count):
        put_faces(end_rows(partial_ref[l]), cross_ref, core_ref, l)


def step_kernel(mats, step_ref, tile_ref):
    tile_ref[...] = jnp.broadcast_to(step_ref[...], (8, SPAN))


def raw_kernel(count, *refs):
    mats, packed, raws = refs[0], refs[2 : count + 2], refs[count + 2 :]
    results = weak_layers(
        [p[:ROWS] for p in packed], [1.0 / p[ROWS : ROWS + 1] for p in packed], mats
    )
    for raw_ref, result in zip(raws, results):
        raw_ref[...] = result


def slots_kernel(order, ready, *refs):
    count = len(order)
    mats, packed, given = refs[0], refs[2 : count + 2], refs[count + 2 : count + 2 + ready]
    field_ref, heights_ref, partial_ref, cross_ref, core_ref = refs[count + 2 + ready :]
    place = lax.axis_index("vert")
    slots = [jnp.bitwise_xor(place, j) for j in order]
    for i in range(count):
        field_ref[slots[i]] = packed[i][:ROWS]
        heights_ref[slots[i]] = packed[i][ROWS:]
    for i in range(ready):
        partial_ref[slots[i]] = given[i][...]
    results = weak_layers(
        [packed[i][:ROWS] for i in range(ready, count)],
        [1.0 / packed[i][ROWS : ROWS + 1] for i in range(ready, count)],
        mats,
    )
    for i in range(ready, count):
        partial_ref[slots[i]] = results[i - ready]
    heights = [heights_ref[l] for l in range(count)]
    join_layers(heights, partial_ref, cross_ref, core_ref)


def first_kernel(count, *refs):
    mats, packed_ref, refs = refs[0], refs[2], refs[3:]
    field_ref, heights_ref, partial_ref, cross_ref, core_ref = refs
    heights = [packed_ref[l, ROWS:] for l in range(count)]
    for l in range(count):
        field_ref[l] = packed_ref[l, :ROWS]
        heights_ref[l] = heights[l]
    results = weak_layers(
        [packed_ref[l, :ROWS] for l in range(count)], [1.0 / h[:1] for h in heights], mats
    )
    for l in range(count):
        partial_ref[l] = results[l]
    join_layers(heights, partial_ref, cross_ref, core_ref)


def stage_layers(count, last):
    if not last:
        return list(range(count))
    place = lax.axis_index("vert")
    return [place, jnp.minimum(place + 1, count - 1), jnp.maximum(place - 1, 0)]


def put_spots(partial, count, share, last, mats, step_ref, field_ref, spots_ref):
    step = step_ref[:1] * share
    fields = []
    for l in stage_layers(count, last):
        fields.append(inner_rows(field_ref[l]) + step * partial(l))
    for i, pair in enumerate(span_forward(fields, mats)):
        for part in range(2):
            for k, half in enumerate(split(pair[part])):
                spots_ref[i, part, k] = half


def first_inner_kernel(
    count, share, last, mats, step_ref, field_ref, partial_ref, spots_ref, total_ref
):
    def partial(l):
        return inner_rows(partial_ref[l])

    put_spots(partial, count, share, last, mats, step_ref, field_ref, spots_ref)
    total_ref[...] = partial(lax.axis_index("vert"))


def span_inner(backs_ref, partial_ref, count, mats):
    results = []
    span_back(count, [inner_rows(backs_ref[i]) for i in range(len(spots_of(count)))], results, mats)
    for l in range(count):
        partial_ref[l] = results[l]


def inner_kernel(count, share, last, *refs):
    mats, step_ref, field_ref, heights_ref, backs_ref, total_ref, spots_ref = refs[:7]
    next_total_ref, partial_ref = refs[7:]
    span_inner(backs_ref, partial_ref, count, mats)
    layers = [partial_ref.at[l] for l in range(count)]
    heights = [heights_ref[l] for l in range(count)]
    join_heights(layers, heights, [(l, l + 1, True) for l in range(count - 1)])

    def partial(l):
        return partial_ref[l]

    put_spots(partial, count, share, last, mats, step_ref, field_ref, spots_ref)
    next_total_ref[...] = total_ref[...] + 2.0 * partial(lax.axis_index("vert"))


def last_inner_kernel(count, mats, heights_ref, backs_ref, total_ref, rate_ref, partial_ref):
    place = lax.axis_index("vert")
    span_inner(backs_ref, partial_ref, 3, mats)
    heights = [heights_ref[l] for l in stage_layers(count, True)]
    layers = [partial_ref.at[i] for i in range(3)]
    join_heights(layers, heights, [(0, 1, place < count - 1), (2, 0, place > 0)])
    rate_ref[...] = (total_ref[...] + partial_ref[0]) / 6.0


def stage_kernel(count, share, first, last, *refs):
    mats, step_ref, field_ref, heights_ref, own_cross_ref, own_core_ref = refs[:6]
    cross_ref, core_ref, spots_ref = refs[6:9]
    total = None if first else refs[9]
    total_ref, backs_ref, next_cross_ref, next_core_ref, faces_ref = refs[-5:]
    place = lax.axis_index("vert")
    step = step_ref[:1] * share
    layers = stage_layers(count, last)
    heights = [heights_ref[l] for l in layers]
    fields = []
    for l in layers:
        ends = join_ends(own_cross_ref[l], own_core_ref[l], cross_ref[l], core_ref[l])
        ends = in_order(*ends).reshape(48, SPAN)
        fields.append(end_rows(field_ref[l]) + step * ends)
    spots = []
    for i, pair in enumerate(face_spots(fields, mats)):
        spots.append([parts_with_faces(spots_ref.at[i, part], pair[part]) for part in range(2)])
    ends, results = [], []

    def put(i, back):
        backs_ref[i] = back
        ends.append(end_rows(back))
        span_back(len(layers), ends, results, mats)

    weak_spots(spots, [1.0 / h[:1] for h in heights], mats, put)
    for i, result in enumerate(results):
        faces_ref[i] = result
    faces = [faces_ref.at[i] for i in range(len(layers))]
    if last:
        join_heights(faces, heights, [(0, 1, place < count - 1), (2, 0, place > 0)])
        put_faces(faces_ref[0], next_cross_ref, next_core_ref, slice(None))
    else:
        join_heights(faces, heights, [(l, l + 1, True) for l in range(count - 1)])
        for l in range(count):
            put_faces(faces_ref[l], next_cross_ref, next_core_ref, l)
    own = join_ends(own_cross_ref[place], own_core_ref[place], cross_ref[place], core_ref[place])
    for k in range(2):
        total_ref[k] = own[k] if first else total[k] + 2.0 * own[k]


def rate_kernel(own_cross_ref, own_core_ref, cross_ref, core_ref, inner_ref, total_ref, rate_ref):
    ends = join_ends(own_cross_ref[...], own_core_ref[...], cross_ref[...], core_ref[...])
    ends = [(total_ref[k] + ends[k]) / 6.0 for k in range(2)]
    rate_ref[...] = with_faces(inner_ref[...], in_order(*ends))


VMEM = pl.BlockSpec(memory_space=pltpu.VMEM)


def call(kernel, outs, args, scratch=(), flops=0):
    shapes = [
        jax.ShapeDtypeStruct(shape, bf16 if len(shape) == 5 else f32) for shape in outs
    ]
    one = len(shapes) == 1
    return pl.pallas_call(
        kernel,
        out_shape=shapes[0] if one else shapes,
        in_specs=[VMEM] * len(args),
        out_specs=VMEM if one else [VMEM] * len(shapes),
        scratch_shapes=list(scratch),
        compiler_params=pltpu.CompilerParams(vmem_limit_bytes=32 * 1024 * 1024),
        cost_estimate=pl.CostEstimate(flops=flops, bytes_accessed=1 << 20, transcendentals=0),
    )(*args)


def swap_stream(cross, core):
    count = lax.axis_size("horiz")
    cores = [(i, i ^ 1) for i in range(count)]
    crosses = [(i, (i + 1) % count if i % 2 else (i - 1) % count) for i in range(count)]
    return lax.ppermute(cross, "horiz", crosses), lax.ppermute(core, "horiz", cores)


def on_device(velocity, heights, time_step):
    layers = lax.axis_size("vert")
    mats = jnp.asarray(matrices()[0])
    unit = 2 * 256 * 256 * 3000
    field = (layers, ROWS, SPAN)
    face = (layers, 3, 8, SPAN)
    small = (3, 8, SPAN)
    first_outs = [field, (layers, 8, SPAN), field, face, face]
    step = time_step.reshape(1, 1)
    tile = (8, SPAN)
    step = call(step_kernel, [tile], [mats, step], flops=2 * unit)
    own_field = velocity.reshape(ROWS, SPAN)
    packed = jnp.concatenate([own_field, jnp.broadcast_to(heights[:, None], (8, SPAN))], axis=0)
    if layers in (1, 2, 4):
        groups = {1: [[0]], 2: [[0], [1]], 4: [[0, 1, 2], [3]]}[layers]
        slots = {0: packed}
        for j in range(layers - 1, 0, -1):
            slots[j] = lax.ppermute(packed, "vert", [(i, i ^ j) for i in range(layers)])
        given = []
        for group in groups[:-1]:
            outs = [(ROWS, SPAN)] * len(group)
            args = [mats, step] + [slots[j] for j in group]
            raw = call(
                functools.partial(raw_kernel, len(group)), outs, args, flops=len(group) * unit
            )
            given += [raw] if len(group) == 1 else raw
        order = sum(groups, [])
        args = [mats, step] + [slots[j] for j in order] + given
        first = functools.partial(slots_kernel, order, len(given))
    else:
        args = [mats, step, lax.all_gather(packed, "vert")]
        first = functools.partial(first_kernel, layers)
    fields, all_heights, partial, cross, core = call(
        first, first_outs, args, flops=layers * unit
    )
    own_ends = cross, core
    ends = swap_stream(cross, core)
    backs = face_total = None
    for stage, share in enumerate((0.5, 0.5, 1.0)):
        last = stage == 2
        used = 3 if last else layers
        outs = [(len(spots_of(used)), 2, 2, 144, SPAN), (144, SPAN)]
        if stage == 0:
            spots, total = call(
                functools.partial(first_inner_kernel, layers, share, last),
                outs,
                [mats, step, fields, partial],
                flops=used * unit // 4,
            )
        else:
            spots, total = call(
                functools.partial(inner_kernel, layers, share, last),
                outs,
                [mats, step, fields, all_heights, backs, total],
                scratch=[pltpu.VMEM((layers, 144, SPAN), f32)],
                flops=used * unit // 2,
            )
        args = [mats, step, fields, all_heights, *own_ends, *ends, spots]
        end = small if last else face
        face_total, backs, cross, core = call(
            functools.partial(stage_kernel, layers, share, stage == 0, last),
            [(2,) + small, (len(spots_of(used)), ROWS, SPAN), end, end],
            args + ([] if stage == 0 else [face_total]),
            scratch=[pltpu.VMEM((used, 48, SPAN), f32)],
            flops=used * unit,
        )
        own_ends = cross, core
        ends = swap_stream(cross, core)
    inner = call(
        functools.partial(last_inner_kernel, layers),
        [(144, SPAN)],
        [mats, all_heights, backs, total],
        scratch=[pltpu.VMEM((3, 144, SPAN), f32)],
        flops=unit // 2,
    )
    rate = call(rate_kernel, [(ROWS, SPAN)], [*own_ends, *ends, inner, face_total])
    return rate.reshape(velocity.shape)


def solution(mesh):
    in_specs = (P(None, "horiz", "vert", None), P("vert"), P())
    out_specs = P(None, "horiz", "vert", None)
    return jax.shard_map(
        on_device, mesh=mesh, in_specs=in_specs, out_specs=out_specs, check_vma=False
    )
```

```python
import functools

import jax
import jax.numpy as jnp
import ml_dtypes
import numpy as np
from jax import lax
from jax.experimental import pallas as pl
from jax.experimental.pallas import tpu as pltpu
from jax.sharding import PartitionSpec as P

gll_half = [1.0, 0.8717401485096066, 0.5917001814331423, 0.2092992179024789]
gll_half_weights = [
    0.03571428571428571,
    0.21070422714350603,
    0.34112269248350435,
    0.4124587946587038,
]
gauss_half = [
    0.9815606342467192,
    0.9041172563704749,
    0.7699026741943047,
    0.5873179542866175,
    0.3678314989981802,
    0.1252334085114689,
]
gauss_half_weights = [
    0.0471753363865118,
    0.1069393259953184,
    0.1600783285433462,
    0.2031674267230659,
    0.2334925365383548,
    0.2491470458134028,
]

f32 = jnp.float32
bf16 = jnp.bfloat16
ROWS = 192
SPAN = 128
SPAN_ELEMENTS = 16


def mirrored(values, sign):
    return np.concatenate([sign * np.array(values), np.array(values[::-1])])


def lagrange(targets, sources):
    matrix = np.ones((targets.size, sources.size))
    for j in range(sources.size):
        for k in range(sources.size):
            if k != j:
                matrix[:, j] = matrix[:, j] * (targets - sources[k]) / (sources[j] - sources[k])
    return matrix


def node_tables():
    gll_points = mirrored(gll_half, -1.0)
    gll_weights = mirrored(gll_half_weights, 1.0)
    fine_points = mirrored(gauss_half, -1.0)
    fine_weights = mirrored(gauss_half_weights, 1.0)
    to_fine = lagrange(fine_points, gll_points)
    products = np.ones(8)
    for i in range(8):
        for k in range(8):
            if k != i:
                products[i] = products[i] * (gll_points[i] - gll_points[k])
    deriv_mat = np.zeros((8, 8))
    for i in range(8):
        for j in range(8):
            if i != j:
                deriv_mat[i, j] = products[i] / (products[j] * (gll_points[i] - gll_points[j]))
                deriv_mat[i, i] = deriv_mat[i, i] + 1.0 / (gll_points[i] - gll_points[j])
    return to_fine, to_fine @ deriv_mat, gll_weights, fine_weights


def halves(matrix):
    high = matrix.astype(ml_dtypes.bfloat16)
    low = (matrix - high.astype(np.float64)).astype(ml_dtypes.bfloat16)
    return high, low


def stack_columns(matrix):
    high, low = halves(matrix)
    return np.concatenate([high, high, low], axis=1)


def span_blocks(block, first, count):
    out = np.zeros((SPAN, SPAN_ELEMENTS * count))
    for e in range(SPAN_ELEMENTS):
        out[e * 8 : e * 8 + 8, e * count : (e + 1) * count] = block[first : first + count].T
    return out


@functools.cache
def matrices():
    interp, deriv, gll_w, fine_w = node_tables()
    a_both = np.concatenate([span_blocks(interp, 0, 8), span_blocks(2.0 * deriv, 0, 8)], axis=1)
    span_a = np.concatenate(halves(a_both), axis=0)
    interp_b = span_blocks(interp, 8, 4)
    deriv_b = span_blocks(2.0 * deriv, 8, 4)
    none = np.zeros_like(interp_b)
    first_b = halves(np.concatenate([interp_b, none, deriv_b, none], axis=1))
    second_b = halves(np.concatenate([none, interp_b, none, deriv_b], axis=1))
    span_b = np.concatenate(first_b + second_b, axis=0)
    values = np.kron(interp, interp)
    plane = np.concatenate([values, np.kron(2.0 * deriv, interp), np.kron(interp, 2.0 * deriv)])
    order = np.concatenate([np.arange(8, 56), np.arange(8), np.arange(56, 64)])
    plane, values = plane[:, order], values[:, order]
    plane = stack_columns(plane)
    values = stack_columns(values)
    back = interp.T * fine_w[None, :] / gll_w[:, None]
    plane_back = np.concatenate(halves(-np.kron(back, back)), axis=0)
    a_back = np.zeros((SPAN, SPAN))
    b_back = np.zeros((SPAN // 2, SPAN))
    for e in range(SPAN_ELEMENTS):
        a_back[e * 8 : e * 8 + 8, e * 8 : e * 8 + 8] = back[:, :8].T
        b_back[e * 4 : e * 4 + 4, e * 8 : e * 8 + 8] = back[:, 8:].T
    span = np.concatenate([a_back, b_back], axis=0)
    summed = span.copy()
    for e in range(SPAN_ELEMENTS):
        last, first = e * 8 + 7, (e * 8 + 8) % SPAN
        mean = 0.5 * (span[:, last] + span[:, first])
        summed[:, last] = mean
        summed[:, first] = mean
    a_back, b_back = summed[:SPAN], summed[SPAN:]
    zero_a, zero_b = np.zeros_like(a_back), np.zeros_like(b_back)
    pair_back = np.concatenate(
        [
            np.concatenate([a_back, zero_a], axis=1),
            np.concatenate([zero_a, a_back], axis=1),
            np.concatenate([b_back, zero_b], axis=1),
            np.concatenate([zero_b, b_back], axis=1),
        ],
        axis=0,
    )
    wide = {
        "span_a": span_a,
        "span_b": span_b,
        "plane": plane,
        "values": values,
        "plane_back": plane_back,
        "pair_back": np.concatenate(halves(pair_back), axis=0),
    }
    rows, places = [], {}
    start = 0
    for name, matrix in wide.items():
        places[name] = (start, matrix.shape[0], matrix.shape[1])
        rows.append(np.pad(matrix, ((0, 0), (0, 256 - matrix.shape[1]))))
        start += matrix.shape[0]
    return np.concatenate(rows, axis=0), places


def read(mats_ref, name):
    start, count, width = matrices()[1][name]
    return mats_ref[start : start + count, :width]


def read_rows(mats_ref, name, *pieces):
    start, count, width = matrices()[1][name]
    half = count // 2
    out = []
    for offset in (0, 0, half):
        for first, rows in pieces:
            at = start + offset + first
            out.append(mats_ref[at : at + rows, :width])
    return jnp.concatenate(out, axis=0)


def read_span_a(mats_ref):
    return read_rows(mats_ref, "span_a", (0, SPAN))


def read_span_b(mats_ref):
    start = matrices()[1]["span_b"][0]
    order = (0, 0, 1, 2, 2, 3)
    return jnp.concatenate(
        [mats_ref[start + i * SPAN : start + i * SPAN + SPAN] for i in order], axis=0
    )


def read_back(mats_ref, size):
    if size == 2:
        return read_rows(mats_ref, "pair_back", (0, 3 * SPAN))
    return read_rows(mats_ref, "pair_back", (0, SPAN), (2 * SPAN, SPAN))[:, :SPAN]


def split(x):
    high = x.astype(bf16)
    return high, (x - high.astype(f32)).astype(bf16)


def dot(a, b):
    return jnp.dot(a, b, preferred_element_type=f32)


def triple(x, axis):
    high, low = split(x)
    return jnp.concatenate([high, low, high], axis=axis)


def spots_of(count):
    spots = []
    for first in range(0, count, 2):
        group = tuple(range(first, min(first + 2, count)))
        spots += [(l,) for l in group] + [group + (None,) * (3 - len(group))]
    return spots


def chunks_of(count):
    spots = spots_of(count)
    return [spots[first : first + 2] for first in range(0, len(spots), 2)]


def span_forward(fields, mats):
    span_a, span_b = read_span_a(mats), read_span_b(mats)
    lefts = [triple(field, 1) for field in fields]
    spots = []
    for spot in spots_of(len(fields)):
        if len(spot) == 1:
            out = dot(lefts[spot[0]], span_a)
        elif spot[1] is None:
            out = dot(lefts[spot[0]], span_b[: 3 * SPAN])
        else:
            out = dot(jnp.concatenate([lefts[spot[0]], lefts[spot[1]]], axis=1), span_b)
        spots.append((out[:, :SPAN], out[:, SPAN:]))
    return spots


def plane_parts(x):
    out = []
    for c in range(3):
        rows = x[c * 64 : c * 64 + 64]
        out.append(split(jnp.concatenate([rows[8:56], rows[:8], rows[56:]], axis=0)))
    return out


def plane_forward(spots, mats):
    plane, values = read(mats, "plane"), read(mats, "values")
    outs = []
    for c in range(3):
        pair = []
        for part, matrix in enumerate((plane, values)):
            high, low = (jnp.concatenate([s[part][c][k] for s in spots], axis=1) for k in range(2))
            pair.append(dot(matrix, jnp.concatenate([high, low, high], axis=0)))
        outs.append(pair)
    return outs


def chunk_inverse(chunk, inverses):
    lane = lax.broadcasted_iota(jnp.int32, (1, SPAN), 1)
    out = []
    for spot in chunk:
        if len(spot) == 1 or spot[1] is None:
            out.append(inverses[spot[0]])
        else:
            out.append(jnp.where(lane < 64, inverses[spot[0]], inverses[spot[1]]))
    return jnp.concatenate(out, axis=1)


def convect_back(fine, inverse, mats):
    back = read(mats, "plane_back")
    parts = [([], []) for _ in range(3)]
    for first in range(0, 144, 48):
        rows = slice(first, first + 48)
        speeds = [fine(c, 0, rows) for c in range(3)]
        speeds[2] = speeds[2] * inverse
        for c in range(3):
            convect = (
                speeds[0] * fine(c, 1, rows)
                + speeds[1] * fine(c, 3, rows)
                + speeds[2] * fine(c, 2, rows)
            )
            for part, half in zip(parts[c], split(convect)):
                part.append(half)
    outs = []
    for high, low in parts:
        out = dot(back, jnp.concatenate(high, axis=0))
        outs.append(out[:64] + out[64:] + dot(back[:64], jnp.concatenate(low, axis=0)))
    return jnp.concatenate(outs, axis=0)


def span_back(count, backs, results, mats):
    for place, spot in enumerate(spots_of(count)):
        if len(spot) == 1 or place >= len(backs) or spot[0] < len(results):
            continue
        size = 1 if spot[1] is None else 2
        joined = jnp.concatenate(backs[place - size : place + 1], axis=1)
        out = dot(triple(joined, 1), read_back(mats, size))
        results += [out[:, i * SPAN : (i + 1) * SPAN] for i in range(size)]


def weak_spots(spots, inverses, mats, put):
    chunks = chunks_of(len(inverses))
    planes = []

    def finish(i):
        def fine(c, kind, rows):
            first, along_y = planes[i][c]
            if kind == 3:
                return along_y[rows]
            return first[kind * 144 + rows.start : kind * 144 + rows.stop]

        out = convect_back(fine, chunk_inverse(chunks[i], inverses), mats)
        for j in range(len(chunks[i])):
            put(2 * i + j, out[:, j * SPAN : (j + 1) * SPAN])

    for i in range(len(chunks)):
        planes.append(plane_forward(spots[2 * i : 2 * i + 2], mats))
        if i > 0:
            finish(i - 1)
    finish(len(chunks) - 1)


def weak_layers(fields, inverses, mats):
    backs, results = [], []

    def put(place, back):
        backs.append(back)
        span_back(len(fields), backs, results, mats)

    spots = [[plane_parts(x) for x in pair] for pair in span_forward(fields, mats)]
    weak_spots(spots, inverses, mats, put)
    return results


def end_rows(x):
    x = x.reshape(3, 8, 8, SPAN)
    return jnp.concatenate([x[:, :1], x[:, 7:]], axis=1).reshape(48, SPAN)


def inner_rows(x):
    return x.reshape(3, 8, 8, SPAN)[:, 1:7].reshape(144, SPAN)


def face_spots(faces, mats):
    out_a = dot(triple(jnp.concatenate(faces, axis=0), 1), read_span_a(mats))
    even, odd = faces[0::2], faces[1::2]
    odd = odd + [jnp.zeros_like(faces[0])] * (len(even) - len(odd))
    even, odd = (triple(jnp.concatenate(x, axis=0), 1) for x in (even, odd))
    out_b = dot(jnp.concatenate([even, odd], axis=1), read_span_b(mats))
    spots = []
    for spot in spots_of(len(faces)):
        if len(spot) == 1:
            out = out_a[spot[0] * 48 : spot[0] * 48 + 48]
        else:
            out = out_b[spot[0] * 24 : spot[0] * 24 + 48]
        spots.append((out[:, :SPAN], out[:, SPAN:]))
    return spots


def with_faces(inner, faces):
    inner = inner.reshape(3, 6, 8, SPAN)
    faces = faces.reshape(3, 2, 8, SPAN)
    return jnp.concatenate([faces[:, :1], inner, faces[:, 1:]], axis=1).reshape(ROWS, SPAN)


def parts_with_faces(inner_ref, faces):
    out = []
    for c in range(3):
        ends = split(faces[c * 16 : c * 16 + 16])
        out.append(
            [
                jnp.concatenate([inner_ref[k, c * 48 : c * 48 + 48], ends[k]], axis=0)
                for k in range(2)
            ]
        )
    return out


def join_heights(layers, heights, joins):
    rows = layers[0].shape[0] // 8
    top, bottom = pl.ds(7, rows, stride=8), pl.ds(0, rows, stride=8)
    for lower, upper, wanted in joins:
        share = heights[upper] / (heights[lower] + heights[upper])
        share = share[:1]
        below, above = layers[lower][top, :], layers[upper][bottom, :]
        mean = below * (1.0 - share) + above * share
        if wanted is True:
            layers[lower][top, :] = mean
            layers[upper][bottom, :] = mean
        else:
            layers[lower][top, :] = jnp.where(wanted, mean, below)
            layers[upper][bottom, :] = jnp.where(wanted, mean, above)


def sides():
    place = lax.axis_index("horiz")
    left_share = jnp.where(place > 0, 0.5, 0.0).astype(f32)
    right_share = jnp.where(place < lax.axis_size("horiz") - 1, 0.5, 0.0).astype(f32)
    return lax.rem(place, 2) == 1, left_share, right_share


def join_ends(own_cross, own_core, cross, core):
    odd, left_share, right_share = sides()
    cross_share = jnp.where(odd, right_share, left_share)
    core_share = jnp.where(odd, left_share, right_share)
    cross = own_cross * (1.0 - cross_share) + cross * cross_share
    return cross, own_core * (1.0 - core_share) + core * core_share


def in_order(cross, core):
    odd = sides()[0]
    ends = jnp.where(odd, core, cross), jnp.where(odd, cross, core)
    return jnp.concatenate([end[:, None] for end in ends], axis=1)


def put_faces(ends, cross_ref, core_ref, at):
    odd = sides()[0]
    ends = ends.reshape(3, 2, 8, SPAN)
    first, last = ends[:, 0], ends[:, 1]
    cross_ref[at] = jnp.where(odd, last, first)
    core_ref[at] = jnp.where(odd, first, last)


def join_layers(heights, partial_ref, cross_ref, core_ref):
    count = len(heights)
    layers = [partial_ref.at[l] for l in range(count)]
    join_heights(layers, heights, [(l, l + 1, True) for l in range(count - 1)])
    for l in range(count):
        put_faces(end_rows(partial_ref[l]), cross_ref, core_ref, l)


def step_kernel(mats, step_ref, tile_ref):
    tile_ref[...] = jnp.broadcast_to(step_ref[...], (8, SPAN))


def raw_kernel(count, *refs):
    mats, packed, raws = refs[0], refs[2 : count + 2], refs[count + 2 :]
    results = weak_layers(
        [p[:ROWS] for p in packed], [1.0 / p[ROWS : ROWS + 1] for p in packed], mats
    )
    for raw_ref, result in zip(raws, results):
        raw_ref[...] = result


def slots_kernel(order, ready, *refs):
    count = len(order)
    mats, packed, given = refs[0], refs[2 : count + 2], refs[count + 2 : count + 2 + ready]
    field_ref, heights_ref, partial_ref, cross_ref, core_ref = refs[count + 2 + ready :]
    place = lax.axis_index("vert")
    slots = [jnp.bitwise_xor(place, j) for j in order]
    for i in range(count):
        field_ref[slots[i]] = packed[i][:ROWS]
        heights_ref[slots[i]] = packed[i][ROWS:]
    for i in range(ready):
        partial_ref[slots[i]] = given[i][...]
    results = weak_layers(
        [packed[i][:ROWS] for i in range(ready, count)],
        [1.0 / packed[i][ROWS : ROWS + 1] for i in range(ready, count)],
        mats,
    )
    for i in range(ready, count):
        partial_ref[slots[i]] = results[i - ready]
    heights = [heights_ref[l] for l in range(count)]
    join_layers(heights, partial_ref, cross_ref, core_ref)


def first_kernel(count, *refs):
    mats, packed_ref, refs = refs[0], refs[2], refs[3:]
    field_ref, heights_ref, partial_ref, cross_ref, core_ref = refs
    heights = [packed_ref[l, ROWS:] for l in range(count)]
    for l in range(count):
        field_ref[l] = packed_ref[l, :ROWS]
        heights_ref[l] = heights[l]
    results = weak_layers(
        [packed_ref[l, :ROWS] for l in range(count)], [1.0 / h[:1] for h in heights], mats
    )
    for l in range(count):
        partial_ref[l] = results[l]
    join_layers(heights, partial_ref, cross_ref, core_ref)


def stage_layers(count, last):
    if not last:
        return list(range(count))
    place = lax.axis_index("vert")
    return [place, jnp.minimum(place + 1, count - 1), jnp.maximum(place - 1, 0)]


def put_spots(partial, count, share, last, mats, step_ref, field_ref, spots_ref):
    step = step_ref[:1] * share
    fields = []
    for l in stage_layers(count, last):
        fields.append(inner_rows(field_ref[l]) + step * partial(l))
    for i, pair in enumerate(span_forward(fields, mats)):
        for part in range(2):
            for k, half in enumerate(split(pair[part])):
                spots_ref[i, part, k] = half


def first_inner_kernel(
    count, share, last, mats, step_ref, field_ref, partial_ref, spots_ref, total_ref
):
    def partial(l):
        return inner_rows(partial_ref[l])

    put_spots(partial, count, share, last, mats, step_ref, field_ref, spots_ref)
    total_ref[...] = partial(lax.axis_index("vert"))


def span_inner(backs_ref, partial_ref, count, mats):
    results = []
    span_back(count, [inner_rows(backs_ref[i]) for i in range(len(spots_of(count)))], results, mats)
    for l in range(count):
        partial_ref[l] = results[l]


def inner_kernel(count, share, last, *refs):
    mats, step_ref, field_ref, heights_ref, backs_ref, total_ref, spots_ref = refs[:7]
    next_total_ref, partial_ref = refs[7:]
    span_inner(backs_ref, partial_ref, count, mats)
    layers = [partial_ref.at[l] for l in range(count)]
    heights = [heights_ref[l] for l in range(count)]
    join_heights(layers, heights, [(l, l + 1, True) for l in range(count - 1)])

    def partial(l):
        return partial_ref[l]

    put_spots(partial, count, share, last, mats, step_ref, field_ref, spots_ref)
    next_total_ref[...] = total_ref[...] + 2.0 * partial(lax.axis_index("vert"))


def last_inner_kernel(count, mats, heights_ref, backs_ref, total_ref, rate_ref, partial_ref):
    place = lax.axis_index("vert")
    span_inner(backs_ref, partial_ref, 3, mats)
    heights = [heights_ref[l] for l in stage_layers(count, True)]
    layers = [partial_ref.at[i] for i in range(3)]
    join_heights(layers, heights, [(0, 1, place < count - 1), (2, 0, place > 0)])
    rate_ref[...] = (total_ref[...] + partial_ref[0]) / 6.0


def stage_kernel(count, share, first, next_last, last, *refs):
    mats, step_ref, field_ref, heights_ref, own_cross_ref, own_core_ref = refs[:6]
    cross_ref, core_ref, spots_ref = refs[6:9]
    total = None if first else refs[9]
    total_ref, backs_ref, next_cross_ref, next_core_ref, faces_ref = refs[-5:]
    place = lax.axis_index("vert")
    step = step_ref[:1] * share
    layers = stage_layers(count, last)
    heights = [heights_ref[l] for l in layers]
    fields = []
    for i, l in enumerate(layers):
        at = i if last else l
        ends = join_ends(own_cross_ref[at], own_core_ref[at], cross_ref[at], core_ref[at])
        ends = in_order(*ends).reshape(48, SPAN)
        fields.append(end_rows(field_ref[l]) + step * ends)
    spots = []
    for i, pair in enumerate(face_spots(fields, mats)):
        spots.append([parts_with_faces(spots_ref.at[i, part], pair[part]) for part in range(2)])
    ends, results = [], []

    def put(i, back):
        backs_ref[i] = back
        ends.append(end_rows(back))
        span_back(len(layers), ends, results, mats)

    weak_spots(spots, [1.0 / h[:1] for h in heights], mats, put)
    for i, result in enumerate(results):
        faces_ref[i] = result
    faces = [faces_ref.at[i] for i in range(len(layers))]
    if last:
        join_heights(faces, heights, [(0, 1, place < count - 1), (2, 0, place > 0)])
        put_faces(faces_ref[0], next_cross_ref, next_core_ref, slice(None))
    else:
        join_heights(faces, heights, [(l, l + 1, True) for l in range(count - 1)])
        for i, l in enumerate(stage_layers(count, next_last)):
            put_faces(faces_ref[l], next_cross_ref, next_core_ref, i)
    place = 0 if last else place
    own = join_ends(own_cross_ref[place], own_core_ref[place], cross_ref[place], core_ref[place])
    for k in range(2):
        total_ref[k] = own[k] if first else total[k] + 2.0 * own[k]


def rate_kernel(own_cross_ref, own_core_ref, cross_ref, core_ref, inner_ref, total_ref, rate_ref):
    ends = join_ends(own_cross_ref[...], own_core_ref[...], cross_ref[...], core_ref[...])
    ends = [(total_ref[k] + ends[k]) / 6.0 for k in range(2)]
    rate_ref[...] = with_faces(inner_ref[...], in_order(*ends))


VMEM = pl.BlockSpec(memory_space=pltpu.VMEM)


def call(kernel, outs, args, scratch=(), flops=0):
    shapes = [
        jax.ShapeDtypeStruct(shape, bf16 if len(shape) == 5 else f32) for shape in outs
    ]
    one = len(shapes) == 1
    return pl.pallas_call(
        kernel,
        out_shape=shapes[0] if one else shapes,
        in_specs=[VMEM] * len(args),
        out_specs=VMEM if one else [VMEM] * len(shapes),
        scratch_shapes=list(scratch),
        compiler_params=pltpu.CompilerParams(vmem_limit_bytes=32 * 1024 * 1024),
        cost_estimate=pl.CostEstimate(flops=flops, bytes_accessed=1 << 20, transcendentals=0),
    )(*args)


def swap_stream(cross, core):
    count = lax.axis_size("horiz")
    cores = [(i, i ^ 1) for i in range(count)]
    crosses = [(i, (i + 1) % count if i % 2 else (i - 1) % count) for i in range(count)]
    return lax.ppermute(cross, "horiz", crosses), lax.ppermute(core, "horiz", cores)


def on_device(velocity, heights, time_step):
    layers = lax.axis_size("vert")
    mats = jnp.asarray(matrices()[0])
    unit = 2 * 256 * 256 * 3000
    field = (layers, ROWS, SPAN)
    face = (layers, 3, 8, SPAN)
    small = (3, 8, SPAN)
    first_outs = [field, (layers, 8, SPAN), field, face, face]
    step = time_step.reshape(1, 1)
    tile = (8, SPAN)
    step = call(step_kernel, [tile], [mats, step], flops=2 * unit)
    own_field = velocity.reshape(ROWS, SPAN)
    packed = jnp.concatenate([own_field, jnp.broadcast_to(heights[:, None], (8, SPAN))], axis=0)
    if layers in (1, 2, 4):
        groups = {1: [[0]], 2: [[0], [1]], 4: [[0, 1, 2], [3]]}[layers]
        slots = {0: packed}
        for j in range(layers - 1, 0, -1):
            slots[j] = lax.ppermute(packed, "vert", [(i, i ^ j) for i in range(layers)])
        given = []
        for group in groups[:-1]:
            outs = [(ROWS, SPAN)] * len(group)
            args = [mats, step] + [slots[j] for j in group]
            raw = call(
                functools.partial(raw_kernel, len(group)), outs, args, flops=len(group) * unit
            )
            given += [raw] if len(group) == 1 else raw
        order = sum(groups, [])
        args = [mats, step] + [slots[j] for j in order] + given
        first = functools.partial(slots_kernel, order, len(given))
    else:
        args = [mats, step, lax.all_gather(packed, "vert")]
        first = functools.partial(first_kernel, layers)
    fields, all_heights, partial, cross, core = call(
        first, first_outs, args, flops=layers * unit
    )
    own_ends = cross, core
    ends = swap_stream(cross, core)
    backs = face_total = None
    for stage, share in enumerate((0.5, 0.5, 1.0)):
        last = stage == 2
        used = 3 if last else layers
        outs = [(len(spots_of(used)), 2, 2, 144, SPAN), (144, SPAN)]
        if stage == 0:
            spots, total = call(
                functools.partial(first_inner_kernel, layers, share, last),
                outs,
                [mats, step, fields, partial],
                flops=used * unit // 4,
            )
        else:
            spots, total = call(
                functools.partial(inner_kernel, layers, share, last),
                outs,
                [mats, step, fields, all_heights, backs, total],
                scratch=[pltpu.VMEM((layers, 144, SPAN), f32)],
                flops=used * unit // 2,
            )
        args = [mats, step, fields, all_heights, *own_ends, *ends, spots]
        end = (small, (3,) + small, face)[2 - stage]
        face_total, backs, cross, core = call(
            functools.partial(stage_kernel, layers, share, stage == 0, stage == 1, last),
            [(2,) + small, (len(spots_of(used)), ROWS, SPAN), end, end],
            args + ([] if stage == 0 else [face_total]),
            scratch=[pltpu.VMEM((used, 48, SPAN), f32)],
            flops=used * unit,
        )
        own_ends = cross, core
        ends = swap_stream(cross, core)
    inner = call(
        functools.partial(last_inner_kernel, layers),
        [(144, SPAN)],
        [mats, all_heights, backs, total],
        scratch=[pltpu.VMEM((3, 144, SPAN), f32)],
        flops=unit // 2,
    )
    rate = call(rate_kernel, [(ROWS, SPAN)], [*own_ends, *ends, inner, face_total])
    return rate.reshape(velocity.shape)


def solution(mesh):
    in_specs = (P(None, "horiz", "vert", None), P("vert"), P())
    out_specs = P(None, "horiz", "vert", None)
    return jax.shard_map(
        on_device, mesh=mesh, in_specs=in_specs, out_specs=out_specs, check_vma=False
    )
```

```python
import functools

import jax
import jax.numpy as jnp
import ml_dtypes
import numpy as np
from jax import lax
from jax.experimental import pallas as pl
from jax.experimental.pallas import tpu as pltpu
from jax.sharding import PartitionSpec as P

gll_half = [1.0, 0.8717401485096066, 0.5917001814331423, 0.2092992179024789]
gll_half_weights = [
    0.03571428571428571,
    0.21070422714350603,
    0.34112269248350435,
    0.4124587946587038,
]
gauss_half = [
    0.9815606342467192,
    0.9041172563704749,
    0.7699026741943047,
    0.5873179542866175,
    0.3678314989981802,
    0.1252334085114689,
]
gauss_half_weights = [
    0.0471753363865118,
    0.1069393259953184,
    0.1600783285433462,
    0.2031674267230659,
    0.2334925365383548,
    0.2491470458134028,
]

f32 = jnp.float32
bf16 = jnp.bfloat16
ROWS = 192
SPAN = 128
SPAN_ELEMENTS = 16


def mirrored(values, sign):
    return np.concatenate([sign * np.array(values), np.array(values[::-1])])


def lagrange(targets, sources):
    matrix = np.ones((targets.size, sources.size))
    for j in range(sources.size):
        for k in range(sources.size):
            if k != j:
                matrix[:, j] = matrix[:, j] * (targets - sources[k]) / (sources[j] - sources[k])
    return matrix


def node_tables():
    gll_points = mirrored(gll_half, -1.0)
    gll_weights = mirrored(gll_half_weights, 1.0)
    fine_points = mirrored(gauss_half, -1.0)
    fine_weights = mirrored(gauss_half_weights, 1.0)
    to_fine = lagrange(fine_points, gll_points)
    products = np.ones(8)
    for i in range(8):
        for k in range(8):
            if k != i:
                products[i] = products[i] * (gll_points[i] - gll_points[k])
    deriv_mat = np.zeros((8, 8))
    for i in range(8):
        for j in range(8):
            if i != j:
                deriv_mat[i, j] = products[i] / (products[j] * (gll_points[i] - gll_points[j]))
                deriv_mat[i, i] = deriv_mat[i, i] + 1.0 / (gll_points[i] - gll_points[j])
    return to_fine, to_fine @ deriv_mat, gll_weights, fine_weights


def halves(matrix):
    high = matrix.astype(ml_dtypes.bfloat16)
    low = (matrix - high.astype(np.float64)).astype(ml_dtypes.bfloat16)
    return high, low


def stack_columns(matrix):
    high, low = halves(matrix)
    return np.concatenate([high, high, low], axis=1)


def span_blocks(block, first, count):
    out = np.zeros((SPAN, SPAN_ELEMENTS * count))
    for e in range(SPAN_ELEMENTS):
        out[e * 8 : e * 8 + 8, e * count : (e + 1) * count] = block[first : first + count].T
    return out


@functools.cache
def matrices():
    interp, deriv, gll_w, fine_w = node_tables()
    a_both = np.concatenate([span_blocks(interp, 0, 8), span_blocks(2.0 * deriv, 0, 8)], axis=1)
    span_a = np.concatenate(halves(a_both), axis=0)
    interp_b = span_blocks(interp, 8, 4)
    deriv_b = span_blocks(2.0 * deriv, 8, 4)
    none = np.zeros_like(interp_b)
    first_b = halves(np.concatenate([interp_b, none, deriv_b, none], axis=1))
    second_b = halves(np.concatenate([none, interp_b, none, deriv_b], axis=1))
    span_b = np.concatenate(first_b + second_b, axis=0)
    values = np.kron(interp, interp)
    plane = np.concatenate([values, np.kron(2.0 * deriv, interp), np.kron(interp, 2.0 * deriv)])
    order = np.concatenate([np.arange(8, 56), np.arange(8), np.arange(56, 64)])
    plane, values = plane[:, order], values[:, order]
    plane = stack_columns(plane)
    values = stack_columns(values)
    back = interp.T * fine_w[None, :] / gll_w[:, None]
    plane_back = np.concatenate(halves(-np.kron(back, back)), axis=0)
    a_back = np.zeros((SPAN, SPAN))
    b_back = np.zeros((SPAN // 2, SPAN))
    for e in range(SPAN_ELEMENTS):
        a_back[e * 8 : e * 8 + 8, e * 8 : e * 8 + 8] = back[:, :8].T
        b_back[e * 4 : e * 4 + 4, e * 8 : e * 8 + 8] = back[:, 8:].T
    span = np.concatenate([a_back, b_back], axis=0)
    summed = span.copy()
    for e in range(SPAN_ELEMENTS):
        last, first = e * 8 + 7, (e * 8 + 8) % SPAN
        mean = 0.5 * (span[:, last] + span[:, first])
        summed[:, last] = mean
        summed[:, first] = mean
    a_back, b_back = summed[:SPAN], summed[SPAN:]
    zero_a, zero_b = np.zeros_like(a_back), np.zeros_like(b_back)
    pair_back = np.concatenate(
        [
            np.concatenate([a_back, zero_a], axis=1),
            np.concatenate([zero_a, a_back], axis=1),
            np.concatenate([b_back, zero_b], axis=1),
            np.concatenate([zero_b, b_back], axis=1),
        ],
        axis=0,
    )
    wide = {
        "span_a": span_a,
        "span_b": span_b,
        "plane": plane,
        "values": values,
        "plane_back": plane_back,
        "pair_back": np.concatenate(halves(pair_back), axis=0),
    }
    rows, places = [], {}
    start = 0
    for name, matrix in wide.items():
        places[name] = (start, matrix.shape[0], matrix.shape[1])
        rows.append(np.pad(matrix, ((0, 0), (0, 256 - matrix.shape[1]))))
        start += matrix.shape[0]
    return np.concatenate(rows, axis=0), places


def read(mats_ref, name):
    start, count, width = matrices()[1][name]
    return mats_ref[start : start + count, :width]


def read_rows(mats_ref, name, *pieces):
    start, count, width = matrices()[1][name]
    half = count // 2
    out = []
    for offset in (0, 0, half):
        for first, rows in pieces:
            at = start + offset + first
            out.append(mats_ref[at : at + rows, :width])
    return jnp.concatenate(out, axis=0)


def read_span_a(mats_ref):
    return read_rows(mats_ref, "span_a", (0, SPAN))


def read_span_b(mats_ref):
    start = matrices()[1]["span_b"][0]
    order = (0, 0, 1, 2, 2, 3)
    return jnp.concatenate(
        [mats_ref[start + i * SPAN : start + i * SPAN + SPAN] for i in order], axis=0
    )


def read_back(mats_ref, size):
    if size == 2:
        return read_rows(mats_ref, "pair_back", (0, 3 * SPAN))
    return read_rows(mats_ref, "pair_back", (0, SPAN), (2 * SPAN, SPAN))[:, :SPAN]


def split(x):
    high = x.astype(bf16)
    return high, (x - high.astype(f32)).astype(bf16)


def dot(a, b):
    return jnp.dot(a, b, preferred_element_type=f32)


def triple(x, axis):
    high, low = split(x)
    return jnp.concatenate([high, low, high], axis=axis)


def spots_of(count):
    spots = []
    for first in range(0, count, 2):
        group = tuple(range(first, min(first + 2, count)))
        spots += [(l,) for l in group] + [group + (None,) * (3 - len(group))]
    return spots


def chunks_of(count):
    spots = spots_of(count)
    return [spots[first : first + 2] for first in range(0, len(spots), 2)]


def span_forward(fields, mats):
    span_a, span_b = read_span_a(mats), read_span_b(mats)
    lefts = [triple(field, 1) for field in fields]
    spots = []
    for spot in spots_of(len(fields)):
        if len(spot) == 1:
            out = dot(lefts[spot[0]], span_a)
        elif spot[1] is None:
            out = dot(lefts[spot[0]], span_b[: 3 * SPAN])
        else:
            out = dot(jnp.concatenate([lefts[spot[0]], lefts[spot[1]]], axis=1), span_b)
        spots.append((out[:, :SPAN], out[:, SPAN:]))
    return spots


def plane_parts(x):
    out = []
    for c in range(3):
        rows = x[c * 64 : c * 64 + 64]
        out.append(split(jnp.concatenate([rows[8:56], rows[:8], rows[56:]], axis=0)))
    return out


def plane_forward(spots, mats):
    plane, values = read(mats, "plane"), read(mats, "values")
    outs = []
    for c in range(3):
        pair = []
        for part, matrix in enumerate((plane, values)):
            high, low = (jnp.concatenate([s[part][c][k] for s in spots], axis=1) for k in range(2))
            pair.append(dot(matrix, jnp.concatenate([high, low, high], axis=0)))
        outs.append(pair)
    return outs


def chunk_inverse(chunk, inverses):
    lane = lax.broadcasted_iota(jnp.int32, (1, SPAN), 1)
    out = []
    for spot in chunk:
        if len(spot) == 1 or spot[1] is None:
            out.append(inverses[spot[0]])
        else:
            out.append(jnp.where(lane < 64, inverses[spot[0]], inverses[spot[1]]))
    return jnp.concatenate(out, axis=1)


def convect_back(fine, inverse, mats):
    back = read(mats, "plane_back")
    parts = [([], []) for _ in range(3)]
    for first in range(0, 144, 48):
        rows = slice(first, first + 48)
        speeds = [fine(c, 0, rows) for c in range(3)]
        speeds[2] = speeds[2] * inverse
        for c in range(3):
            convect = (
                speeds[0] * fine(c, 1, rows)
                + speeds[1] * fine(c, 3, rows)
                + speeds[2] * fine(c, 2, rows)
            )
            for part, half in zip(parts[c], split(convect)):
                part.append(half)
    outs = []
    for high, low in parts:
        out = dot(back, jnp.concatenate(high, axis=0))
        outs.append(out[:64] + out[64:] + dot(back[:64], jnp.concatenate(low, axis=0)))
    return jnp.concatenate(outs, axis=0)


def span_back(count, backs, results, mats):
    for place, spot in enumerate(spots_of(count)):
        if len(spot) == 1 or place >= len(backs) or spot[0] < len(results):
            continue
        size = 1 if spot[1] is None else 2
        joined = jnp.concatenate(backs[place - size : place + 1], axis=1)
        out = dot(triple(joined, 1), read_back(mats, size))
        results += [out[:, i * SPAN : (i + 1) * SPAN] for i in range(size)]


def weak_spots(spots, inverses, mats, put):
    chunks = chunks_of(len(inverses))
    planes = []

    def finish(i):
        def fine(c, kind, rows):
            first, along_y = planes[i][c]
            if kind == 3:
                return along_y[rows]
            return first[kind * 144 + rows.start : kind * 144 + rows.stop]

        out = convect_back(fine, chunk_inverse(chunks[i], inverses), mats)
        for j in range(len(chunks[i])):
            put(2 * i + j, out[:, j * SPAN : (j + 1) * SPAN])

    for i in range(len(chunks)):
        planes.append(plane_forward(spots[2 * i : 2 * i + 2], mats))
        if i > 0:
            finish(i - 1)
    finish(len(chunks) - 1)


def weak_layers(fields, inverses, mats):
    backs, results = [], []

    def put(place, back):
        backs.append(back)
        span_back(len(fields), backs, results, mats)

    spots = [[plane_parts(x) for x in pair] for pair in span_forward(fields, mats)]
    weak_spots(spots, inverses, mats, put)
    return results


def end_rows(x):
    x = x.reshape(3, 8, 8, SPAN)
    return jnp.concatenate([x[:, :1], x[:, 7:]], axis=1).reshape(48, SPAN)


def inner_rows(x):
    return x.reshape(3, 8, 8, SPAN)[:, 1:7].reshape(144, SPAN)


def face_spots(faces, mats):
    out_a = dot(triple(jnp.concatenate(faces, axis=0), 1), read_span_a(mats))
    even, odd = faces[0::2], faces[1::2]
    odd = odd + [jnp.zeros_like(faces[0])] * (len(even) - len(odd))
    even, odd = (triple(jnp.concatenate(x, axis=0), 1) for x in (even, odd))
    out_b = dot(jnp.concatenate([even, odd], axis=1), read_span_b(mats))
    spots = []
    for spot in spots_of(len(faces)):
        if len(spot) == 1:
            out = out_a[spot[0] * 48 : spot[0] * 48 + 48]
        else:
            out = out_b[spot[0] * 24 : spot[0] * 24 + 48]
        spots.append((out[:, :SPAN], out[:, SPAN:]))
    return spots


def with_faces(inner, faces):
    inner = inner.reshape(3, 6, 8, SPAN)
    faces = faces.reshape(3, 2, 8, SPAN)
    return jnp.concatenate([faces[:, :1], inner, faces[:, 1:]], axis=1).reshape(ROWS, SPAN)


def parts_with_faces(inner_ref, faces):
    out = []
    for c in range(3):
        ends = split(faces[c * 16 : c * 16 + 16])
        out.append(
            [
                jnp.concatenate([inner_ref[k, c * 48 : c * 48 + 48], ends[k]], axis=0)
                for k in range(2)
            ]
        )
    return out


def join_heights(layers, heights, joins):
    rows = layers[0].shape[0] // 8
    top, bottom = pl.ds(7, rows, stride=8), pl.ds(0, rows, stride=8)
    for lower, upper, wanted in joins:
        share = heights[upper] / (heights[lower] + heights[upper])
        share = share[:1]
        below, above = layers[lower][top, :], layers[upper][bottom, :]
        mean = below * (1.0 - share) + above * share
        if wanted is True:
            layers[lower][top, :] = mean
            layers[upper][bottom, :] = mean
        else:
            layers[lower][top, :] = jnp.where(wanted, mean, below)
            layers[upper][bottom, :] = jnp.where(wanted, mean, above)


def sides():
    place = lax.axis_index("horiz")
    left_share = jnp.where(place > 0, 0.5, 0.0).astype(f32)
    right_share = jnp.where(place < lax.axis_size("horiz") - 1, 0.5, 0.0).astype(f32)
    return lax.rem(place, 2) == 1, left_share, right_share


def join_ends(own_cross, own_core, cross, core):
    odd, left_share, right_share = sides()
    cross_share = jnp.where(odd, right_share, left_share)
    core_share = jnp.where(odd, left_share, right_share)
    cross = own_cross * (1.0 - cross_share) + cross * cross_share
    return cross, own_core * (1.0 - core_share) + core * core_share


def in_order(cross, core):
    odd = sides()[0]
    ends = jnp.where(odd, core, cross), jnp.where(odd, cross, core)
    return jnp.concatenate([end[:, None] for end in ends], axis=1)


def put_faces(ends, cross_ref, core_ref, at):
    odd = sides()[0]
    ends = ends.reshape(3, 2, 8, SPAN)
    first, last = ends[:, 0], ends[:, 1]
    cross_ref[at] = jnp.where(odd, last, first)
    core_ref[at] = jnp.where(odd, first, last)


def join_layers(heights, partial_ref, cross_ref, core_ref):
    count = len(heights)
    layers = [partial_ref.at[l] for l in range(count)]
    join_heights(layers, heights, [(l, l + 1, True) for l in range(count - 1)])
    for l in range(count):
        put_faces(end_rows(partial_ref[l]), cross_ref, core_ref, l)


def step_kernel(mats, step_ref, tile_ref):
    tile_ref[...] = jnp.broadcast_to(step_ref[...], (8, SPAN))


def raw_kernel(count, *refs):
    mats, packed, raws = refs[0], refs[2 : count + 2], refs[count + 2 :]
    results = weak_layers(
        [p[:ROWS] for p in packed], [1.0 / p[ROWS : ROWS + 1] for p in packed], mats
    )
    for raw_ref, result in zip(raws, results):
        raw_ref[...] = result


def slots_kernel(order, ready, *refs):
    count = len(order)
    mats, packed, given = refs[0], refs[2 : count + 2], refs[count + 2 : count + 2 + ready]
    field_ref, heights_ref, partial_ref, cross_ref, core_ref = refs[count + 2 + ready :]
    place = lax.axis_index("vert")
    slots = [jnp.bitwise_xor(place, j) for j in order]
    for i in range(count):
        field_ref[slots[i]] = packed[i][:ROWS]
        heights_ref[slots[i]] = packed[i][ROWS:]
    for i in range(ready):
        partial_ref[slots[i]] = given[i][...]
    results = weak_layers(
        [packed[i][:ROWS] for i in range(ready, count)],
        [1.0 / packed[i][ROWS : ROWS + 1] for i in range(ready, count)],
        mats,
    )
    for i in range(ready, count):
        partial_ref[slots[i]] = results[i - ready]
    heights = [heights_ref[l] for l in range(count)]
    join_layers(heights, partial_ref, cross_ref, core_ref)


def first_kernel(count, *refs):
    mats, packed_ref, refs = refs[0], refs[2], refs[3:]
    field_ref, heights_ref, partial_ref, cross_ref, core_ref = refs
    heights = [packed_ref[l, ROWS:] for l in range(count)]
    for l in range(count):
        field_ref[l] = packed_ref[l, :ROWS]
        heights_ref[l] = heights[l]
    results = weak_layers(
        [packed_ref[l, :ROWS] for l in range(count)], [1.0 / h[:1] for h in heights], mats
    )
    for l in range(count):
        partial_ref[l] = results[l]
    join_layers(heights, partial_ref, cross_ref, core_ref)


def stage_layers(count, last):
    if not last:
        return list(range(count))
    place = lax.axis_index("vert")
    return [place, jnp.minimum(place + 1, count - 1), jnp.maximum(place - 1, 0)]


def put_spots(partial, count, share, last, mats, step_ref, field_ref, spots_ref):
    step = step_ref[:1] * share
    fields = []
    for l in stage_layers(count, last):
        fields.append(inner_rows(field_ref[l]) + step * partial(l))
    for i, pair in enumerate(span_forward(fields, mats)):
        for part in range(2):
            for k, half in enumerate(split(pair[part])):
                spots_ref[i, part, k] = half


def first_inner_kernel(
    count, share, last, mats, step_ref, field_ref, partial_ref, spots_ref, total_ref
):
    def partial(l):
        return inner_rows(partial_ref[l])

    put_spots(partial, count, share, last, mats, step_ref, field_ref, spots_ref)
    total_ref[...] = partial(lax.axis_index("vert"))


def span_inner(backs_ref, partial_ref, count, mats):
    results = []
    span_back(count, [inner_rows(backs_ref[i]) for i in range(len(spots_of(count)))], results, mats)
    for l in range(count):
        partial_ref[l] = results[l]


def inner_kernel(count, share, last, *refs):
    mats, step_ref, field_ref, heights_ref, backs_ref, total_ref, spots_ref = refs[:7]
    next_total_ref, partial_ref = refs[7:]
    span_inner(backs_ref, partial_ref, count, mats)
    layers = [partial_ref.at[l] for l in range(count)]
    heights = [heights_ref[l] for l in range(count)]
    join_heights(layers, heights, [(l, l + 1, True) for l in range(count - 1)])

    def partial(l):
        return partial_ref[l]

    put_spots(partial, count, share, last, mats, step_ref, field_ref, spots_ref)
    next_total_ref[...] = total_ref[...] + 2.0 * partial(lax.axis_index("vert"))


def last_inner_kernel(count, mats, heights_ref, backs_ref, total_ref, rate_ref, partial_ref):
    place = lax.axis_index("vert")
    span_inner(backs_ref, partial_ref, 3, mats)
    heights = [heights_ref[l] for l in stage_layers(count, True)]
    layers = [partial_ref.at[i] for i in range(3)]
    join_heights(layers, heights, [(0, 1, place < count - 1), (2, 0, place > 0)])
    rate_ref[...] = (total_ref[...] + partial_ref[0]) / 6.0


def ends_kernel(first, last, *refs):
    own_cross_ref, own_core_ref, cross_ref, core_ref = refs[:4]
    place = 0 if last else lax.axis_index("vert")
    own = join_ends(own_cross_ref[place], own_core_ref[place], cross_ref[place], core_ref[place])
    for k in range(2):
        refs[-1][k] = own[k] if first else refs[4][k] + 2.0 * own[k]


def stage_kernel(count, share, next_last, last, *refs):
    mats, step_ref, field_ref, heights_ref, own_cross_ref, own_core_ref = refs[:6]
    cross_ref, core_ref, spots_ref = refs[6:9]
    backs_ref, next_cross_ref, next_core_ref, faces_ref = refs[-4:]
    place = lax.axis_index("vert")
    step = step_ref[:1] * share
    layers = stage_layers(count, last)
    heights = [heights_ref[l] for l in layers]
    fields = []
    for i, l in enumerate(layers):
        at = i if last else l
        ends = join_ends(own_cross_ref[at], own_core_ref[at], cross_ref[at], core_ref[at])
        ends = in_order(*ends).reshape(48, SPAN)
        fields.append(end_rows(field_ref[l]) + step * ends)
    spots = []
    for i, pair in enumerate(face_spots(fields, mats)):
        spots.append([parts_with_faces(spots_ref.at[i, part], pair[part]) for part in range(2)])
    ends, results = [], []

    def put(i, back):
        backs_ref[i] = back
        ends.append(end_rows(back))
        span_back(len(layers), ends, results, mats)

    weak_spots(spots, [1.0 / h[:1] for h in heights], mats, put)
    for i, result in enumerate(results):
        faces_ref[i] = result
    faces = [faces_ref.at[i] for i in range(len(layers))]
    if last:
        join_heights(faces, heights, [(0, 1, place < count - 1), (2, 0, place > 0)])
        put_faces(faces_ref[0], next_cross_ref, next_core_ref, slice(None))
    else:
        join_heights(faces, heights, [(l, l + 1, True) for l in range(count - 1)])
        for i, l in enumerate(stage_layers(count, next_last)):
            put_faces(faces_ref[l], next_cross_ref, next_core_ref, i)


def rate_kernel(own_cross_ref, own_core_ref, cross_ref, core_ref, inner_ref, total_ref, rate_ref):
    ends = join_ends(own_cross_ref[...], own_core_ref[...], cross_ref[...], core_ref[...])
    ends = [(total_ref[k] + ends[k]) / 6.0 for k in range(2)]
    rate_ref[...] = with_faces(inner_ref[...], in_order(*ends))


VMEM = pl.BlockSpec(memory_space=pltpu.VMEM)


def call(kernel, outs, args, scratch=(), flops=0):
    shapes = [
        jax.ShapeDtypeStruct(shape, bf16 if len(shape) == 5 else f32) for shape in outs
    ]
    one = len(shapes) == 1
    return pl.pallas_call(
        kernel,
        out_shape=shapes[0] if one else shapes,
        in_specs=[VMEM] * len(args),
        out_specs=VMEM if one else [VMEM] * len(shapes),
        scratch_shapes=list(scratch),
        compiler_params=pltpu.CompilerParams(vmem_limit_bytes=32 * 1024 * 1024),
        cost_estimate=pl.CostEstimate(flops=flops, bytes_accessed=1 << 20, transcendentals=0),
    )(*args)


def swap_stream(cross, core):
    count = lax.axis_size("horiz")
    cores = [(i, i ^ 1) for i in range(count)]
    crosses = [(i, (i + 1) % count if i % 2 else (i - 1) % count) for i in range(count)]
    return lax.ppermute(cross, "horiz", crosses), lax.ppermute(core, "horiz", cores)


def on_device(velocity, heights, time_step):
    layers = lax.axis_size("vert")
    mats = jnp.asarray(matrices()[0])
    unit = 2 * 256 * 256 * 3000
    field = (layers, ROWS, SPAN)
    face = (layers, 3, 8, SPAN)
    small = (3, 8, SPAN)
    first_outs = [field, (layers, 8, SPAN), field, face, face]
    step = time_step.reshape(1, 1)
    tile = (8, SPAN)
    step = call(step_kernel, [tile], [mats, step], flops=2 * unit)
    own_field = velocity.reshape(ROWS, SPAN)
    packed = jnp.concatenate([own_field, jnp.broadcast_to(heights[:, None], (8, SPAN))], axis=0)
    if layers in (1, 2, 4):
        groups = {1: [[0]], 2: [[0], [1]], 4: [[0, 1, 2], [3]]}[layers]
        slots = {0: packed}
        for j in range(layers - 1, 0, -1):
            slots[j] = lax.ppermute(packed, "vert", [(i, i ^ j) for i in range(layers)])
        given = []
        for group in groups[:-1]:
            outs = [(ROWS, SPAN)] * len(group)
            args = [mats, step] + [slots[j] for j in group]
            raw = call(
                functools.partial(raw_kernel, len(group)), outs, args, flops=len(group) * unit
            )
            given += [raw] if len(group) == 1 else raw
        order = sum(groups, [])
        args = [mats, step] + [slots[j] for j in order] + given
        first = functools.partial(slots_kernel, order, len(given))
    else:
        args = [mats, step, lax.all_gather(packed, "vert")]
        first = functools.partial(first_kernel, layers)
    fields, all_heights, partial, cross, core = call(
        first, first_outs, args, flops=layers * unit
    )
    own_ends = cross, core
    ends = swap_stream(cross, core)
    backs = face_total = None
    for stage, share in enumerate((0.5, 0.5, 1.0)):
        last = stage == 2
        used = 3 if last else layers
        outs = [(len(spots_of(used)), 2, 2, 144, SPAN), (144, SPAN)]
        if stage == 0:
            spots, total = call(
                functools.partial(first_inner_kernel, layers, share, last),
                outs,
                [mats, step, fields, partial],
                flops=used * unit // 4,
            )
        else:
            spots, total = call(
                functools.partial(inner_kernel, layers, share, last),
                outs,
                [mats, step, fields, all_heights, backs, total],
                scratch=[pltpu.VMEM((layers, 144, SPAN), f32)],
                flops=used * unit // 2,
            )
        args = [mats, step, fields, all_heights, *own_ends, *ends, spots]
        end = (small, (3,) + small, face)[2 - stage]
        backs, cross, core = call(
            functools.partial(stage_kernel, layers, share, stage == 1, last),
            [(len(spots_of(used)), ROWS, SPAN), end, end],
            args,
            scratch=[pltpu.VMEM((used, 48, SPAN), f32)],
            flops=used * unit,
        )
        before = [*own_ends, *ends]
        own_ends = cross, core
        ends = swap_stream(cross, core)
        face_total = call(
            functools.partial(ends_kernel, stage == 0, last),
            [(2,) + small],
            before + ([] if stage == 0 else [face_total]),
        )
    inner = call(
        functools.partial(last_inner_kernel, layers),
        [(144, SPAN)],
        [mats, all_heights, backs, total],
        scratch=[pltpu.VMEM((3, 144, SPAN), f32)],
        flops=unit // 2,
    )
    rate = call(rate_kernel, [(ROWS, SPAN)], [*own_ends, *ends, inner, face_total])
    return rate.reshape(velocity.shape)


def solution(mesh):
    in_specs = (P(None, "horiz", "vert", None), P("vert"), P())
    out_specs = P(None, "horiz", "vert", None)
    return jax.shard_map(
        on_device, mesh=mesh, in_specs=in_specs, out_specs=out_specs, check_vma=False
    )
```
